32 devices in a mesh: page: 4 (over y, x), rows: 8 (over z, core).
Axes of the slice: x: 2, y: 2, z: 4, core: 2. Of those that a mesh axis runs over, the one named last changes fastest.
Arguments:
- patches: bfloat16 [8, 80, 120, 512], P('page', 'rows'), may hold values from -6 to 6
- out_grad: bfloat16 [8, 80, 120, 512], P('page', 'rows'), may hold values from -6 to 6
- page_windows: int32 [8], P('page'), may hold values from 6 to 12, as said below
- region_ids: int32 [8, 80, 120], P('page', 'rows'), may hold values from 0 to 3
- offset_index: int32 [100, 100], replicated, may hold values from 0 to 360
- weights_in: bfloat16 [512, 4096], replicated, may hold values from -0.25 to 0.25
- weights_out: bfloat16 [2048, 512], replicated, may hold values from -0.125 to 0.125
- norm_gains: float32 [2, 512], replicated, may hold values from 0.5 to 1.5
- biases: float32 [5120], replicated, may hold values from -1.75 to 1.75
- bias_table: float32 [361, 16], replicated, may hold values from -6 to 6
- master_in: float32 [512, 4096], P('rows'), may hold values from -0.25 to 0.25
- master_out: float32 [2048, 512], P('rows'), may hold values from -0.125 to 0.125
- first_in: float32 [512, 4096], P('rows'), may hold values from -96 to 96
- second_in: float32 [512, 4096], P('rows'), may hold values from 15.36 to 76.8
- first_out: float32 [2048, 512], P('rows'), may hold values from -96 to 96
- second_out: float32 [2048, 512], P('rows'), may hold values from 15.36 to 76.8
- first_small: float32 [11920], replicated, may hold values from -80 to 80
- second_small: float32 [11920], replicated, may hold values from 7.68 to 38.4
Outputs:
- mixed: bfloat16 [8, 80, 120, 512], P('page', 'rows')
- patch_grad: bfloat16 [8, 80, 120, 512], P('page', 'rows')
- new_in: float32 [512, 4096], P('rows')
- moment_in: float32 [512, 4096], P('rows')
- square_in: float32 [512, 4096], P('rows')
- new_out: float32 [2048, 512], P('rows')
- moment_out: float32 [2048, 512], P('rows')
- square_out: float32 [2048, 512], P('rows')
- new_small: float32 [11920], replicated
- moment_small: float32 [11920], replicated
- square_small: float32 [11920], replicated
The draws below stay inside these ranges and needn't reach their ends.
Inputs may be any that keep to these rules, and one draw needn't show every extreme that they name: `page_windows`: some page is 12 windows wide and some (12 + 1) // 2.
All inputs are finite; a program needn't handle non-finite values.
Results may differ from the reference program's by a relative error of at most 0.0085.
Values may be sent and summed in bfloat16 or wider, within the bound.
A program may use at most 256 MiB of HBM per device.

```python
import math
import jax
import jax.numpy as jnp
from jax import lax

D = 512
HEADS = 16
HEAD = 32
FF = 2048
WIN = 10
STEP = 10
CW = 12
SHIFT = 5
TABLE = 361
COLS = 120
PAGES = 8
PAGE_ROWS = 80
TOKENS = 76800


def draw_page_windows(key, part):
    key = jax.random.fold_in(key, 11)
    first, second, third = jax.random.split(key, 3)
    widths = jax.random.randint(first, (PAGES,), (CW + 1) // 2, CW + 1)
    widest = jax.random.randint(second, (), 0, PAGES)
    narrow = (widest + 1 + jax.random.randint(third, (), 0, PAGES - 1)) % PAGES
    places = jnp.arange(PAGES)
    widths = jnp.where(places == narrow, (CW + 1) // 2, widths)
    widths = jnp.where(places == widest, CW, widths)
    return widths.astype(jnp.int32)


def with_ends(values, rng, smallest, high):
    longest = values.shape.index(max(values.shape))
    spots = []
    for shift in (0, 1):
        where = [jax.random.randint(jax.random.fold_in(rng, axis), (), 0, length) for axis, length in enumerate(values.shape)]
        where[longest] = (where[longest] + shift) % values.shape[longest]
        spots.append(tuple(where))
    return values.at[spots[0]].set(smallest).at[spots[1]].set(high)


def shard_levels(own_key, extent, shards, least, largest):
    loudness, own = 1.0, jax.random.fold_in(own_key, 6)
    for position, blocks in shards:
        draws = jnp.exp(jax.random.uniform(jax.random.fold_in(own, position), (blocks,), jnp.float32, least / len(shards), largest / len(shards)))
        loudness = loudness * jnp.repeat(draws, extent[position] // blocks).reshape([-1 if axis == position else 1 for axis in range(len(extent))])
    return loudness


def centred(own_key, dims, scale, reach, cuts=(), kind=jnp.bfloat16):
    entries = scale * jax.random.normal(own_key, dims, jnp.float32)
    if cuts:
        entries = entries * shard_levels(own_key, dims, cuts, -0.22, 0.18)
    return jnp.clip(entries, -reach, reach).astype(kind)


def setup_inputs(seed: int = 0) -> dict:
    keys = jax.random.split(jax.random.key(seed), 19)
    patches = centred(keys[0], (PAGES, PAGE_ROWS, COLS, D), 1.0, 6.0, ((0, 4), (1, 8)))
    out_grad = centred(keys[1], (PAGES, PAGE_ROWS, COLS, D), 1.0, 6.0, ((0, 4), (1, 8)))
    page_windows = draw_page_windows(jax.random.fold_in(keys[18], 71), 0)
    region_ids = with_ends(jax.random.randint(keys[3], (PAGES, PAGE_ROWS, COLS), 0, 4), jax.random.fold_in(keys[3], 1), 0, 3).astype(jnp.int32)
    offset_index = with_ends(jax.random.randint(keys[4], (WIN * WIN, WIN * WIN), 0, TABLE), jax.random.fold_in(keys[4], 1), 0, TABLE - 1).astype(jnp.int32)
    weights_in = centred(keys[5], (D, 4 * D + FF), D ** -0.5, 0.25)
    weights_out = centred(keys[6], (FF, D), FF ** -0.5, 0.125)
    norm_gains = jnp.clip(1.0 + 0.1 * jax.random.normal(keys[7], (2, D), jnp.float32), 0.5, 1.5)
    biases = centred(keys[8], (6 * D + FF,), 0.3, 1.75, (), jnp.float32)
    bias_table = centred(keys[9], (TABLE, HEADS), 1.0, 6.0, (), jnp.float32)
    master_in = centred(keys[10], (D, 4 * D + FF), D ** -0.5, 0.25, ((0, 8),), jnp.float32)
    master_out = centred(keys[11], (FF, D), FF ** -0.5, 0.125, ((0, 8),), jnp.float32)
    first_in = centred(keys[12], (D, 4 * D + FF), (0.06 * TOKENS ** 0.5), 96.0, ((0, 8),), jnp.float32)
    second_in = jnp.clip(jnp.exp(math.log(76.8) - 1.609438 * jax.random.uniform(keys[13], (D, 4 * D + FF), jnp.float32) ** shard_levels(keys[13], (D, 4 * D + FF), ((0, 8),), -0.2, 0.2)), 15.36, 76.8)
    first_out = centred(keys[14], (FF, D), (0.06 * TOKENS ** 0.5), 96.0, ((0, 8),), jnp.float32)
    second_out = jnp.clip(jnp.exp(math.log(76.8) - 1.609438 * jax.random.uniform(keys[15], (FF, D), jnp.float32) ** shard_levels(keys[15], (FF, D), ((0, 8),), -0.2, 0.2)), 15.36, 76.8)
    first_small = centred(keys[16], (8 * D + FF + TABLE * HEADS,), (0.05 * TOKENS ** 0.5), 80.0, (), jnp.float32)
    second_small = jnp.clip(jnp.exp(jax.random.uniform(keys[17], (8 * D + FF + TABLE * HEADS,), jnp.float32, math.log(7.68), math.log(38.4))), 7.68, 38.4)
    return dict(patches=patches, out_grad=out_grad, page_windows=page_windows, region_ids=region_ids, offset_index=offset_index, weights_in=weights_in, weights_out=weights_out, norm_gains=norm_gains, biases=biases, bias_table=bias_table, master_in=master_in, master_out=master_out, first_in=first_in, second_in=second_in, first_out=first_out, second_out=second_out, first_small=first_small, second_small=second_small)


NORM_EPS = 1e-05
BETA_ONE = 0.9
BETA_TWO = 0.999
LEARN_RATE = 0.04
WEIGHT_DECAY = 0.05
ADAM_EPS = 1e-08
MASK_VALUE = -1000000000.0
HIGH = lax.Precision.HIGHEST

@jax.custom_vjp
def low(v):
    return lax.optimization_barrier(v.astype(jnp.bfloat16)).astype(jnp.float32)

@jax.custom_vjp
def low_back(v):
    return v

def low_keep(v):
    return (low(v), None)

def low_pass(kept, grad):
    return (grad,)

def back_keep(v):
    return (v, None)

def back_low(kept, grad):
    return (low(grad),)
low.defvjp(low_keep, low_pass)
low_back.defvjp(back_keep, back_low)

def layer_norm(value, gain, offset):
    centre = lax.optimization_barrier(jnp.mean(value, axis=-1, keepdims=True))
    centered = value - centre
    spread = lax.rsqrt(lax.optimization_barrier(jnp.mean(centered * centered, axis=-1, keepdims=True)) + NORM_EPS)
    return centered * spread * gain + offset

def to_windows(field, window):
    pages, height, width = (field.shape[0], field.shape[1], field.shape[2])
    count = width // window
    rest = field.shape[3:]
    shaped = field.reshape((pages, height // window, window, count, window) + rest)
    order = (0, 1, 3, 2, 4) + tuple(range(5, 5 + len(rest)))
    return shaped.transpose(order).reshape((pages * (height // window) * count, window * window) + rest)

def from_windows(tiles, pages, height, width, window):
    count = width // window
    rest = tiles.shape[2:]
    shaped = tiles.reshape((pages, height // window, count, window, window) + rest)
    order = (0, 1, 3, 2, 4) + tuple(range(5, 5 + len(rest)))
    return shaped.transpose(order).reshape((pages, height, width) + rest)

def column_tables(page_windows, width, window, offset):
    columns = jnp.arange(width, dtype=jnp.int32)[None, :]
    live_width = page_windows.astype(jnp.int32)[:, None] * window
    inside = columns < live_width
    forward_cols = jnp.where(inside, (columns + offset) % live_width, columns)
    backward_cols = jnp.where(inside, (columns - offset) % live_width, columns)
    return (inside, forward_cols, backward_cols)

def pick_columns(field, table):
    return jax.vmap(lambda page, cols: page[:, cols])(field, table)

def block_forward(field, regions, offset_index, params):
    w_in, w_out, gains, biases, table = params
    tiles = to_windows(field[None], WIN)
    labels = to_windows(regions[None], WIN)
    groups, tokens = (tiles.shape[0], tiles.shape[1])
    zeros = jnp.zeros((D,), jnp.float32)
    bias_qkv = jnp.concatenate([biases[D:2 * D], zeros, biases[2 * D:3 * D]])
    norm_one = low(layer_norm(tiles, gains[0], biases[0:D]))
    qkv = jnp.einsum('gtd,de->gte', norm_one, w_in[:, :3 * D], precision=HIGH) + bias_qkv
    qkv = low(low_back(qkv))
    query = qkv[..., :D].reshape(groups, tokens, HEADS, HEAD)
    key_part = qkv[..., D:2 * D].reshape(groups, tokens, HEADS, HEAD)
    value = qkv[..., 2 * D:].reshape(groups, tokens, HEADS, HEAD)
    table_bias = table[offset_index].transpose(2, 0, 1)
    scores = jnp.einsum('gqhe,gkhe->ghqk', query, key_part, precision=HIGH) * HEAD ** (-0.5) + table_bias[None]
    same = labels[:, :, None] == labels[:, None, :]
    scores = low_back(jnp.where(same[:, None], scores, MASK_VALUE))
    probs = jax.nn.softmax(scores, axis=-1)
    attended = jnp.einsum('ghqk,gkhe->gqhe', low(probs), value, precision=HIGH)
    attended = low(low_back(attended)).reshape(groups, tokens, D)
    branch = low_back(jnp.einsum('gtd,de->gte', attended, w_in[:, 3 * D:4 * D], precision=HIGH) + biases[3 * D:4 * D])
    first = tiles + branch
    norm_two = low(layer_norm(first, gains[1], biases[4 * D:5 * D]))
    pre_act = low_back(jnp.einsum('gtd,df->gtf', norm_two, w_in[:, 4 * D:], precision=HIGH) + biases[6 * D:])
    act = low(jax.nn.gelu(pre_act, approximate=False))
    mlp = low_back(jnp.einsum('gtf,fd->gtd', act, w_out, precision=HIGH) + biases[5 * D:6 * D])
    result = first + mlp
    return from_windows(result, 1, PAGE_ROWS, COLS, WIN)[0]

def adam_update(master, first, second, grad):
    moment = BETA_ONE * first + (1.0 - BETA_ONE) * grad
    square = BETA_TWO * second + (1.0 - BETA_TWO) * grad * grad
    fix_one = 1.0 - BETA_ONE ** STEP
    fix_two = 1.0 - BETA_TWO ** STEP
    fresh = master - LEARN_RATE * (moment / fix_one / (jnp.sqrt(square / fix_two) + ADAM_EPS) + WEIGHT_DECAY * master)
    return (fresh, moment, square)

def reference(patches, out_grad, page_windows, region_ids, offset_index, weights_in, weights_out, norm_gains, biases, bias_table, master_in, master_out, first_in, second_in, first_out, second_out, first_small, second_small):
    inside, forward_cols, backward_cols = column_tables(page_windows, COLS, WIN, SHIFT)
    live = inside.astype(jnp.float32)[:, None, :, None]
    shifted = pick_columns(jnp.roll(patches.astype(jnp.float32), -SHIFT, axis=1), forward_cols)
    cotangent = pick_columns(jnp.roll(out_grad.astype(jnp.float32), -SHIFT, axis=1), forward_cols) * live
    params = (weights_in.astype(jnp.float32), weights_out.astype(jnp.float32), norm_gains, biases, bias_table)

    def forward(fields, weights):
        step_fn = jax.checkpoint(lambda item: block_forward(item[0], item[1], offset_index, weights))
        return lax.map(step_fn, (fields, region_ids))
    result, pullback = jax.vjp(forward, shifted, params)
    grad_shifted, grads = pullback(cotangent)
    grad_in, grad_out, grad_gains, grad_biases, grad_table = grads
    mixed = jnp.roll(pick_columns(result * live, backward_cols), SHIFT, axis=1).astype(jnp.bfloat16)
    patch_grad = jnp.roll(pick_columns(grad_shifted * live, backward_cols), SHIFT, axis=1).astype(jnp.bfloat16)
    grad_small = jnp.concatenate([grad_gains.reshape(-1), grad_biases, grad_table.reshape(-1)])
    small_master = jnp.concatenate([norm_gains.reshape(-1), biases, bias_table.reshape(-1)])
    new_in, moment_in, square_in = adam_update(master_in, first_in, second_in, grad_in)
    new_out, moment_out, square_out = adam_update(master_out, first_out, second_out, grad_out)
    new_small, moment_small, square_small = adam_update(small_master, first_small, second_small, grad_small)
    return (mixed, patch_grad, new_in, moment_in, square_in, new_out, moment_out, square_out, new_small, moment_small, square_small)
```

```python
import functools
import math

import jax
import jax.numpy as jnp
from jax import lax
from jax.experimental import pallas as pl
from jax.experimental.pallas import tpu as pltpu
from jax.sharding import PartitionSpec as P

STEP = 10
NORM_EPS = 1e-05
BETA_ONE = 0.9
BETA_TWO = 0.999
LEARN_RATE = 0.04
WEIGHT_DECAY = 0.05
ADAM_EPS = 1e-08
MASK_VALUE = -1000000000.0

F32 = jnp.float32
B16 = jnp.bfloat16
LOG2E = math.log2(math.e)
VMEM_LIMIT = 60 * 2**20

QUAD = 4
SLOT = 128
KEYS = 104


def dot(left, right, form="NN"):
    sides = {
        "NN": ((1,), (0,)),
        "NT": ((1,), (1,)),
        "TN": ((0,), (0,)),
    }[form]
    return lax.dot_general(left, right, (sides, ((), ())), preferred_element_type=F32)


def load_band(band, low_ref, high_ref, live, half, width, window, least):
    band[:half, :width] = low_ref[...].astype(F32)
    band[half:, :width] = high_ref[...].astype(F32)
    band[:, width:] = jnp.zeros((window, band.shape[1] - width, band.shape[2]), F32)
    wrap_band(band, live, half, width, window, least)


def wrap_band(band, live, half, width, window, least):
    for count in range(least, width // window + 1):
        at = slice(count * window, count * window + half)
        band[:, at] = jnp.where(live == count, band[:, :half], band[:, at])


def unwrap_band(band, live, half, width, window, least):
    for count in range(least, width // window + 1):

        @pl.when(live == count)
        def _():
            edge = count * window
            band[:, :half] = band[:, edge : edge + half]
            band[:, edge:] = jnp.zeros((window, band.shape[1] - edge, band.shape[2]), F32)


def piece(band, row, base, place, window, half):
    start = window * place + half
    aligned = start // 8 * 8
    skip = start - aligned
    size = -(-(skip + window) // 8) * 8
    ref = band.at[row, pl.ds(pl.multiple_of(base, 8) + aligned, size), :]
    return ref, skip


def gather_window(band, base, place, window, half):
    parts = []
    for row in range(window):
        ref, skip = piece(band, row, base, place, window, half)
        parts.append(ref[skip : skip + window, :])
    return parts


def norm_stats(value):
    centre = jnp.mean(value, axis=-1, keepdims=True)
    centered = value - centre
    spread = lax.rsqrt(jnp.mean(centered * centered, axis=-1, keepdims=True) + NORM_EPS)
    return centered * spread, spread


def fold(value):
    rows, cols = value.shape
    return jnp.sum(value.reshape(rows // 8, 8, cols), axis=0)


MESH = pl.DeviceIdType.MESH


def remote(src, dst, send, recv, device):
    return pltpu.make_async_remote_copy(
        src_ref=src, dst_ref=dst, send_sem=send, recv_sem=recv, device_id=device, device_id_type=MESH
    )


def attn_forward_kernel(
    sizes,
    live_ref,
    patches_ref,
    grads_ref,
    low_ref,
    label_ref,
    off_ref,
    tab_ref,
    wqkv_ref,
    bqkv_ref,
    wproj_ref,
    vec_ref,
    x_ref,
    n1_ref,
    qkv_ref,
    probs_ref,
    att_ref,
    first_ref,
    n2_ref,
    grad_halo_ref,
    halo,
    send,
    recv,
    band,
    bias,
    scores,
    bdq,
    bdv,
    stacked,
    xs,
    ns,
):
    window, half, width, model, heads, least, pages, rows_count = sizes
    slots = window * window
    size_head = model // heads
    page, quad = pl.program_id(0), pl.program_id(1)
    live = live_ref[page]
    pairs = heads // 2
    row = lax.axis_index("rows")
    behind, ahead = lax.rem(row + rows_count - 1, rows_count), lax.rem(row + 1, rows_count)

    def halo_copy(p):
        return remote(
            patches_ref.at[p, pl.ds(0, half)], halo.at[p], send.at[p], recv.at[p], {"rows": behind}
        )

    def grad_copy(p):
        return remote(
            grads_ref.at[p, pl.ds(0, half)],
            grad_halo_ref.at[p],
            send.at[pages + p],
            recv.at[pages + p],
            {"rows": behind},
        )

    @pl.when(jnp.logical_and(page == 0, quad == 0))
    def _():
        barrier = pltpu.get_barrier_semaphore()
        for neighbour in (behind, ahead):
            pl.semaphore_signal(barrier, inc=1, device_id={"rows": neighbour}, device_id_type=MESH)
        pl.semaphore_wait(barrier, 2)
        for p in range(pages):
            halo_copy(p).start()
        for p in range(pages):
            grad_copy(p).start()
        off = off_ref[...]
        low, high = jnp.bitwise_and(off, 127), jnp.right_shift(off, 7)
        for h in range(heads):
            got = jnp.zeros((KEYS, SLOT), F32)
            for c in range(tab_ref.shape[1] // 128):
                source = jnp.broadcast_to(tab_ref[h : h + 1, 128 * c : 128 * c + 128], (KEYS, SLOT))
                picked = jnp.take_along_axis(source, low, axis=1, mode="promise_in_bounds")
                got = jnp.where(high == c, picked, got)
            bias[h] = got
        bdq[...] = jnp.zeros_like(bdq)
        bdv[...] = jnp.zeros_like(bdv)
        stacked[...] = jnp.zeros_like(stacked)

    for p in range(pages):

        @pl.when(jnp.logical_and(page == p, quad == 0))
        def _():
            halo_copy(p).wait()
            load_band(band, low_ref.at[0], halo.at[p], live, half, width, window, least)

    @pl.when(jnp.logical_and(page == pages - 1, quad == pl.num_programs(1) - 1))
    def _():
        for p in range(pages):
            grad_copy(p).wait()

    base = quad * (QUAD * window)
    for w in range(QUAD):
        for r, part in enumerate(gather_window(band, base, w, window, half)):
            at = slots * w + window * r
            xs[at : at + window, :] = part
    x = xs[...]
    x_ref[...] = x.astype(B16)
    xhat, _ = norm_stats(x)
    ns[...] = xhat * vec_ref[0:1, :] + vec_ref[1:2, :]
    for w in range(QUAD):
        n1_ref[SLOT * w : SLOT * w + slots, :] = ns[slots * w : slots * w + slots, :].astype(B16)
        n1_ref[SLOT * w + slots : SLOT * w + SLOT, :] = jnp.zeros((SLOT - slots, model), B16)
    scale = size_head**-0.5 * LOG2E
    n1 = n1_ref[...]
    for part in range(3):
        rows = slice(part * model, part * model + model)
        got = dot(wqkv_ref[rows, :], n1, "NT") + bqkv_ref[rows, :]
        if part == 0:
            got = got * scale
        qkv_ref[rows, :] = got.astype(B16)

    sames = []
    for w in range(QUAD):
        spread = jnp.broadcast_to(label_ref[0, w : w + 1, :], (SLOT, SLOT))
        sames.append((spread == spread.T)[:KEYS])
    pair = 2 * size_head

    def score(w, g):
        low = pair * g
        lanes = slice(SLOT * w, SLOT * w + SLOT)
        for j in range(2):
            at = slice(low + size_head * j, low + size_head * (j + 1))
            cols = slice(SLOT * j, SLOT * j + SLOT)
            bdq[w % 2, at, cols] = qkv_ref[at, lanes]
            values = slice(2 * model + low + size_head * j, 2 * model + low + size_head * (j + 1))
            bdv[w % 3, at, cols] = qkv_ref[values, lanes]
        keys = qkv_ref[model + low : model + low + pair, SLOT * w : SLOT * w + KEYS]
        scores[w % 2, g] = dot(keys, bdq[w % 2, low : low + pair, :], "TN")

    def soften(w, g):
        for j in range(2):
            cols = slice(SLOT * j, SLOT * j + SLOT)
            s = jnp.where(sames[w], scores[w % 2, g, :, cols] + bias[2 * g + j], MASK_VALUE)
            s = jnp.exp2(s - jnp.max(s, axis=0, keepdims=True))
            low_probs = (s * (1.0 / jnp.sum(s, axis=0, keepdims=True))).astype(B16)
            probs_ref[w, g, :KEYS, cols] = low_probs
            probs_ref[w, g, KEYS:, cols] = jnp.zeros((SLOT - KEYS, SLOT), B16)
            stacked[w % 2, g, SLOT * j : SLOT * j + KEYS, :] = low_probs

    def attend(w, g):
        low = pair * g
        got = dot(bdv[w % 3, low : low + pair, :], stacked[w % 2, g])
        att_ref[low : low + pair, SLOT * w : SLOT * w + SLOT] = got.astype(B16)

    for step in range(QUAD + 2):
        for g in range(pairs):
            if step < QUAD:
                score(step, g)
            if 1 <= step <= QUAD:
                soften(step - 1, g)
            if step >= 2:
                attend(step - 2, g)

    branch = dot(att_ref[...], wproj_ref[...], "TN")
    for w in range(QUAD):
        rows = slice(slots * w, slots * w + slots)
        first_ref[rows, :] = xs[rows, :] + branch[SLOT * w : SLOT * w + slots, :] + vec_ref[2:3, :]
    xhat, _ = norm_stats(first_ref[...])
    n2_ref[...] = (xhat * vec_ref[3:4, :] + vec_ref[4:5, :]).astype(B16)


def attn_forward(live, patches, out_grad, labels, off, tab, wqkv, bqkv, wproj, vecs, least):
    pages, window, width, model = patches.shape
    half = window // 2
    heads = tab.shape[0]
    quads = width // window // QUAD
    tokens = pages * window * width
    slots = window * window
    padded = pages * quads * QUAD * SLOT
    steps = (pages, quads)
    whole = lambda a: pl.BlockSpec(a.shape, lambda p, j: (0,) * a.ndim, pipeline_mode=pl.Buffered(1))
    at = lambda p, j: p * quads + j
    return pl.pallas_call(
        functools.partial(
            attn_forward_kernel,
            (window, half, width, model, heads, least, pages, lax.axis_size("rows")),
        ),
        grid=steps,
        in_specs=[
            pl.BlockSpec(memory_space=pltpu.SMEM),
            pl.BlockSpec(memory_space=pl.ANY),
            pl.BlockSpec(memory_space=pl.ANY),
            pl.BlockSpec((1, half, width, model), lambda p, j: (p, 1, 0, 0)),
            pl.BlockSpec((1, 8, SLOT), lambda p, j: (at(p, j), 0, 0)),
            whole(off),
            whole(tab),
            whole(wqkv),
            whole(bqkv),
            whole(wproj),
            whole(vecs),
        ],
        out_specs=[
            pl.BlockSpec((QUAD * slots, model), lambda p, j: (at(p, j), 0)),
            pl.BlockSpec((QUAD * SLOT, model), lambda p, j: (at(p, j), 0)),
            pl.BlockSpec((3 * model, QUAD * SLOT), lambda p, j: (0, at(p, j))),
            pl.BlockSpec((QUAD, heads // 2, SLOT, 2 * SLOT), lambda p, j: (at(p, j), 0, 0, 0)),
            pl.BlockSpec((model, QUAD * SLOT), lambda p, j: (0, at(p, j))),
            pl.BlockSpec((QUAD * slots, model), lambda p, j: (at(p, j), 0)),
            pl.BlockSpec((QUAD * slots, model), lambda p, j: (at(p, j), 0)),
            pl.BlockSpec(memory_space=pl.ANY),
        ],
        out_shape=[
            jax.ShapeDtypeStruct((tokens, model), B16),
            jax.ShapeDtypeStruct((padded, model), B16),
            jax.ShapeDtypeStruct((3 * model, padded), B16),
            jax.ShapeDtypeStruct((pages * quads * QUAD, heads // 2, SLOT, 2 * SLOT), B16),
            jax.ShapeDtypeStruct((model, padded), B16),
            jax.ShapeDtypeStruct((tokens, model), F32),
            jax.ShapeDtypeStruct((tokens, model), B16),
            jax.ShapeDtypeStruct((pages, half, width, model), B16),
        ],
        scratch_shapes=[
            pltpu.VMEM((pages, half, width, model), B16),
            pltpu.SemaphoreType.DMA((2 * pages,)),
            pltpu.SemaphoreType.DMA((2 * pages,)),
            pltpu.VMEM((window, width + 8, model), F32),
            pltpu.VMEM((heads, KEYS, SLOT), F32),
            pltpu.VMEM((2, heads // 2, KEYS, 2 * SLOT), F32),
            pltpu.VMEM((2, model, 2 * SLOT), B16),
            pltpu.VMEM((3, model, 2 * SLOT), B16),
            pltpu.VMEM((2, heads // 2, 2 * SLOT, SLOT), B16),
            pltpu.VMEM((QUAD * slots, model), F32),
            pltpu.VMEM((QUAD * slots, model), F32),
        ],
        compiler_params=pltpu.CompilerParams(
            vmem_limit_bytes=VMEM_LIMIT, collective_id=1, has_side_effects=True
        ),
    )(live, patches, out_grad, patches, labels, off, tab, wqkv, bqkv, wproj, vecs)


MLP_COLS = 512
MLP_ROWS = 480


def mlp_kernel(
    sizes,
    live_ref,
    low_ref,
    high_ref,
    n2_ref,
    first_ref,
    wup_ref,
    wout_ref,
    bup_ref,
    vec_ref,
    dwup_ref,
    dwout_ref,
    dbup_ref,
    gf_ref,
    own_ref,
    next_ref,
    sums_ref,
    band,
    cot,
    res,
    dn2,
    act_all,
    pre_all,
):
    window, half, width, model, least, share = sizes
    pages = low_ref.shape[0]
    slots = window * window
    count = width // window
    quads = count // QUAD
    chunk = pl.program_id(0)
    tokens = n2_ref.shape[0]
    cols = wup_ref.shape[1]

    @pl.when(chunk == 0)
    def _():
        for page in range(pages):
            live = live_ref[page]
            load_band(band, low_ref.at[page], high_ref.at[page], live, half, width, window, least)

            def body(j, carry):
                for w in range(QUAD):
                    alive = jnp.where(j * QUAD + w < live, 1.0, 0.0)
                    for r, part in enumerate(gather_window(band, j * QUAD * window, w, window, half)):
                        at = slots * w + window * r
                        gf_ref[at : at + window, :] = part * alive
                rows = pl.ds(pl.multiple_of((page * quads + j) * QUAD * slots, 16), QUAD * slots)
                cot[rows, :] = gf_ref[: QUAD * slots, :].astype(B16)
                return carry

            lax.fori_loop(0, quads, body, 0)

    def body(i, total):
        rows = pl.ds(pl.multiple_of(i * MLP_ROWS, 16), MLP_ROWS)
        grad = cot[rows, :]
        pre = dot(n2_ref[rows, :], wup_ref[...]) + bup_ref[...]
        grad_act = dot(grad, wout_ref[...], "NT")
        share = 0.5 * (1.0 + lax.erf(pre * 0.5**0.5))
        act = (pre * share).astype(B16)
        slope = share + pre * (jnp.exp2((-0.5 * LOG2E) * pre * pre) * (2.0 * math.pi) ** -0.5)
        grad_pre = (grad_act * slope).astype(B16)
        act_all[rows, :] = act
        pre_all[rows, :] = grad_pre
        up = dot(act, wout_ref[...])
        down = dot(grad_pre, wup_ref[...], "NT")

        @pl.when(chunk == 0)
        def _():
            res[rows, :] = up
            dn2[rows, :] = down

        @pl.when(chunk > 0)
        def _():
            res[rows, :] += up
            dn2[rows, :] += down

        return total + fold(grad_pre.astype(F32))

    total = lax.fori_loop(0, tokens // MLP_ROWS, body, jnp.zeros((8, cols), F32))
    dbup_ref[...] = jnp.sum(total, axis=0, keepdims=True)
    grad_out = dot(act_all[...], cot[...], "TN").astype(B16)
    for s in range(dwout_ref.shape[0] // share):
        for a in range(dwout_ref.shape[1] // model):
            at = (s * (dwout_ref.shape[1] // model) + a) * share
            dwout_ref[share * s : share * s + share, model * a : model * a + model] = grad_out[at : at + share, :]
    dwup_ref[...] = dot(n2_ref[...], pre_all[...], "TN").astype(B16)

    @pl.when(chunk == pl.num_programs(0) - 1)
    def _():
        sums_ref[...] = jnp.zeros_like(sums_ref)
        for page in range(pages):
            live = live_ref[page]

            def body(j, carry):
                at = pl.multiple_of((page * quads + j) * QUAD * slots, 16)
                rows = pl.ds(at, QUAD * slots)
                first = first_ref[rows, :]
                res[rows, :] += first + vec_ref[1:2, :]
                xhat, spread = norm_stats(first)
                grad = dn2[rows, :]
                given = cot[rows, :].astype(F32)
                scaled = grad * vec_ref[0:1, :]
                mean_one = jnp.mean(scaled, axis=-1, keepdims=True)
                mean_two = jnp.mean(scaled * xhat, axis=-1, keepdims=True)
                whole = given + spread * (scaled - mean_one - xhat * mean_two)
                gf_ref[rows, :] = whole
                sums_ref[0:8, :] += fold(grad * xhat)
                sums_ref[8:16, :] += fold(grad)
                sums_ref[16:24, :] += fold(given)
                sums_ref[24:32, :] += fold(whole)
                for w in range(QUAD):
                    for r in range(window):
                        ref, skip = piece(band, r, j * QUAD * window, w, window, half)
                        ref[skip : skip + window, :] = res[
                            pl.ds(at + slots * w // 8 * 8, slots + 4), :
                        ][slots * w % 8 + window * r : slots * w % 8 + window * r + window, :]
                return carry

            lax.fori_loop(0, quads, body, 0)
            unwrap_band(band, live, half, width, window, least)
            own_ref[page] = band[:half, :width].astype(B16)
            next_ref[page] = band[half:, :width].astype(B16)


def mlp(live, out_grad, halo, n2, first, weights_in, weights_out, bup, vecs, least, share):
    pages, window, width, model = out_grad.shape
    half = window // 2
    tokens = n2.shape[0]
    hidden = weights_out.shape[0]
    skip = (weights_in.shape[1] - hidden) // MLP_COLS
    once = pl.Buffered(1)
    whole = lambda a: pl.BlockSpec(a.shape, lambda c: (0,) * a.ndim, pipeline_mode=once)
    band_block = (pages, half, width, model)
    return pl.pallas_call(
        functools.partial(mlp_kernel, (window, half, width, model, least, share)),
        grid=(hidden // MLP_COLS,),
        in_specs=[
            pl.BlockSpec(memory_space=pltpu.SMEM),
            pl.BlockSpec(band_block, lambda c: (0, 1, 0, 0), pipeline_mode=once),
            pl.BlockSpec(band_block, lambda c: (0, 0, 0, 0), pipeline_mode=once),
            whole(n2),
            whole(first),
            pl.BlockSpec((model, MLP_COLS), lambda c: (0, c + skip)),
            pl.BlockSpec((MLP_COLS, model), lambda c: (c, 0)),
            pl.BlockSpec((1, MLP_COLS), lambda c: (0, c)),
            whole(vecs),
        ],
        out_specs=[
            pl.BlockSpec((model, MLP_COLS), lambda c: (0, c)),
            pl.BlockSpec((model * MLP_COLS // hidden, hidden), lambda c: (c, 0)),
            pl.BlockSpec((1, MLP_COLS), lambda c: (0, c)),
            pl.BlockSpec((tokens, model), lambda c: (0, 0), pipeline_mode=once),
            pl.BlockSpec(band_block, lambda c: (0, 1, 0, 0), pipeline_mode=once),
            pl.BlockSpec(band_block, lambda c: (0, 0, 0, 0), pipeline_mode=once),
            pl.BlockSpec((32, model), lambda c: (0, 0)),
        ],
        out_shape=[
            jax.ShapeDtypeStruct((model, hidden), B16),
            jax.ShapeDtypeStruct((model, hidden), B16),
            jax.ShapeDtypeStruct((1, hidden), F32),
            jax.ShapeDtypeStruct((tokens, model), F32),
            jax.ShapeDtypeStruct(out_grad.shape, B16),
            jax.ShapeDtypeStruct(band_block, B16),
            jax.ShapeDtypeStruct((32, model), F32),
        ],
        scratch_shapes=[
            pltpu.VMEM((window, width + 8, model), F32),
            pltpu.VMEM((tokens, model), B16),
            pltpu.VMEM((tokens, model), F32),
            pltpu.VMEM((tokens, model), F32),
            pltpu.VMEM((tokens, MLP_COLS), B16),
            pltpu.VMEM((tokens, MLP_COLS), B16),
        ],
        compiler_params=pltpu.CompilerParams(vmem_limit_bytes=VMEM_LIMIT),
    )(live, out_grad, halo, n2, first, weights_in, weights_out, bup, vecs)


def attn_backward_kernel(
    sizes,
    live_ref,
    gf_ref,
    x_ref,
    n1_ref,
    qkv_ref,
    probs_ref,
    att_ref,
    wproj_ref,
    wqkv_ref,
    vec_ref,
    dwa_ref,
    dbqkv_ref,
    dscore_ref,
    sums_ref,
    own_ref,
    next_ref,
    band,
    gbp,
    datt,
    dprobs,
    bdq,
    bdk,
    bdo,
    stacked,
    beside,
    dqkv,
    dwq,
    dwp,
    compact,
):
    window, half, width, model, heads, least = sizes
    slots = window * window
    size_head = model // heads
    page, quad = pl.program_id(0), pl.program_id(1)
    live = live_ref[page]
    pairs = heads // 2
    pair = 2 * size_head

    @pl.when(jnp.logical_and(page == 0, quad == 0))
    def _():
        for ref in (bdq, bdk, bdo, stacked, beside, gbp, dwq, dwp, dbqkv_ref, dscore_ref, sums_ref):
            ref[...] = jnp.zeros_like(ref)

    for w in range(QUAD):
        gbp[SLOT * w : SLOT * w + slots, :] = gf_ref[slots * w : slots * w + slots, :].astype(B16)
    datt[...] = dot(wproj_ref[...], gbp[...], "NT").astype(B16)
    dwp[...] += dot(att_ref[...], gbp[...])

    @pl.when(quad * QUAD >= live)
    def _():
        dqkv[...] = jnp.zeros_like(dqkv)

    @pl.when(quad * QUAD < live)
    def _():
        ratio = size_head**-0.5

        def score(w, g):
            low = pair * g
            lanes = slice(SLOT * w, SLOT * w + SLOT)
            for j in range(2):
                at = slice(low + size_head * j, low + size_head * (j + 1))
                keys = slice(model + low + size_head * j, model + low + size_head * (j + 1))
                cols = slice(SLOT * j, SLOT * j + SLOT)
                bdo[w % 3, at, cols] = datt[at, lanes]
                bdq[w % 3, at, cols] = qkv_ref[at, lanes]
                bdk[w % 3, at, cols] = qkv_ref[keys, lanes]
            values = qkv_ref[2 * model + low : 2 * model + low + pair, SLOT * w : SLOT * w + KEYS]
            dprobs[w % 2, g] = dot(values, bdo[w % 3, low : low + pair, :], "TN")

        def soften(w, g):
            probs = probs_ref[w, g, :KEYS, :].astype(F32)
            term = probs * dprobs[w % 2, g]
            grad = term - probs * jnp.sum(term, axis=0, keepdims=True)
            dscore_ref[g] += grad
            low_grad = grad.astype(B16)
            beside[w % 2, g, :KEYS, :] = low_grad
            for j in range(2):
                stacked[w % 2, g, SLOT * j : SLOT * j + KEYS, :] = low_grad[:, SLOT * j : SLOT * j + SLOT]

        def attend(w, g):
            low = pair * g
            lanes = slice(SLOT * w, SLOT * w + SLOT)
            rows = slice(low, low + pair)
            got = dot(bdk[w % 3, rows, :], stacked[w % 2, g]) * ratio
            dqkv[low : low + pair, lanes] = got.astype(B16)
            got = dot(bdq[w % 3, rows, :], beside[w % 2, g], "NT") * (1.0 / LOG2E)
            dqkv[model + low : model + low + pair, lanes] = got.astype(B16)
            got = dot(bdo[w % 3, rows, :], probs_ref[w, g], "NT")
            dqkv[2 * model + low : 2 * model + low + pair, lanes] = got.astype(B16)

        for step in range(QUAD + 2):
            for g in range(pairs):
                if step < QUAD:
                    score(step, g)
                if 1 <= step <= QUAD:
                    soften(step - 1, g)
                if step >= 2:
                    attend(step - 2, g)

    n1 = n1_ref[...]
    for part in range(3):
        rows = slice(part * model, part * model + model)
        grad = dqkv[rows, :]
        dwq[rows, :] += dot(grad, n1)
        wide = grad.astype(F32)
        both = wide[:, :SLOT]
        for w in range(1, QUAD):
            both = both + wide[:, SLOT * w : SLOT * w + SLOT]
        dbqkv_ref[rows, :] += both
    dn1 = dot(dqkv[...], wqkv_ref[...], "TN")
    for w in range(QUAD):
        compact[slots * w : slots * w + slots, :] = dn1[SLOT * w : SLOT * w + slots, :]
    grad = compact[...]
    xhat, spread = norm_stats(x_ref[...].astype(F32))
    scaled = grad * vec_ref[0:1, :]
    mean_one = jnp.mean(scaled, axis=-1, keepdims=True)
    mean_two = jnp.mean(scaled * xhat, axis=-1, keepdims=True)
    sums_ref[0:8, :] += fold(grad * xhat)
    sums_ref[8:16, :] += fold(grad)
    compact[...] = gf_ref[...] + spread * (scaled - mean_one - xhat * mean_two)
    for w in range(QUAD):
        for r in range(window):
            ref, skip = piece(band, r, quad * QUAD * window, w, window, half)
            at = slots * w + window * r
            ref[skip : skip + window, :] = compact[at : at + window, :]

    @pl.when(quad == pl.num_programs(1) - 1)
    def _():
        unwrap_band(band, live, half, width, window, least)
        own_ref[0] = band[:half, :width].astype(B16)
        next_ref[0] = band[half:, :width].astype(B16)

    @pl.when(jnp.logical_and(page == pl.num_programs(0) - 1, quad == pl.num_programs(1) - 1))
    def _():
        dwa_ref[:, 3 * model :] = dwp[...].astype(B16)
        for part in range(3):
            rows = slice(part * model, part * model + model)
            dwa_ref[:, rows] = dwq[rows, :].T.astype(B16)


def attn_backward(live, gf, x, n1, qkv, probs, att, wproj, wqkv, vecs, shape, heads, least):
    pages, window, width, model = shape
    half = window // 2
    quads = width // window // QUAD
    slots = window * window
    once = pl.Buffered(1)
    whole = lambda a: pl.BlockSpec(a.shape, lambda p, j: (0,) * a.ndim, pipeline_mode=once)
    held = lambda s: pl.BlockSpec(s, lambda p, j: (0,) * len(s), pipeline_mode=once)
    at = lambda p, j: p * quads + j
    pairs = heads // 2
    return pl.pallas_call(
        functools.partial(attn_backward_kernel, (window, half, width, model, heads, least)),
        grid=(pages, quads),
        in_specs=[
            pl.BlockSpec(memory_space=pltpu.SMEM),
            pl.BlockSpec((QUAD * slots, model), lambda p, j: (at(p, j), 0)),
            pl.BlockSpec((QUAD * slots, model), lambda p, j: (at(p, j), 0)),
            pl.BlockSpec((QUAD * SLOT, model), lambda p, j: (at(p, j), 0)),
            pl.BlockSpec((3 * model, QUAD * SLOT), lambda p, j: (0, at(p, j))),
            pl.BlockSpec((QUAD, pairs, SLOT, 2 * SLOT), lambda p, j: (at(p, j), 0, 0, 0)),
            pl.BlockSpec((model, QUAD * SLOT), lambda p, j: (0, at(p, j))),
            whole(wproj),
            whole(wqkv),
            whole(vecs),
        ],
        out_specs=[
            held((model, 4 * model)),
            held((3 * model, SLOT)),
            held((pairs, KEYS, 2 * SLOT)),
            held((16, model)),
            pl.BlockSpec((1, half, width, model), lambda p, j: (p, 1, 0, 0)),
            pl.BlockSpec((1, half, width, model), lambda p, j: (p, 0, 0, 0)),
        ],
        out_shape=[
            jax.ShapeDtypeStruct((model, 4 * model), B16),
            jax.ShapeDtypeStruct((3 * model, SLOT), F32),
            jax.ShapeDtypeStruct((pairs, KEYS, 2 * SLOT), F32),
            jax.ShapeDtypeStruct((16, model), F32),
            jax.ShapeDtypeStruct(shape, B16),
            jax.ShapeDtypeStruct((pages, half, width, model), B16),
        ],
        scratch_shapes=[
            pltpu.VMEM((window, width + 8, model), F32),
            pltpu.VMEM((QUAD * SLOT, model), B16),
            pltpu.VMEM((model, QUAD * SLOT), B16),
            pltpu.VMEM((2, pairs, KEYS, 2 * SLOT), F32),
            pltpu.VMEM((3, model, 2 * SLOT), B16),
            pltpu.VMEM((3, model, 2 * SLOT), B16),
            pltpu.VMEM((3, model, 2 * SLOT), B16),
            pltpu.VMEM((2, pairs, 2 * SLOT, SLOT), B16),
            pltpu.VMEM((2, pairs, SLOT, 2 * SLOT), B16),
            pltpu.VMEM((3 * model, QUAD * SLOT), B16),
            pltpu.VMEM((3 * model, model), F32),
            pltpu.VMEM((model, model), F32),
            pltpu.VMEM((QUAD * slots, model), F32),
        ],
        compiler_params=pltpu.CompilerParams(vmem_limit_bytes=VMEM_LIMIT),
    )(live, gf, x, n1, qkv, probs, att, wproj, wqkv, vecs)


def table_sum(off_ref, grad_ref, out_ref):
    heads = grad_ref.shape[0]
    chunks = out_ref.shape[0] // heads
    rows = 128 * chunks
    step = 1024
    names = lax.broadcasted_iota(jnp.int32, (rows, step), 0)
    total = jnp.zeros((3 * heads, rows), F32)
    for i in range(off_ref.shape[1] // step):
        at = slice(step * i, step * i + step)
        hot = jnp.where(names == off_ref[:, at], 1.0, 0.0).astype(B16)
        value = grad_ref[:, at]
        high = value.astype(B16)
        rest = value - high.astype(F32)
        middle = rest.astype(B16)
        low = (rest - middle.astype(F32)).astype(B16)
        total += dot(jnp.concatenate([high, middle, low], axis=0), hot, "NT")
    total = total[:heads] + total[heads : 2 * heads] + total[2 * heads :]
    for c in range(chunks):
        out_ref[heads * c : heads * c + heads, :] = total[:, 128 * c : 128 * c + 128]


def sums_kernel(
    peers,
    ga_ref,
    gb_ref,
    gc_ref,
    small_ref,
    mixed_ref,
    patch_ref,
    off_ref,
    dscore_ref,
    outa_ref,
    outb_ref,
    outc_ref,
    small_out_ref,
    mixed_out_ref,
    patch_out_ref,
    own1,
    rec1,
    s1,
    rec2,
    s2,
    rec3,
    s3,
    rec4,
    small_all,
    small1,
    small2,
    small2s,
    small3,
    small3s,
    local,
    send1,
    recv1,
    send2,
    recv2,
    send3,
    recv3,
    send4,
    recv4,
    tiny_send,
    tiny_recv,
    halo_send,
    halo_recv,
):
    pages, chips, table_at, heads = peers
    grads = (ga_ref, gb_ref, gc_ref)
    outs = (outa_ref, outb_ref, outc_ref)
    page, row = lax.axis_index("page"), lax.axis_index("rows")
    chip, core = row // 2, row % 2
    other = 2 * chip + 1 - core
    share, cols = outa_ref.shape
    piece_cols = cols // pages

    def page_peer(d):
        return lax.rem(page + d, pages)

    def chip_peer(d):
        return lax.rem(chip + d, chips)

    barrier = pltpu.get_barrier_semaphore()
    pl.semaphore_signal(barrier, inc=1, device_id={"rows": other}, device_id_type=MESH)
    for d in range(1, pages):
        pl.semaphore_signal(barrier, inc=1, device_id={"page": page_peer(d)}, device_id_type=MESH)
    for d in range(1, chips):
        pl.semaphore_signal(
            barrier, inc=1, device_id={"rows": 2 * chip_peer(d) + core}, device_id_type=MESH
        )
    behind, ahead = lax.rem(row + 2 * chips - 1, 2 * chips), lax.rem(row + 1, 2 * chips)
    for neighbour in (behind, ahead):
        pl.semaphore_signal(barrier, inc=1, device_id={"rows": neighbour}, device_id_type=MESH)
    pl.semaphore_wait(barrier, pages + chips + 1)

    def rows_of(ref, z, c):
        return ref.at[pl.ds(pl.multiple_of((2 * z + c) * share, 16), share), :]

    started = {}

    def phase_one(m):
        copies = []
        for z in range(chips):
            copy = remote(
                rows_of(grads[m], z, 1 - core),
                rec1.at[m, z],
                send1.at[m, z],
                recv1.at[m, z],
                {"rows": other},
            )
            copy.start()
            mine = pltpu.make_async_copy(rows_of(grads[m], z, core), own1.at[m, z], local.at[m, z])
            mine.start()
            copies += [copy, mine]
        started[1, m] = copies

    def phase_two(m):
        for copy in started[1, m]:
            copy.wait()
        for q in range(pages):
            at = slice(piece_cols * q, piece_cols * q + piece_cols)
            total = own1[m, :, :, at].astype(F32) + rec1[m, :, :, at].astype(F32)
            s1[m, q] = total.astype(B16)
        copies = []
        for d in range(1, pages):
            copy = remote(
                s1.at[m, page_peer(d)],
                rec2.at[m, page],
                send2.at[m, d],
                recv2.at[m, d],
                {"page": page_peer(d)},
            )
            copy.start()
            copies.append(copy)
        rec2[m, page] = s1[m, page]
        started[2, m] = copies

    def phase_three(m):
        for copy in started[2, m]:
            copy.wait()
        total = rec2[m, 0].astype(F32)
        for q in range(1, pages):
            total = total + rec2[m, q].astype(F32)
        s2[m] = total.astype(B16)
        copies = []
        for d in range(1, chips):
            copy = remote(
                s2.at[m, chip_peer(d)],
                rec3.at[m, chip],
                send3.at[m, d],
                recv3.at[m, d],
                {"rows": 2 * chip_peer(d) + core},
            )
            copy.start()
            copies.append(copy)
        rec3[m, chip] = s2[m, chip]
        started[3, m] = copies

    def phase_four(m):
        for copy in started[3, m]:
            copy.wait()
        total = rec3[m, 0].astype(F32)
        for z in range(1, chips):
            total = total + rec3[m, z].astype(F32)
        s3[m] = total.astype(B16)
        copies = []
        for d in range(1, pages):
            copy = remote(
                s3.at[m], rec4.at[m, page], send4.at[m, d], recv4.at[m, d], {"page": page_peer(d)}
            )
            copy.start()
            copies.append(copy)
        rec4[m, page] = s3[m]
        started[4, m] = copies

    def finish(m):
        for copy in started[4, m]:
            copy.wait()
        for q in range(pages):
            outs[m][:, piece_cols * q : piece_cols * q + piece_cols] = rec4[m, q].astype(F32)

    count = len(grads)
    for m in range(count):
        phase_one(m)
    halos = [
        remote(mixed_ref, mixed_out_ref, halo_send.at[0], halo_recv.at[0], {"rows": ahead}),
        remote(patch_ref, patch_out_ref, halo_send.at[1], halo_recv.at[1], {"rows": ahead}),
    ]
    for copy in halos:
        copy.start()
    phase_two(0)
    small_all[...] = small_ref[...]
    table_sum(off_ref, dscore_ref, small_all.at[pl.ds(table_at, small_all.shape[0] - table_at), :])
    tiny = remote(small_all, small1, tiny_send.at[0], tiny_recv.at[0], {"rows": other})
    tiny.start()
    for m in range(1, count):
        phase_two(m)
    tiny.wait()
    small2s[...] = small_all[...] + small1[...]
    small2[page] = small2s[...]
    tinies = []
    for d in range(1, pages):
        copy = remote(small2s, small2.at[page], tiny_send.at[d], tiny_recv.at[d], {"page": page_peer(d)})
        copy.start()
        tinies.append(copy)
    for m in range(count):
        phase_three(m)
    for copy in tinies:
        copy.wait()
    total = small2[0]
    for q in range(1, pages):
        total = total + small2[q]
    small3s[...] = total
    small3[chip] = total
    tinies = []
    for d in range(1, chips):
        copy = remote(
            small3s,
            small3.at[chip],
            tiny_send.at[pages + d],
            tiny_recv.at[pages + d],
            {"rows": 2 * chip_peer(d) + core},
        )
        copy.start()
        tinies.append(copy)
    for m in range(count):
        phase_four(m)
    for copy in tinies:
        copy.wait()
    total = small3[0]
    for z in range(1, chips):
        total = total + small3[z]
    small_out_ref[...] = total
    for m in range(count):
        finish(m)
    for copy in halos:
        copy.wait()


def sums(grads, small, mixed, patch, off, dscore, table_at, pages, rows):
    chips = rows // 2
    model, cols = grads[0].shape
    share, piece_cols = model // rows, cols // pages
    n = len(grads)
    vmem = pl.BlockSpec(memory_space=pltpu.VMEM)
    dma = pltpu.SemaphoreType.DMA
    return pl.pallas_call(
        functools.partial(sums_kernel, (pages, chips, table_at, dscore.shape[0])),
        in_specs=[pl.BlockSpec(memory_space=pl.ANY)] * n
        + [vmem]
        + [pl.BlockSpec(memory_space=pl.ANY)] * 2
        + [vmem] * 2,
        out_specs=[vmem] * (n + 1) + [pl.BlockSpec(memory_space=pl.ANY)] * 2,
        out_shape=[jax.ShapeDtypeStruct((share, cols), F32)] * n
        + [jax.ShapeDtypeStruct(a.shape, a.dtype) for a in (small, mixed, patch)],
        scratch_shapes=[
            pltpu.VMEM((n, chips, share, cols), B16),
            pltpu.VMEM((n, chips, share, cols), B16),
            pltpu.VMEM((n, pages, chips, share, piece_cols), B16),
            pltpu.VMEM((n, pages, chips, share, piece_cols), B16),
            pltpu.VMEM((n, chips, share, piece_cols), B16),
            pltpu.VMEM((n, chips, share, piece_cols), B16),
            pltpu.VMEM((n, share, piece_cols), B16),
            pltpu.VMEM((n, pages, share, piece_cols), B16),
            pltpu.VMEM(small.shape, F32),
            pltpu.VMEM(small.shape, F32),
            pltpu.VMEM((pages,) + small.shape, F32),
            pltpu.VMEM(small.shape, F32),
            pltpu.VMEM((chips,) + small.shape, F32),
            pltpu.VMEM(small.shape, F32),
            dma((n, chips)),
            dma((n, chips)),
            dma((n, chips)),
            dma((n, pages)),
            dma((n, pages)),
            dma((n, chips)),
            dma((n, chips)),
            dma((n, pages)),
            dma((n, pages)),
            dma((pages + chips,)),
            dma((pages + chips,)),
            dma((2,)),
            dma((2,)),
        ],
        compiler_params=pltpu.CompilerParams(
            vmem_limit_bytes=VMEM_LIMIT, collective_id=0, has_side_effects=True
        ),
    )(*grads, small, mixed, patch, off, dscore)


def adam_update(master, first, second, grad):
    moment = BETA_ONE * first + (1.0 - BETA_ONE) * grad
    square = BETA_TWO * second + (1.0 - BETA_TWO) * grad * grad
    fix_one = 1.0 - BETA_ONE**STEP
    fix_two = 1.0 - BETA_TWO**STEP
    fresh = master - LEARN_RATE * (
        moment / fix_one / (jnp.sqrt(square / fix_two) + ADAM_EPS) + WEIGHT_DECAY * master
    )
    return (fresh, moment, square)


def shards(
    patches,
    out_grad,
    page_windows,
    region_ids,
    offset_index,
    weights_in,
    weights_out,
    norm_gains,
    biases,
    bias_table,
    master_in,
    master_out,
    first_in,
    second_in,
    first_out,
    second_out,
    first_small,
    second_small,
):
    pages, window, width, model = patches.shape
    half = window // 2
    count = width // window
    least = (count + 1) // 2
    slots = window * window
    table_rows, heads = bias_table.shape
    hidden = weights_out.shape[0]

    labels = region_ids.reshape(pages, window, count, window).transpose(0, 2, 1, 3)
    labels = labels.reshape(pages * count // QUAD, QUAD, slots).astype(F32)
    labels = jnp.pad(labels, ((0, 0), (0, 8 - QUAD), (0, SLOT - slots)), constant_values=-1.0)
    off = offset_index.T
    off_gather = jnp.pad(off, ((0, KEYS - slots), (0, SLOT - slots)))
    off_scatter = jnp.pad(off, ((0, KEYS - slots), (0, SLOT - slots)), constant_values=-1).reshape(1, -1)
    table_lanes = -(-table_rows // 128) * 128
    tab = jnp.pad(bias_table.T * LOG2E, ((0, 0), (0, table_lanes - table_rows)))
    wqkv = weights_in[:, : 3 * model].T
    wproj = weights_in[:, 3 * model : 4 * model]
    bias_qkv = jnp.concatenate(
        [biases[model : 2 * model], jnp.zeros((model,), F32), biases[2 * model : 3 * model]]
    )[:, None]
    zero = jnp.zeros((model,), F32)
    vec_one = jnp.stack(
        [
            norm_gains[0],
            biases[:model],
            biases[3 * model : 4 * model],
            norm_gains[1],
            biases[4 * model : 5 * model],
            zero,
            zero,
            zero,
        ]
    )
    vec_two = jnp.stack([norm_gains[1], biases[5 * model : 6 * model]] + [zero] * 6)

    x, n1, qkv, probs, att, first, n2, below_grad = attn_forward(
        page_windows, patches, out_grad, labels, off_gather, tab, wqkv, bias_qkv, wproj, vec_one, least
    )
    dwup, dwout, dbup, gf, mixed_own, mixed_next, sums_two = mlp(
        page_windows, out_grad, below_grad, n2, first, weights_in, weights_out,
        biases[None, 6 * model :], vec_two, least, master_in.shape[0],
    )
    dwa, dbqkv, dscore, sums_one, patch_own, patch_next = attn_backward(
        page_windows, gf, x, n1, qkv, probs, att, wproj, wqkv, vec_one, patches.shape, heads, least
    )
    dscore = dscore.reshape(heads // 2, KEYS, 2, SLOT).transpose(0, 2, 1, 3).reshape(heads, KEYS * SLOT)
    sums_one = sums_one.reshape(2, 8, model).sum(1)
    sums_two = sums_two.reshape(4, 8, model).sum(1)
    dbqkv = dbqkv.sum(1)
    grad_small = jnp.concatenate(
        [
            sums_one[0],
            sums_two[0],
            sums_one[1],
            dbqkv[:model],
            dbqkv[2 * model :],
            sums_two[3],
            sums_two[1],
            sums_two[2],
            dbup.reshape(-1),
            jnp.zeros((table_lanes * heads,), F32),
        ]
    ).reshape(-1, 128)
    table_at = grad_small.shape[0] - table_lanes * heads // 128
    total_a, total_up, total_out, total_small, above, above_grad = sums(
        [dwa, dwup, dwout],
        grad_small,
        mixed_next,
        patch_next,
        off_scatter,
        dscore,
        table_at,
        lax.axis_size("page"),
        lax.axis_size("rows"),
    )
    mixed = lax.dynamic_update_slice(mixed_own, above, (0, 0, 0, 0))
    patch_grad = lax.dynamic_update_slice(patch_own, above_grad, (0, 0, 0, 0))
    total_table = total_small[table_at:].reshape(table_lanes // 128, heads, 128).transpose(0, 2, 1)
    total_table = total_table.reshape(table_lanes, heads)[:table_rows]
    total_small = jnp.concatenate([total_small[:table_at].reshape(-1), total_table.reshape(-1)])
    part_in = jnp.concatenate([total_a, total_up], axis=1)
    ratio = hidden // model
    total_out = total_out.reshape(-1, ratio, model).transpose(1, 0, 2).reshape(-1, model)
    small_master = jnp.concatenate([norm_gains.reshape(-1), biases, bias_table.reshape(-1)])
    new_in, moment_in, square_in = adam_update(master_in, first_in, second_in, part_in)
    new_out, moment_out, square_out = adam_update(master_out, first_out, second_out, total_out)
    new_small, moment_small, square_small = adam_update(
        small_master, first_small, second_small, total_small
    )
    return (
        mixed,
        patch_grad,
        new_in,
        moment_in,
        square_in,
        new_out,
        moment_out,
        square_out,
        new_small,
        moment_small,
        square_small,
    )


def solution(mesh):
    return jax.shard_map(
        shards,
        mesh=mesh,
        in_specs=(
            P("page", "rows", None, None),
            P("page", "rows", None, None),
            P("page"),
            P("page", "rows", None),
            P(),
            P(),
            P(),
            P(),
            P(),
            P(),
            P("rows", None),
            P("rows", None),
            P("rows", None),
            P("rows", None),
            P("rows", None),
            P("rows", None),
            P(),
            P(),
        ),
        out_specs=(
            P("page", "rows", None, None),
            P("page", "rows", None, None),
            P("rows", None),
            P("rows", None),
            P("rows", None),
            P("rows", None),
            P("rows", None),
            P("rows", None),
            P(),
            P(),
            P(),
        ),
        check_vma=False,
    )
```

```python
import functools
import math

import jax
import jax.numpy as jnp
from jax import lax
from jax.experimental import pallas as pl
from jax.experimental.pallas import tpu as pltpu
from jax.sharding import PartitionSpec as P

STEP = 10
NORM_EPS = 1e-05
BETA_ONE = 0.9
BETA_TWO = 0.999
LEARN_RATE = 0.04
WEIGHT_DECAY = 0.05
ADAM_EPS = 1e-08
MASK_VALUE = -1000000000.0

F32 = jnp.float32
B16 = jnp.bfloat16
LOG2E = math.log2(math.e)
VMEM_LIMIT = 60 * 2**20

QUAD = 4
SLOT = 128
KEYS = 104


def dot(left, right, form="NN"):
    sides = {
        "NN": ((1,), (0,)),
        "NT": ((1,), (1,)),
        "TN": ((0,), (0,)),
    }[form]
    return lax.dot_general(left, right, (sides, ((), ())), preferred_element_type=F32)


def load_band(band, low_ref, high_ref, live, half, width, window, least):
    band[:half, :width] = low_ref[...].astype(F32)
    band[half:, :width] = high_ref[...].astype(F32)
    band[:, width:] = jnp.zeros((window, band.shape[1] - width, band.shape[2]), F32)
    wrap_band(band, live, half, width, window, least)


def wrap_band(band, live, half, width, window, least):
    for count in range(least, width // window + 1):
        at = slice(count * window, count * window + half)
        band[:, at] = jnp.where(live == count, band[:, :half], band[:, at])


def unwrap_band(band, live, half, width, window, least):
    front = band[:, :half]
    for count in range(least, width // window + 1):
        at = slice(count * window, count * window + half)
        front = jnp.where(live == count, band[:, at], front)
    band[:, :half] = front
    edge = least * window // 8 * 8
    columns = lax.broadcasted_iota(jnp.int32, (window, width - edge, band.shape[2]), 1) + edge
    band[:, edge:width] = jnp.where(columns < live * window, band[:, edge:width], 0.0)


def piece(band, row, base, place, window, half):
    start = window * place + half
    aligned = start // 8 * 8
    skip = start - aligned
    size = -(-(skip + window) // 8) * 8
    ref = band.at[row, pl.ds(pl.multiple_of(base, 8) + aligned, size), :]
    return ref, skip


def gather_window(band, base, place, window, half):
    parts = []
    for row in range(window):
        ref, skip = piece(band, row, base, place, window, half)
        parts.append(ref[skip : skip + window, :])
    return parts


def norm_stats(value):
    centre = jnp.mean(value, axis=-1, keepdims=True)
    centered = value - centre
    spread = lax.rsqrt(jnp.mean(centered * centered, axis=-1, keepdims=True) + NORM_EPS)
    return centered * spread, spread


def fold(value):
    rows, cols = value.shape
    return jnp.sum(value.reshape(rows // 8, 8, cols), axis=0)


MESH = pl.DeviceIdType.MESH


def remote(src, dst, send, recv, device):
    return pltpu.make_async_remote_copy(
        src_ref=src, dst_ref=dst, send_sem=send, recv_sem=recv, device_id=device, device_id_type=MESH
    )


def attn_forward_kernel(
    sizes,
    live_ref,
    patches_ref,
    grads_ref,
    low_ref,
    label_ref,
    off_ref,
    tab_ref,
    wqkv_ref,
    bqkv_ref,
    wproj_ref,
    vec_ref,
    x_ref,
    n1_ref,
    qkv_ref,
    probs_ref,
    att_ref,
    first_ref,
    n2_ref,
    grad_halo_ref,
    halo,
    send,
    recv,
    band,
    bias,
    scores,
    bdq,
    bdv,
    stacked,
    xs,
    ns,
):
    window, half, width, model, heads, least, pages, rows_count = sizes
    slots = window * window
    size_head = model // heads
    page, quad = pl.program_id(0), pl.program_id(1)
    live = live_ref[page]
    pairs = heads // 2
    row = lax.axis_index("rows")
    behind, ahead = lax.rem(row + rows_count - 1, rows_count), lax.rem(row + 1, rows_count)

    def halo_copy(p):
        return remote(
            patches_ref.at[p, pl.ds(0, half)], halo.at[p], send.at[p], recv.at[p], {"rows": behind}
        )

    def grad_copy(p):
        return remote(
            grads_ref.at[p, pl.ds(0, half)],
            grad_halo_ref.at[p],
            send.at[pages + p],
            recv.at[pages + p],
            {"rows": behind},
        )

    @pl.when(jnp.logical_and(page == 0, quad == 0))
    def _():
        barrier = pltpu.get_barrier_semaphore()
        for neighbour in (behind, ahead):
            pl.semaphore_signal(barrier, inc=1, device_id={"rows": neighbour}, device_id_type=MESH)
        pl.semaphore_wait(barrier, 2)
        for p in range(pages):
            halo_copy(p).start()
        for p in range(pages):
            grad_copy(p).start()
        off = off_ref[...]
        low, high = jnp.bitwise_and(off, 127), jnp.right_shift(off, 7)
        for h in range(heads):
            got = jnp.zeros((KEYS, SLOT), F32)
            for c in range(tab_ref.shape[1] // 128):
                source = jnp.broadcast_to(tab_ref[h : h + 1, 128 * c : 128 * c + 128], (KEYS, SLOT))
                picked = jnp.take_along_axis(source, low, axis=1, mode="promise_in_bounds")
                got = jnp.where(high == c, picked, got)
            bias[h] = got
        bdq[...] = jnp.zeros_like(bdq)
        bdv[...] = jnp.zeros_like(bdv)
        stacked[...] = jnp.zeros_like(stacked)

    for p in range(pages):

        @pl.when(jnp.logical_and(page == p, quad == 0))
        def _():
            halo_copy(p).wait()
            load_band(band, low_ref.at[0], halo.at[p], live, half, width, window, least)

    @pl.when(jnp.logical_and(page == pages - 1, quad == pl.num_programs(1) - 1))
    def _():
        for p in range(pages):
            grad_copy(p).wait()

    base = quad * (QUAD * window)
    for w in range(QUAD):
        for r, part in enumerate(gather_window(band, base, w, window, half)):
            at = slots * w + window * r
            xs[at : at + window, :] = part
    x = xs[...]
    x_ref[...] = x.astype(B16)
    xhat, _ = norm_stats(x)
    ns[...] = xhat * vec_ref[0:1, :] + vec_ref[1:2, :]
    for w in range(QUAD):
        n1_ref[SLOT * w : SLOT * w + slots, :] = ns[slots * w : slots * w + slots, :].astype(B16)
        n1_ref[SLOT * w + slots : SLOT * w + SLOT, :] = jnp.zeros((SLOT - slots, model), B16)
    scale = size_head**-0.5 * LOG2E
    n1 = n1_ref[...]
    for part in range(3):
        rows = slice(part * model, part * model + model)
        got = dot(wqkv_ref[rows, :], n1, "NT") + bqkv_ref[rows, :]
        if part == 0:
            got = got * scale
        qkv_ref[rows, :] = got.astype(B16)

    sames = []
    for w in range(QUAD):
        spread = jnp.broadcast_to(label_ref[0, w : w + 1, :], (SLOT, SLOT))
        sames.append((spread == spread.T)[:KEYS])
    pair = 2 * size_head

    def score(w, g):
        low = pair * g
        lanes = slice(SLOT * w, SLOT * w + SLOT)
        for j in range(2):
            at = slice(low + size_head * j, low + size_head * (j + 1))
            cols = slice(SLOT * j, SLOT * j + SLOT)
            bdq[w % 2, at, cols] = qkv_ref[at, lanes]
            values = slice(2 * model + low + size_head * j, 2 * model + low + size_head * (j + 1))
            bdv[w % 3, at, cols] = qkv_ref[values, lanes]
        keys = qkv_ref[model + low : model + low + pair, SLOT * w : SLOT * w + KEYS]
        scores[w % 2, g] = dot(keys, bdq[w % 2, low : low + pair, :], "TN")

    def soften(w, g):
        for j in range(2):
            cols = slice(SLOT * j, SLOT * j + SLOT)
            s = jnp.where(sames[w], scores[w % 2, g, :, cols] + bias[2 * g + j], MASK_VALUE)
            s = jnp.exp2(s - jnp.max(s, axis=0, keepdims=True))
            low_probs = (s * (1.0 / jnp.sum(s, axis=0, keepdims=True))).astype(B16)
            probs_ref[w, g, :KEYS, cols] = low_probs
            probs_ref[w, g, KEYS:, cols] = jnp.zeros((SLOT - KEYS, SLOT), B16)
            stacked[w % 2, g, SLOT * j : SLOT * j + KEYS, :] = low_probs

    def attend(w, g):
        low = pair * g
        got = dot(bdv[w % 3, low : low + pair, :], stacked[w % 2, g])
        att_ref[low : low + pair, SLOT * w : SLOT * w + SLOT] = got.astype(B16)

    for step in range(QUAD + 2):
        for g in range(pairs):
            if step < QUAD:
                score(step, g)
            if 1 <= step <= QUAD:
                soften(step - 1, g)
            if step >= 2:
                attend(step - 2, g)

    branch = dot(att_ref[...], wproj_ref[...], "TN")
    for w in range(QUAD):
        rows = slice(slots * w, slots * w + slots)
        first_ref[rows, :] = xs[rows, :] + branch[SLOT * w : SLOT * w + slots, :] + vec_ref[2:3, :]
    xhat, _ = norm_stats(first_ref[...])
    n2_ref[...] = (xhat * vec_ref[3:4, :] + vec_ref[4:5, :]).astype(B16)


def attn_forward(live, patches, out_grad, labels, off, tab, wqkv, bqkv, wproj, vecs, least):
    pages, window, width, model = patches.shape
    half = window // 2
    heads = tab.shape[0]
    quads = width // window // QUAD
    tokens = pages * window * width
    slots = window * window
    padded = pages * quads * QUAD * SLOT
    steps = (pages, quads)
    whole = lambda a: pl.BlockSpec(a.shape, lambda p, j: (0,) * a.ndim, pipeline_mode=pl.Buffered(1))
    at = lambda p, j: p * quads + j
    return pl.pallas_call(
        functools.partial(
            attn_forward_kernel,
            (window, half, width, model, heads, least, pages, lax.axis_size("rows")),
        ),
        grid=steps,
        in_specs=[
            pl.BlockSpec(memory_space=pltpu.SMEM),
            pl.BlockSpec(memory_space=pl.ANY),
            pl.BlockSpec(memory_space=pl.ANY),
            pl.BlockSpec((1, half, width, model), lambda p, j: (p, 1, 0, 0)),
            pl.BlockSpec((1, 8, SLOT), lambda p, j: (at(p, j), 0, 0)),
            whole(off),
            whole(tab),
            whole(wqkv),
            whole(bqkv),
            whole(wproj),
            whole(vecs),
        ],
        out_specs=[
            pl.BlockSpec((QUAD * slots, model), lambda p, j: (at(p, j), 0)),
            pl.BlockSpec((QUAD * SLOT, model), lambda p, j: (at(p, j), 0)),
            pl.BlockSpec((3 * model, QUAD * SLOT), lambda p, j: (0, at(p, j))),
            pl.BlockSpec((QUAD, heads // 2, SLOT, 2 * SLOT), lambda p, j: (at(p, j), 0, 0, 0)),
            pl.BlockSpec((model, QUAD * SLOT), lambda p, j: (0, at(p, j))),
            pl.BlockSpec((QUAD * slots, model), lambda p, j: (at(p, j), 0)),
            pl.BlockSpec((QUAD * slots, model), lambda p, j: (at(p, j), 0)),
            pl.BlockSpec(memory_space=pl.ANY),
        ],
        out_shape=[
            jax.ShapeDtypeStruct((tokens, model), B16),
            jax.ShapeDtypeStruct((padded, model), B16),
            jax.ShapeDtypeStruct((3 * model, padded), B16),
            jax.ShapeDtypeStruct((pages * quads * QUAD, heads // 2, SLOT, 2 * SLOT), B16),
            jax.ShapeDtypeStruct((model, padded), B16),
            jax.ShapeDtypeStruct((tokens, model), F32),
            jax.ShapeDtypeStruct((tokens, model), B16),
            jax.ShapeDtypeStruct((pages, half, width, model), B16),
        ],
        scratch_shapes=[
            pltpu.VMEM((pages, half, width, model), B16),
            pltpu.SemaphoreType.DMA((2 * pages,)),
            pltpu.SemaphoreType.DMA((2 * pages,)),
            pltpu.VMEM((window, width + 8, model), F32),
            pltpu.VMEM((heads, KEYS, SLOT), F32),
            pltpu.VMEM((2, heads // 2, KEYS, 2 * SLOT), F32),
            pltpu.VMEM((2, model, 2 * SLOT), B16),
            pltpu.VMEM((3, model, 2 * SLOT), B16),
            pltpu.VMEM((2, heads // 2, 2 * SLOT, SLOT), B16),
            pltpu.VMEM((QUAD * slots, model), F32),
            pltpu.VMEM((QUAD * slots, model), F32),
        ],
        compiler_params=pltpu.CompilerParams(
            vmem_limit_bytes=VMEM_LIMIT, collective_id=1, has_side_effects=True
        ),
    )(live, patches, out_grad, patches, labels, off, tab, wqkv, bqkv, wproj, vecs)


MLP_COLS = 512
MLP_ROWS = 480


def mlp_kernel(
    sizes,
    live_ref,
    low_ref,
    high_ref,
    n2_ref,
    first_ref,
    wup_ref,
    wout_ref,
    bup_ref,
    vec_ref,
    dwup_ref,
    dwout_ref,
    dbup_ref,
    gf_ref,
    own_ref,
    next_ref,
    sums_ref,
    band,
    cot,
    res,
    dn2,
    act_all,
    pre_all,
):
    window, half, width, model, least, share = sizes
    pages = low_ref.shape[0]
    slots = window * window
    count = width // window
    quads = count // QUAD
    chunk = pl.program_id(0)
    tokens = n2_ref.shape[0]
    cols = wup_ref.shape[1]

    @pl.when(chunk == 0)
    def _():
        for page in range(pages):
            live = live_ref[page]
            load_band(band, low_ref.at[page], high_ref.at[page], live, half, width, window, least)

            def body(j, carry):
                for w in range(QUAD):
                    alive = jnp.where(j * QUAD + w < live, 1.0, 0.0)
                    for r, part in enumerate(gather_window(band, j * QUAD * window, w, window, half)):
                        at = slots * w + window * r
                        gf_ref[at : at + window, :] = part * alive
                rows = pl.ds(pl.multiple_of((page * quads + j) * QUAD * slots, 16), QUAD * slots)
                cot[rows, :] = gf_ref[: QUAD * slots, :].astype(B16)
                return carry

            lax.fori_loop(0, quads, body, 0)

    def body(i, total):
        rows = pl.ds(pl.multiple_of(i * MLP_ROWS, 16), MLP_ROWS)
        grad = cot[rows, :]
        pre = dot(n2_ref[rows, :], wup_ref[...]) + bup_ref[...]
        grad_act = dot(grad, wout_ref[...], "NT")
        share = 0.5 * (1.0 + lax.erf(pre * 0.5**0.5))
        act = (pre * share).astype(B16)
        slope = share + pre * (jnp.exp2((-0.5 * LOG2E) * pre * pre) * (2.0 * math.pi) ** -0.5)
        grad_pre = (grad_act * slope).astype(B16)
        act_all[rows, :] = act
        pre_all[rows, :] = grad_pre
        up = dot(act, wout_ref[...])
        down = dot(grad_pre, wup_ref[...], "NT")

        @pl.when(chunk == 0)
        def _():
            res[rows, :] = up
            dn2[rows, :] = down

        @pl.when(chunk > 0)
        def _():
            res[rows, :] += up
            dn2[rows, :] += down

        return total + fold(grad_pre.astype(F32))

    total = lax.fori_loop(0, tokens // MLP_ROWS, body, jnp.zeros((8, cols), F32))
    dbup_ref[...] = jnp.sum(total, axis=0, keepdims=True)
    grad_out = dot(act_all[...], cot[...], "TN").astype(B16)
    for s in range(dwout_ref.shape[0] // share):
        for a in range(dwout_ref.shape[1] // model):
            at = (s * (dwout_ref.shape[1] // model) + a) * share
            dwout_ref[share * s : share * s + share, model * a : model * a + model] = grad_out[at : at + share, :]
    dwup_ref[...] = dot(n2_ref[...], pre_all[...], "TN").astype(B16)

    @pl.when(chunk == pl.num_programs(0) - 1)
    def _():
        sums_ref[...] = jnp.zeros_like(sums_ref)
        for page in range(pages):
            live = live_ref[page]

            def body(j, carry):
                at = pl.multiple_of((page * quads + j) * QUAD * slots, 16)
                rows = pl.ds(at, QUAD * slots)
                first = first_ref[rows, :]
                res[rows, :] += first + vec_ref[1:2, :]
                xhat, spread = norm_stats(first)
                grad = dn2[rows, :]
                given = cot[rows, :].astype(F32)
                scaled = grad * vec_ref[0:1, :]
                mean_one = jnp.mean(scaled, axis=-1, keepdims=True)
                mean_two = jnp.mean(scaled * xhat, axis=-1, keepdims=True)
                whole = given + spread * (scaled - mean_one - xhat * mean_two)
                gf_ref[rows, :] = whole
                sums_ref[0:8, :] += fold(grad * xhat)
                sums_ref[8:16, :] += fold(grad)
                sums_ref[16:24, :] += fold(given)
                sums_ref[24:32, :] += fold(whole)
                for w in range(QUAD):
                    for r in range(window):
                        ref, skip = piece(band, r, j * QUAD * window, w, window, half)
                        ref[skip : skip + window, :] = res[
                            pl.ds(at + slots * w // 8 * 8, slots + 4), :
                        ][slots * w % 8 + window * r : slots * w % 8 + window * r + window, :]
                return carry

            lax.fori_loop(0, quads, body, 0)
            unwrap_band(band, live, half, width, window, least)
            own_ref[page] = band[:half, :width].astype(B16)
            next_ref[page] = band[half:, :width].astype(B16)


def mlp(live, out_grad, halo, n2, first, weights_in, weights_out, bup, vecs, least, share):
    pages, window, width, model = out_grad.shape
    half = window // 2
    tokens = n2.shape[0]
    hidden = weights_out.shape[0]
    skip = (weights_in.shape[1] - hidden) // MLP_COLS
    once = pl.Buffered(1)
    whole = lambda a: pl.BlockSpec(a.shape, lambda c: (0,) * a.ndim, pipeline_mode=once)
    band_block = (pages, half, width, model)
    return pl.pallas_call(
        functools.partial(mlp_kernel, (window, half, width, model, least, share)),
        grid=(hidden // MLP_COLS,),
        in_specs=[
            pl.BlockSpec(memory_space=pltpu.SMEM),
            pl.BlockSpec(band_block, lambda c: (0, 1, 0, 0), pipeline_mode=once),
            pl.BlockSpec(band_block, lambda c: (0, 0, 0, 0), pipeline_mode=once),
            whole(n2),
            whole(first),
            pl.BlockSpec((model, MLP_COLS), lambda c: (0, c + skip)),
            pl.BlockSpec((MLP_COLS, model), lambda c: (c, 0)),
            pl.BlockSpec((1, MLP_COLS), lambda c: (0, c)),
            whole(vecs),
        ],
        out_specs=[
            pl.BlockSpec((model, MLP_COLS), lambda c: (0, c)),
            pl.BlockSpec((model * MLP_COLS // hidden, hidden), lambda c: (c, 0)),
            pl.BlockSpec((1, MLP_COLS), lambda c: (0, c)),
            pl.BlockSpec((tokens, model), lambda c: (0, 0), pipeline_mode=once),
            pl.BlockSpec(band_block, lambda c: (0, 1, 0, 0), pipeline_mode=once),
            pl.BlockSpec(band_block, lambda c: (0, 0, 0, 0), pipeline_mode=once),
            pl.BlockSpec((32, model), lambda c: (0, 0)),
        ],
        out_shape=[
            jax.ShapeDtypeStruct((model, hidden), B16),
            jax.ShapeDtypeStruct((model, hidden), B16),
            jax.ShapeDtypeStruct((1, hidden), F32),
            jax.ShapeDtypeStruct((tokens, model), F32),
            jax.ShapeDtypeStruct(out_grad.shape, B16),
            jax.ShapeDtypeStruct(band_block, B16),
            jax.ShapeDtypeStruct((32, model), F32),
        ],
        scratch_shapes=[
            pltpu.VMEM((window, width + 8, model), F32),
            pltpu.VMEM((tokens, model), B16),
            pltpu.VMEM((tokens, model), F32),
            pltpu.VMEM((tokens, model), F32),
            pltpu.VMEM((tokens, MLP_COLS), B16),
            pltpu.VMEM((tokens, MLP_COLS), B16),
        ],
        compiler_params=pltpu.CompilerParams(vmem_limit_bytes=VMEM_LIMIT),
    )(live, out_grad, halo, n2, first, weights_in, weights_out, bup, vecs)


def table_sum(off_ref, grad_ref, out_ref, at, heads, chunks):
    rows = 128 * chunks
    keys = grad_ref.shape[1]
    names = lax.broadcasted_iota(jnp.int32, (rows, SLOT), 0)
    total = jnp.zeros((3 * heads, rows), F32)
    grad = jnp.swapaxes(grad_ref[...], 0, 1)
    for k in range(0, keys, 8):
        hot = jnp.concatenate(
            [jnp.where(names == off_ref[i : i + 1, :], 1.0, 0.0).astype(B16) for i in range(k, k + 8)], axis=1
        )
        value = jnp.concatenate([grad[i] for i in range(k, k + 8)], axis=1)
        high = value.astype(B16)
        rest = value - high.astype(F32)
        middle = rest.astype(B16)
        low = (rest - middle.astype(F32)).astype(B16)
        total += dot(jnp.concatenate([high, middle, low], axis=0), hot, "NT")
    total = total[:heads] + total[heads : 2 * heads] + total[2 * heads :]
    for c in range(chunks):
        out_ref[at + heads * c : at + heads * c + heads, :] = total[:, 128 * c : 128 * c + 128]


class Exchange:
    def __init__(self, pages, chips, share, bufs, sems):
        self.pages, self.chips, self.share = pages, chips, share
        self.rec1, self.s1, self.rec2, self.s2, self.rec3, self.s3, self.rec4 = bufs
        self.send1, self.recv1, self.send2, self.recv2, self.send3, self.recv3, self.send4, self.recv4 = sems
        self.page, row = lax.axis_index("page"), lax.axis_index("rows")
        self.chip, self.core = row // 2, row % 2
        self.other = 2 * self.chip + 1 - self.core
        self.cols = self.s3.shape[-1]

    def page_peer(self, d):
        return lax.rem(self.page + d, self.pages)

    def chip_peer(self, d):
        return lax.rem(self.chip + d, self.chips)

    def along(self, d):
        return {"rows": 2 * self.chip_peer(d) + self.core}

    def rows_of(self, ref, z, c):
        return ref.at[pl.ds(pl.multiple_of((2 * z + c) * self.share, 16), self.share), :]

    def one(self, m, grad):
        return [
            remote(
                self.rows_of(grad, z, 1 - self.core),
                self.rec1.at[m, z],
                self.send1.at[m, z],
                self.recv1.at[m, z],
                {"rows": self.other},
            )
            for z in range(self.chips)
        ]

    def two(self, m):
        return [
            remote(
                self.s1.at[m, self.page_peer(d)],
                self.rec2.at[m, self.page],
                self.send2.at[m, d],
                self.recv2.at[m, d],
                {"page": self.page_peer(d)},
            )
            for d in range(1, self.pages)
        ]

    def three(self, m):
        return [
            remote(
                self.s2.at[m, self.chip_peer(d)],
                self.rec3.at[m, self.chip],
                self.send3.at[m, d],
                self.recv3.at[m, d],
                self.along(d),
            )
            for d in range(1, self.chips)
        ]

    def four(self, m):
        return [
            remote(
                self.s3.at[m],
                self.rec4.at[m, self.page],
                self.send4.at[m, d],
                self.recv4.at[m, d],
                {"page": self.page_peer(d)},
            )
            for d in range(1, self.pages)
        ]

    def start_one(self, m, grad):
        start(self.one(m, grad))

    def start_two(self, m, grad, own):
        wait(self.one(m, grad))
        for q in range(self.pages):
            at = slice(self.cols * q, self.cols * q + self.cols)
            for z in range(self.chips):
                self.s1[m, q, z] = (own(z)[:, at].astype(F32) + self.rec1[m, z, :, at].astype(F32)).astype(B16)
        start(self.two(m))
        self.rec2[m, self.page] = self.s1[m, self.page]

    def start_three(self, m):
        wait(self.two(m))
        total = self.rec2[m, 0].astype(F32)
        for q in range(1, self.pages):
            total = total + self.rec2[m, q].astype(F32)
        self.s2[m] = total.astype(B16)
        start(self.three(m))
        self.rec3[m, self.chip] = self.s2[m, self.chip]

    def start_four(self, m):
        wait(self.three(m))
        total = self.rec3[m, 0].astype(F32)
        for z in range(1, self.chips):
            total = total + self.rec3[m, z].astype(F32)
        self.s3[m] = total.astype(B16)
        start(self.four(m))
        self.rec4[m, self.page] = self.s3[m]

    def finish(self, m, out_ref):
        wait(self.four(m))
        for q in range(self.pages):
            out_ref[:, self.cols * q : self.cols * q + self.cols] = self.rec4[m, q]


class SmallExchange:
    def __init__(self, big, bufs, sems):
        self.big = big
        self.mine, self.one_in, self.two_out, self.two_in, self.three_out, self.three_in = bufs
        self.send, self.recv = sems

    def one(self):
        return [remote(self.mine, self.one_in, self.send.at[0], self.recv.at[0], {"rows": self.big.other})]

    def two(self):
        big = self.big
        return [
            remote(
                self.two_out,
                self.two_in.at[big.page],
                self.send.at[d],
                self.recv.at[d],
                {"page": big.page_peer(d)},
            )
            for d in range(1, big.pages)
        ]

    def three(self):
        big = self.big
        return [
            remote(
                self.three_out,
                self.three_in.at[big.chip],
                self.send.at[big.pages + d],
                self.recv.at[big.pages + d],
                big.along(d),
            )
            for d in range(1, big.chips)
        ]

    def start_one(self):
        start(self.one())

    def start_two(self):
        wait(self.one())
        total = self.mine[...] + self.one_in[...]
        self.two_out[...] = total
        start(self.two())
        self.two_in[self.big.page] = total

    def start_three(self):
        wait(self.two())
        total = self.two_in[0]
        for q in range(1, self.big.pages):
            total = total + self.two_in[q]
        self.three_out[...] = total
        start(self.three())
        self.three_in[self.big.chip] = total

    def finish(self, out_ref, at):
        wait(self.three())
        total = self.three_in[0]
        for z in range(1, self.big.chips):
            total = total + self.three_in[z]
        out_ref[at : at + total.shape[0], :] = total


def start(copies):
    for copy in copies:
        copy.start()


def wait(copies):
    for copy in copies:
        copy.wait()


LATE = 8


def attn_backward_kernel(
    sizes,
    live_ref,
    up_ref,
    out_ref,
    mixed_ref,
    gf_ref,
    x_ref,
    n1_ref,
    qkv_ref,
    probs_ref,
    att_ref,
    wproj_ref,
    wqkv_ref,
    vec_ref,
    off_ref,
    early_ref,
    suma_ref,
    sumu_ref,
    sumo_ref,
    small_ref,
    own_ref,
    mixed_halo_ref,
    patch_halo_ref,
    band,
    gbp,
    datt,
    dprobs,
    bdq,
    bdk,
    bdo,
    stacked,
    beside,
    dqkv,
    dwq,
    dwp,
    compact,
    dscore,
    dbqkv,
    sums,
    dwa,
    edge,
    own1,
    *rest,
):
    window, half, width, model, heads, least, pages, devices, share = sizes
    slots = window * window
    size_head = model // heads
    sweep, page, quad = pl.program_id(0), pl.program_id(1), pl.program_id(2)
    quads = pl.num_programs(2)
    step = page * quads + quad
    live = live_ref[page]
    pairs = heads // 2
    pair = 2 * size_head
    big = Exchange(devices[0], devices[1] // 2, share, rest[:7], rest[7:15])
    early = SmallExchange(big, (rest[15],) + rest[16:21], rest[21:23])
    late = SmallExchange(big, (rest[23],) + rest[24:29], rest[29:31])
    local, halo_send, halo_recv = rest[31:]
    row = lax.axis_index("rows")
    behind, ahead = lax.rem(row + devices[1] - 1, devices[1]), lax.rem(row + 1, devices[1])
    matrices = (dwa, up_ref, out_ref)

    def fetch(m):
        return [
            pltpu.make_async_copy(
                big.rows_of(matrices[m], z, big.core), own1.at[m - 1, z], local.at[m - 1, z]
            )
            for z in range(big.chips)
        ]

    def mixed_copy():
        return remote(mixed_ref, mixed_halo_ref, halo_send.at[0], halo_recv.at[0], {"rows": ahead})

    def patch_copy(p):
        return remote(
            edge.at[p], patch_halo_ref.at[p], halo_send.at[1 + p], halo_recv.at[1 + p], {"rows": ahead}
        )

    def moment(at_sweep, at_step):
        return jnp.logical_and(sweep == at_sweep, step == at_step)

    @pl.when(moment(0, 0))
    def _():
        barrier = pltpu.get_barrier_semaphore()
        peers = [{"rows": big.other}, {"rows": behind}, {"rows": ahead}]
        peers += [{"page": big.page_peer(d)} for d in range(1, big.pages)]
        peers += [big.along(d) for d in range(1, big.chips)]
        for peer in peers:
            pl.semaphore_signal(barrier, inc=1, device_id=peer, device_id_type=MESH)
        pl.semaphore_wait(barrier, len(peers))
        for m in (1, 2):
            big.start_one(m, matrices[m])
            start(fetch(m))
        mixed_copy().start()
        for ref in (bdq, bdk, bdo, stacked, beside, gbp, dwq, dwp, dbqkv, dscore, sums):
            ref[...] = jnp.zeros_like(ref)

    last = pages * (width // window // QUAD) - 1
    for m, (at_two, at_three, at_four) in ((1, (1, 3, 4)), (2, (1, 4, 5))):

        @pl.when(moment(0, at_two))
        def _():
            wait(fetch(m))
            big.start_two(m, matrices[m], lambda z: own1.at[m - 1, z])

        @pl.when(moment(0, at_three))
        def _():
            big.start_three(m)

        @pl.when(moment(0, at_four))
        def _():
            big.start_four(m)

    @pl.when(sweep == 0)
    def _():
        for w in range(QUAD):
            gbp[SLOT * w : SLOT * w + slots, :] = gf_ref[slots * w : slots * w + slots, :].astype(B16)
        datt[...] = dot(wproj_ref[...], gbp[...], "NT").astype(B16)
        dwp[...] += dot(att_ref[...], gbp[...])
        ratio = size_head**-0.5
        target = dqkv.at[step]

        def score(w, g):
            low = pair * g
            lanes = slice(SLOT * w, SLOT * w + SLOT)
            for j in range(2):
                at = slice(low + size_head * j, low + size_head * (j + 1))
                keys = slice(model + low + size_head * j, model + low + size_head * (j + 1))
                cols = slice(SLOT * j, SLOT * j + SLOT)
                bdo[w % 3, at, cols] = datt[at, lanes]
                bdq[w % 3, at, cols] = qkv_ref[at, lanes]
                bdk[w % 3, at, cols] = qkv_ref[keys, lanes]
            values = qkv_ref[2 * model + low : 2 * model + low + pair, SLOT * w : SLOT * w + KEYS]
            dprobs[w % 2, g] = dot(values, bdo[w % 3, low : low + pair, :], "TN")

        def soften(w, g):
            probs = probs_ref[w, g, :KEYS, :].astype(F32)
            term = probs * dprobs[w % 2, g]
            grad = term - probs * jnp.sum(term, axis=0, keepdims=True)
            low_grad = grad.astype(B16)
            beside[w % 2, g, :KEYS, :] = low_grad
            for j in range(2):
                cols = slice(SLOT * j, SLOT * j + SLOT)
                dscore[2 * g + j] += grad[:, cols]
                stacked[w % 2, g, SLOT * j : SLOT * j + KEYS, :] = low_grad[:, cols]

        def attend(w, g):
            low = pair * g
            lanes = slice(SLOT * w, SLOT * w + SLOT)
            rows = slice(low, low + pair)
            got = dot(bdk[w % 3, rows, :], stacked[w % 2, g]) * ratio
            target[low : low + pair, lanes] = got.astype(B16)
            got = dot(bdq[w % 3, rows, :], beside[w % 2, g], "NT") * (1.0 / LOG2E)
            target[model + low : model + low + pair, lanes] = got.astype(B16)
            got = dot(bdo[w % 3, rows, :], probs_ref[w, g], "NT")
            target[2 * model + low : 2 * model + low + pair, lanes] = got.astype(B16)

        for stage in range(QUAD + 2):
            for g in range(pairs):
                if stage < QUAD:
                    score(stage, g)
                if 1 <= stage <= QUAD:
                    soften(stage - 1, g)
                if stage >= 2:
                    attend(stage - 2, g)

        n1 = n1_ref[...]
        for part in range(3):
            rows = slice(part * model, part * model + model)
            grad = dqkv[step, rows, :]
            dwq[rows, :] += dot(grad, n1)
            wide = grad.astype(F32)
            both = wide[:, :SLOT]
            for w in range(1, QUAD):
                both = both + wide[:, SLOT * w : SLOT * w + SLOT]
            dbqkv[rows, :] += both

    @pl.when(moment(1, 0))
    def _():
        dwa[:, 3 * model :] = dwp[...].astype(B16)
        for part in range(3):
            rows = slice(part * model, part * model + model)
            dwa[:, rows] = dwq[rows, :].T.astype(B16)
        big.start_one(0, dwa)
        early.mine[...] = early_ref[...]
        lines = model // 128
        for k, part in enumerate((0, 2)):
            total = jnp.sum(dbqkv[part * model : part * model + model, :].T, axis=0, keepdims=True)
            for i in range(lines):
                early.mine[lines * k + i : lines * k + i + 1, :] = total[:, 128 * i : 128 * i + 128]

    @pl.when(moment(1, 1))
    def _():
        big.start_two(0, dwa, lambda z: big.rows_of(dwa, z, big.core))

    @pl.when(moment(1, 2))
    def _():
        chunks = -(-(2 * window - 1) ** 2 // 128)
        table_sum(off_ref, dscore, early.mine, early.mine.shape[0] - heads * chunks, heads, chunks)
        early.start_one()

    @pl.when(moment(1, 3))
    def _():
        early.start_two()

    @pl.when(moment(1, 4))
    def _():
        early.start_three()

    @pl.when(sweep == 1)
    def _():
        dn1 = dot(dqkv[step], wqkv_ref[...], "TN")
        for w in range(QUAD):
            compact[slots * w : slots * w + slots, :] = dn1[SLOT * w : SLOT * w + slots, :]
        grad = compact[...]
        xhat, spread = norm_stats(x_ref[...].astype(F32))
        scaled = grad * vec_ref[0:1, :]
        mean_one = jnp.mean(scaled, axis=-1, keepdims=True)
        mean_two = jnp.mean(scaled * xhat, axis=-1, keepdims=True)
        sums[0:8, :] += fold(grad * xhat)
        sums[8:16, :] += fold(grad)
        compact[...] = gf_ref[...] + spread * (scaled - mean_one - xhat * mean_two)
        for w in range(QUAD):
            for r in range(window):
                ref, skip = piece(band, r, quad * QUAD * window, w, window, half)
                at = slots * w + window * r
                ref[skip : skip + window, :] = compact[at : at + window, :]

    for p in range(pages):

        @pl.when(jnp.logical_and(sweep == 1, jnp.logical_and(page == p, quad == quads - 1)))
        def _():
            unwrap_band(band, live, half, width, window, least)
            edge[p] = band[half:, :width].astype(B16)
            patch_copy(p).start()
            own_ref[0] = band[:half, :width].astype(B16)

    @pl.when(moment(1, last))
    def _():
        big.start_three(0)
        lines = model // 128
        for k in range(2):
            total = jnp.sum(sums[8 * k : 8 * k + 8, :], axis=0, keepdims=True)
            for i in range(lines):
                late.mine[lines * k + i : lines * k + i + 1, :] = total[:, 128 * i : 128 * i + 128]
        late.start_one()
        for m, ref in ((1, sumu_ref), (2, sumo_ref)):
            big.finish(m, ref)
        late.start_two()
        early.finish(small_ref, LATE)
        big.start_four(0)
        late.start_three()
        mixed_copy().wait()
        late.finish(small_ref, 0)
        big.finish(0, suma_ref)
        for p in range(pages):
            patch_copy(p).wait()


def attn_backward(
    live, dwup, dwout, mixed_next, gf, x, n1, qkv, probs, att, wproj, wqkv, vecs, off, early, shape, heads, least, share
):
    pages, window, width, model = shape
    half = window // 2
    quads = width // window // QUAD
    slots = window * window
    pairs = heads // 2
    devices = (lax.axis_size("page"), lax.axis_size("rows"))
    chips = devices[1] // 2
    hidden = dwup.shape[1]
    cols = hidden // devices[0]
    once = pl.Buffered(1)
    whole = lambda a: pl.BlockSpec(a.shape, lambda s, p, j: (0,) * a.ndim, pipeline_mode=once)
    held = lambda dims: pl.BlockSpec(dims, lambda s, p, j: (0,) * len(dims), pipeline_mode=once)
    anywhere = pl.BlockSpec(memory_space=pl.ANY)
    at = lambda p, j: p * quads + j
    last = pages * quads - 1
    first = lambda s, p, j: jnp.where(s == 0, at(p, j), last)
    second = lambda s, p, j: jnp.where(s == 0, 0, at(p, j))
    own_at = lambda s, p, j: (jnp.where(s == 0, 0, p), 1, 0, 0)
    dma = pltpu.SemaphoreType.DMA
    vmem = pltpu.VMEM
    n = 3
    lines = early.shape[0]

    def small_scratch(rows):
        return [
            vmem((rows, 128), F32),
            vmem((rows, 128), F32),
            vmem((rows, 128), F32),
            vmem((devices[0], rows, 128), F32),
            vmem((rows, 128), F32),
            vmem((chips, rows, 128), F32),
            dma((devices[0] + chips,)),
            dma((devices[0] + chips,)),
        ]

    return pl.pallas_call(
        functools.partial(
            attn_backward_kernel, (window, half, width, model, heads, least, pages, devices, share)
        ),
        grid=(2, pages, quads),
        in_specs=[
            pl.BlockSpec(memory_space=pltpu.SMEM),
            anywhere,
            anywhere,
            anywhere,
            pl.BlockSpec((QUAD * slots, model), lambda s, p, j: (at(p, j), 0)),
            pl.BlockSpec((QUAD * slots, model), lambda s, p, j: (second(s, p, j), 0)),
            pl.BlockSpec((QUAD * SLOT, model), lambda s, p, j: (first(s, p, j), 0)),
            pl.BlockSpec((3 * model, QUAD * SLOT), lambda s, p, j: (0, first(s, p, j))),
            pl.BlockSpec((QUAD, pairs, SLOT, 2 * SLOT), lambda s, p, j: (first(s, p, j), 0, 0, 0)),
            pl.BlockSpec((model, QUAD * SLOT), lambda s, p, j: (0, first(s, p, j))),
            whole(wproj),
            whole(wqkv),
            whole(vecs),
            whole(off),
            whole(early),
        ],
        out_specs=[
            held((share, hidden)),
            held((share, hidden)),
            held((share, hidden)),
            held((LATE + lines, 128)),
            pl.BlockSpec((1, half, width, model), own_at),
            anywhere,
            anywhere,
        ],
        out_shape=[
            jax.ShapeDtypeStruct((share, hidden), B16),
            jax.ShapeDtypeStruct((share, hidden), B16),
            jax.ShapeDtypeStruct((share, hidden), B16),
            jax.ShapeDtypeStruct((LATE + lines, 128), F32),
            jax.ShapeDtypeStruct(shape, B16),
            jax.ShapeDtypeStruct((pages, half, width, model), B16),
            jax.ShapeDtypeStruct((pages, half, width, model), B16),
        ],
        scratch_shapes=[
            vmem((window, width + 8, model), F32),
            vmem((QUAD * SLOT, model), B16),
            vmem((model, QUAD * SLOT), B16),
            vmem((2, pairs, KEYS, 2 * SLOT), F32),
            vmem((3, model, 2 * SLOT), B16),
            vmem((3, model, 2 * SLOT), B16),
            vmem((3, model, 2 * SLOT), B16),
            vmem((2, pairs, 2 * SLOT, SLOT), B16),
            vmem((2, pairs, SLOT, 2 * SLOT), B16),
            vmem((pages * quads, 3 * model, QUAD * SLOT), B16),
            vmem((3 * model, model), F32),
            vmem((model, model), F32),
            vmem((QUAD * slots, model), F32),
            vmem((heads, KEYS, SLOT), F32),
            vmem((3 * model, SLOT), F32),
            vmem((16, model), F32),
            vmem((model, hidden), B16),
            vmem((pages, half, width, model), B16),
            vmem((2, chips, share, hidden), B16),
            vmem((n, chips, share, hidden), B16),
            vmem((n, devices[0], chips, share, cols), B16),
            vmem((n, devices[0], chips, share, cols), B16),
            vmem((n, chips, share, cols), B16),
            vmem((n, chips, share, cols), B16),
            vmem((n, share, cols), B16),
            vmem((n, devices[0], share, cols), B16),
            dma((n, chips)),
            dma((n, chips)),
            dma((n, devices[0])),
            dma((n, devices[0])),
            dma((n, chips)),
            dma((n, chips)),
            dma((n, devices[0])),
            dma((n, devices[0])),
        ]
        + small_scratch(lines)
        + small_scratch(LATE)
        + [dma((2, chips)), dma((1 + pages,)), dma((1 + pages,))],
        compiler_params=pltpu.CompilerParams(
            vmem_limit_bytes=63 * 2**20, collective_id=0, has_side_effects=True
        ),
    )(live, dwup, dwout, mixed_next, gf, x, n1, qkv, probs, att, wproj, wqkv, vecs, off, early)


def adam_update(master, first, second, grad):
    moment = BETA_ONE * first + (1.0 - BETA_ONE) * grad
    square = BETA_TWO * second + (1.0 - BETA_TWO) * grad * grad
    fix_one = 1.0 - BETA_ONE**STEP
    fix_two = 1.0 - BETA_TWO**STEP
    fresh = master - LEARN_RATE * (
        moment / fix_one / (jnp.sqrt(square / fix_two) + ADAM_EPS) + WEIGHT_DECAY * master
    )
    return (fresh, moment, square)


def shards(
    patches,
    out_grad,
    page_windows,
    region_ids,
    offset_index,
    weights_in,
    weights_out,
    norm_gains,
    biases,
    bias_table,
    master_in,
    master_out,
    first_in,
    second_in,
    first_out,
    second_out,
    first_small,
    second_small,
):
    pages, window, width, model = patches.shape
    half = window // 2
    count = width // window
    least = (count + 1) // 2
    slots = window * window
    table_rows, heads = bias_table.shape
    hidden = weights_out.shape[0]

    labels = region_ids.reshape(pages, window, count, window).transpose(0, 2, 1, 3)
    labels = labels.reshape(pages * count // QUAD, QUAD, slots).astype(F32)
    labels = jnp.pad(labels, ((0, 0), (0, 8 - QUAD), (0, SLOT - slots)), constant_values=-1.0)
    off = offset_index.T
    off_gather = jnp.pad(off, ((0, KEYS - slots), (0, SLOT - slots)))
    off_scatter = jnp.pad(off, ((0, KEYS - slots), (0, SLOT - slots)), constant_values=-1)
    table_lanes = -(-table_rows // 128) * 128
    tab = jnp.pad(bias_table.T * LOG2E, ((0, 0), (0, table_lanes - table_rows)))
    wqkv = weights_in[:, : 3 * model].T
    wproj = weights_in[:, 3 * model : 4 * model]
    bias_qkv = jnp.concatenate(
        [biases[model : 2 * model], jnp.zeros((model,), F32), biases[2 * model : 3 * model]]
    )[:, None]
    zero = jnp.zeros((model,), F32)
    vec_one = jnp.stack(
        [
            norm_gains[0],
            biases[:model],
            biases[3 * model : 4 * model],
            norm_gains[1],
            biases[4 * model : 5 * model],
            zero,
            zero,
            zero,
        ]
    )
    vec_two = jnp.stack([norm_gains[1], biases[5 * model : 6 * model]] + [zero] * 6)

    x, n1, qkv, probs, att, first, n2, below_grad = attn_forward(
        page_windows, patches, out_grad, labels, off_gather, tab, wqkv, bias_qkv, wproj, vec_one, least
    )
    dwup, dwout, dbup, gf, mixed_own, mixed_next, sums_two = mlp(
        page_windows, out_grad, below_grad, n2, first, weights_in, weights_out,
        biases[None, 6 * model :], vec_two, least, master_in.shape[0],
    )
    sums_two = sums_two.reshape(4, 8, model).sum(1)
    lines = model // 128
    early = jnp.concatenate(
        [
            jnp.zeros((2 * lines, 128), F32),
            sums_two[jnp.array([0, 3, 1, 2])].reshape(4 * lines, 128),
            dbup.reshape(-1, 128),
            jnp.zeros((table_lanes * heads // 128, 128), F32),
        ]
    )
    total_a, total_up, total_out, small, patch_own, above, above_grad = attn_backward(
        page_windows, dwup, dwout, mixed_next, gf, x, n1, qkv, probs, att, wproj, wqkv, vec_one,
        off_scatter, early, patches.shape, heads, least, master_in.shape[0],
    )
    mixed = lax.dynamic_update_slice(mixed_own, above, (0, 0, 0, 0))
    patch_grad = lax.dynamic_update_slice(patch_own, above_grad, (0, 0, 0, 0))
    small_at = [0, 4, 1, 2, 3, 5, 6, 7]
    table_at = small.shape[0] - table_lanes * heads // 128
    total_table = small[table_at:].reshape(table_lanes // 128, heads, 128).transpose(0, 2, 1)
    total_table = total_table.reshape(table_lanes, heads)[:table_rows]
    head = [small[lines * k : lines * k + lines] for k in small_at] + [small[8 * lines : table_at]]
    total_small = jnp.concatenate([jnp.concatenate(head).reshape(-1), total_table.reshape(-1)])
    part_in = jnp.concatenate([total_a, total_up], axis=1).astype(F32)
    ratio = hidden // model
    total_out = total_out.reshape(-1, ratio, model).transpose(1, 0, 2).reshape(-1, model).astype(F32)
    small_master = jnp.concatenate([norm_gains.reshape(-1), biases, bias_table.reshape(-1)])
    new_in, moment_in, square_in = adam_update(master_in, first_in, second_in, part_in)
    new_out, moment_out, square_out = adam_update(master_out, first_out, second_out, total_out)
    new_small, moment_small, square_small = adam_update(
        small_master, first_small, second_small, total_small
    )
    return (
        mixed,
        patch_grad,
        new_in,
        moment_in,
        square_in,
        new_out,
        moment_out,
        square_out,
        new_small,
        moment_small,
        square_small,
    )


def solution(mesh):
    return jax.shard_map(
        shards,
        mesh=mesh,
        in_specs=(
            P("page", "rows", None, None),
            P("page", "rows", None, None),
            P("page"),
            P("page", "rows", None),
            P(),
            P(),
            P(),
            P(),
            P(),
            P(),
            P("rows", None),
            P("rows", None),
            P("rows", None),
            P("rows", None),
            P("rows", None),
            P("rows", None),
            P(),
            P(),
        ),
        out_specs=(
            P("page", "rows", None, None),
            P("page", "rows", None, None),
            P("rows", None),
            P("rows", None),
            P("rows", None),
            P("rows", None),
            P("rows", None),
            P("rows", None),
            P(),
            P(),
            P(),
        ),
        check_vma=False,
    )
```

```python
import functools
import math

import jax
import jax.numpy as jnp
from jax import lax
from jax.experimental import pallas as pl
from jax.experimental.pallas import tpu as pltpu
from jax.sharding import PartitionSpec as P

STEP = 10
NORM_EPS = 1e-05
BETA_ONE = 0.9
BETA_TWO = 0.999
LEARN_RATE = 0.04
WEIGHT_DECAY = 0.05
ADAM_EPS = 1e-08
MASK_VALUE = -1000000000.0

F32 = jnp.float32
B16 = jnp.bfloat16
LOG2E = math.log2(math.e)
VMEM_LIMIT = 60 * 2**20

QUAD = 4
SLOT = 128
KEYS = 104


def dot(left, right, form="NN"):
    sides = {
        "NN": ((1,), (0,)),
        "NT": ((1,), (1,)),
        "TN": ((0,), (0,)),
    }[form]
    return lax.dot_general(left, right, (sides, ((), ())), preferred_element_type=F32)


def load_band(band, low_ref, high_ref, live, half, width, window, least):
    band[:half, :width] = low_ref[...].astype(F32)
    band[half:, :width] = high_ref[...].astype(F32)
    band[:, width:] = jnp.zeros((window, band.shape[1] - width, band.shape[2]), F32)
    wrap_band(band, live, half, width, window, least)


def wrap_band(band, live, half, width, window, least):
    for count in range(least, width // window + 1):
        at = slice(count * window, count * window + half)
        band[:, at] = jnp.where(live == count, band[:, :half], band[:, at])


def unwrap_band(band, live, half, width, window, least):
    front = band[:, :half]
    for count in range(least, width // window + 1):
        at = slice(count * window, count * window + half)
        front = jnp.where(live == count, band[:, at], front)
    band[:, :half] = front
    edge = least * window // 8 * 8
    shape = (band.shape[0], width - edge, band.shape[2])
    columns = lax.broadcasted_iota(jnp.int32, shape, 1) + edge
    band[:, edge:width] = jnp.where(columns < live * window, band[:, edge:width], 0.0)


def piece(band, row, base, place, window, half):
    start = window * place + half
    aligned = start // 8 * 8
    skip = start - aligned
    size = -(-(skip + window) // 8) * 8
    ref = band.at[row, pl.ds(pl.multiple_of(base, 8) + aligned, size), :]
    return ref, skip


def gather_window(band, base, place, window, half):
    parts = []
    for row in range(window):
        ref, skip = piece(band, row, base, place, window, half)
        parts.append(ref[skip : skip + window, :])
    return parts


def norm_stats(value):
    centre = jnp.mean(value, axis=-1, keepdims=True)
    centered = value - centre
    spread = lax.rsqrt(jnp.mean(centered * centered, axis=-1, keepdims=True) + NORM_EPS)
    return centered * spread, spread


def fold(value):
    rows, cols = value.shape
    return jnp.sum(value.reshape(rows // 8, 8, cols), axis=0)


MESH = pl.DeviceIdType.MESH


def remote(src, dst, send, recv, device):
    return pltpu.make_async_remote_copy(
        src_ref=src, dst_ref=dst, send_sem=send, recv_sem=recv, device_id=device, device_id_type=MESH
    )


def lay_lines(lines_ref, at, row):
    for i in range(row.shape[1] // 128):
        lines_ref[at + i : at + i + 1, :] = row[:, 128 * i : 128 * i + 128]


def lay_row(ref, row, lines_ref, at, count):
    for i in range(count):
        ref[row : row + 1, 128 * i : 128 * i + 128] = lines_ref[at + i : at + i + 1, :]


def attn_forward_kernel(
    sizes,
    live_ref,
    patches_ref,
    grads_ref,
    low_ref,
    label_ref,
    off_ref,
    tab_ref,
    wqkv_ref,
    wproj_ref,
    gains_ref,
    biases_ref,
    x_ref,
    n1_ref,
    qkv_ref,
    probs_ref,
    att_ref,
    first_ref,
    n2_ref,
    grad_halo_ref,
    turned_ref,
    places_ref,
    halo,
    send,
    recv,
    band,
    bias,
    scores,
    bdq,
    bdv,
    stacked,
    xs,
    ns,
    vecs,
    column,
    square,
    tall,
    flat,
):
    window, half, width, model, heads, least, pages, rows_count = sizes
    slots = window * window
    size_head = model // heads
    page, quad = pl.program_id(0), pl.program_id(1)
    live = live_ref[page]
    pairs = heads // 2
    part_rows = model // 2
    lines = model // 128
    row = lax.axis_index("rows")
    behind, ahead = lax.rem(row + rows_count - 1, rows_count), lax.rem(row + 1, rows_count)

    def halo_copy(p):
        return remote(
            patches_ref.at[p, pl.ds(0, half)], halo.at[p], send.at[p], recv.at[p], {"rows": behind}
        )

    def grad_copy(p):
        return remote(
            grads_ref.at[p, pl.ds(0, half)],
            grad_halo_ref.at[p],
            send.at[pages + p],
            recv.at[pages + p],
            {"rows": behind},
        )

    @pl.when(jnp.logical_and(page == 0, quad == 0))
    def _():
        barrier = pltpu.get_barrier_semaphore()
        for neighbour in (behind, ahead):
            pl.semaphore_signal(barrier, inc=1, device_id={"rows": neighbour}, device_id_type=MESH)
        pl.semaphore_wait(barrier, 2)
        for p in range(pages):
            halo_copy(p).start()
        for p in range(pages):
            grad_copy(p).start()
        vecs[...] = jnp.zeros_like(vecs)
        vecs[0:1, :] = gains_ref[0:1, :]
        lay_row(vecs, 1, biases_ref, 0, lines)
        lay_row(vecs, 2, biases_ref, 3 * lines, lines)
        vecs[3:4, :] = gains_ref[1:2, :]
        lay_row(vecs, 4, biases_ref, 4 * lines, lines)
        column[...] = jnp.zeros_like(column)
        for h in range(2):
            for part in range(3):
                rows = slice(part * part_rows, part * part_rows + part_rows)
                cols = slice(part * model + h * part_rows, part * model + (h + 1) * part_rows)
                turned_ref[h, rows, :] = wqkv_ref[:, cols].T
                if part != 1:
                    for i in range(part_rows // 128):
                        line = lines * (1 + part // 2) + h * (part_rows // 128) + i
                        spread = jnp.broadcast_to(biases_ref[line : line + 1, :], (128, 128))
                        at = part * part_rows + 128 * i
                        column[h, at : at + 128, :] = spread.T
        square[...] = jnp.full_like(square, -1)
        square[:slots, :slots] = off_ref[...]
        places = square[...].T[:KEYS]
        places_ref[...] = places
        off = jnp.maximum(places, 0)
        tall[...] = jnp.zeros_like(tall)
        tall[: tab_ref.shape[0], :heads] = tab_ref[...] * LOG2E
        for c in range(tall.shape[0] // 128):
            flat[:, 128 * c : 128 * c + 128] = tall[128 * c : 128 * c + 128, :].T[:heads]
        low, high = jnp.bitwise_and(off, 127), jnp.right_shift(off, 7)
        for h in range(heads):
            got = jnp.zeros((KEYS, SLOT), F32)
            for c in range(tall.shape[0] // 128):
                source = jnp.broadcast_to(flat[h : h + 1, 128 * c : 128 * c + 128], (KEYS, SLOT))
                picked = jnp.take_along_axis(source, low, axis=1, mode="promise_in_bounds")
                got = jnp.where(high == c, picked, got)
            bias[h] = got
        bdq[...] = jnp.zeros_like(bdq)
        bdv[...] = jnp.zeros_like(bdv)
        stacked[...] = jnp.zeros_like(stacked)

    for p in range(pages):

        @pl.when(jnp.logical_and(page == p, quad == 0))
        def _():
            halo_copy(p).wait()
            load_band(band, low_ref.at[0], halo.at[p], live, half, width, window, least)

    @pl.when(jnp.logical_and(page == pages - 1, quad == pl.num_programs(1) - 1))
    def _():
        for p in range(pages):
            grad_copy(p).wait()

    base = quad * (QUAD * window)
    for w in range(QUAD):
        for r, part in enumerate(gather_window(band, base, w, window, half)):
            at = slots * w + window * r
            xs[at : at + window, :] = part
    x = xs[...]
    x_ref[...] = x.astype(B16)
    xhat, _ = norm_stats(x)
    ns[...] = xhat * vecs[0:1, :] + vecs[1:2, :]
    for w in range(QUAD):
        n1_ref[SLOT * w : SLOT * w + slots, :] = ns[slots * w : slots * w + slots, :].astype(B16)
        n1_ref[SLOT * w + slots : SLOT * w + SLOT, :] = jnp.zeros((SLOT - slots, model), B16)
    scale = size_head**-0.5 * LOG2E
    n1 = n1_ref[...]
    for h in range(2):
        got = dot(turned_ref[h], n1, "NT") + column[h, :, 0:1]
        at = slice(h * part_rows, h * part_rows + part_rows)
        qkv_ref[0, at, :] = (got[:part_rows] * scale).astype(B16)
        qkv_ref[1, at, :] = got[part_rows : 2 * part_rows].astype(B16)
        qkv_ref[2, at, :] = got[2 * part_rows :].astype(B16)

    sames = []
    for w in range(QUAD):
        spread = jnp.broadcast_to(label_ref[0, w : w + 1, :], (SLOT, SLOT))
        sames.append((spread == spread.T)[:KEYS])
    pair = 2 * size_head

    def score(w, g):
        low = pair * g
        lanes = slice(SLOT * w, SLOT * w + SLOT)
        for j in range(2):
            at = slice(low + size_head * j, low + size_head * (j + 1))
            cols = slice(SLOT * j, SLOT * j + SLOT)
            bdq[w % 2, at, cols] = qkv_ref[0, at, lanes]
            bdv[w % 3, at, cols] = qkv_ref[2, at, lanes]
        keys = qkv_ref[1, low : low + pair, SLOT * w : SLOT * w + KEYS]
        scores[w % 2, g] = dot(keys, bdq[w % 2, low : low + pair, :], "TN")

    def soften(w, g):
        for j in range(2):
            cols = slice(SLOT * j, SLOT * j + SLOT)
            s = jnp.where(sames[w], scores[w % 2, g, :, cols] + bias[2 * g + j], MASK_VALUE)
            s = jnp.exp2(s - jnp.max(s, axis=0, keepdims=True))
            low_probs = (s * (1.0 / jnp.sum(s, axis=0, keepdims=True))).astype(B16)
            probs_ref[w, g, :KEYS, cols] = low_probs
            probs_ref[w, g, KEYS:, cols] = jnp.zeros((SLOT - KEYS, SLOT), B16)
            stacked[w % 2, g, SLOT * j : SLOT * j + KEYS, :] = low_probs

    def attend(w, g):
        low = pair * g
        got = dot(bdv[w % 3, low : low + pair, :], stacked[w % 2, g])
        att_ref[low : low + pair, SLOT * w : SLOT * w + SLOT] = got.astype(B16)

    for step in range(QUAD + 2):
        for g in range(pairs):
            if step < QUAD:
                score(step, g)
            if 1 <= step <= QUAD:
                soften(step - 1, g)
            if step >= 2:
                attend(step - 2, g)

    branch = dot(att_ref[...], wproj_ref[...], "TN")
    for w in range(QUAD):
        rows = slice(slots * w, slots * w + slots)
        first_ref[rows, :] = xs[rows, :] + branch[SLOT * w : SLOT * w + slots, :] + vecs[2:3, :]
    xhat, _ = norm_stats(first_ref[...])
    n2_ref[...] = (xhat * vecs[3:4, :] + vecs[4:5, :]).astype(B16)


def attn_forward(live, patches, out_grad, labels, off, tab, weights_in, gains, biases, least):
    pages, window, width, model = patches.shape
    half = window // 2
    table_rows, heads = tab.shape
    table_lanes = -(-table_rows // 128) * 128
    quads = width // window // QUAD
    tokens = pages * window * width
    slots = window * window
    padded = pages * quads * QUAD * SLOT
    steps = (pages, quads)
    whole = lambda a: pl.BlockSpec(a.shape, lambda p, j: (0,) * a.ndim, pipeline_mode=pl.Buffered(1))
    at = lambda p, j: p * quads + j
    return pl.pallas_call(
        functools.partial(
            attn_forward_kernel,
            (window, half, width, model, heads, least, pages, lax.axis_size("rows")),
        ),
        grid=steps,
        in_specs=[
            pl.BlockSpec(memory_space=pltpu.SMEM),
            pl.BlockSpec(memory_space=pl.ANY),
            pl.BlockSpec(memory_space=pl.ANY),
            pl.BlockSpec((1, half, width, model), lambda p, j: (p, 1, 0, 0)),
            pl.BlockSpec((1, 8, SLOT), lambda p, j: (at(p, j), 0, 0)),
            whole(off),
            whole(tab),
            pl.BlockSpec((model, 3 * model), lambda p, j: (0, 0), pipeline_mode=pl.Buffered(1)),
            pl.BlockSpec((model, model), lambda p, j: (0, 3), pipeline_mode=pl.Buffered(1)),
            whole(gains),
            whole(biases),
        ],
        out_specs=[
            pl.BlockSpec((QUAD * slots, model), lambda p, j: (at(p, j), 0)),
            pl.BlockSpec((QUAD * SLOT, model), lambda p, j: (at(p, j), 0)),
            pl.BlockSpec((3, model, QUAD * SLOT), lambda p, j: (0, 0, at(p, j))),
            pl.BlockSpec((QUAD, heads // 2, SLOT, 2 * SLOT), lambda p, j: (at(p, j), 0, 0, 0)),
            pl.BlockSpec((model, QUAD * SLOT), lambda p, j: (0, at(p, j))),
            pl.BlockSpec((QUAD * slots, model), lambda p, j: (at(p, j), 0)),
            pl.BlockSpec((QUAD * slots, model), lambda p, j: (at(p, j), 0)),
            pl.BlockSpec(memory_space=pl.ANY),
            pl.BlockSpec((2, 3 * model // 2, model), lambda p, j: (0, 0, 0), pipeline_mode=pl.Buffered(1)),
            pl.BlockSpec((KEYS, SLOT), lambda p, j: (0, 0)),
        ],
        out_shape=[
            jax.ShapeDtypeStruct((tokens, model), B16),
            jax.ShapeDtypeStruct((padded, model), B16),
            jax.ShapeDtypeStruct((3, model, padded), B16),
            jax.ShapeDtypeStruct((pages * quads * QUAD, heads // 2, SLOT, 2 * SLOT), B16),
            jax.ShapeDtypeStruct((model, padded), B16),
            jax.ShapeDtypeStruct((tokens, model), F32),
            jax.ShapeDtypeStruct((tokens, model), B16),
            jax.ShapeDtypeStruct((pages, half, width, model), B16),
            jax.ShapeDtypeStruct((2, 3 * model // 2, model), B16),
            jax.ShapeDtypeStruct((KEYS, SLOT), jnp.int32),
        ],
        scratch_shapes=[
            pltpu.VMEM((pages, half, width, model), B16),
            pltpu.SemaphoreType.DMA((2 * pages,)),
            pltpu.SemaphoreType.DMA((2 * pages,)),
            pltpu.VMEM((window, width + 8, model), F32),
            pltpu.VMEM((heads, KEYS, SLOT), F32),
            pltpu.VMEM((2, heads // 2, KEYS, 2 * SLOT), F32),
            pltpu.VMEM((2, model, 2 * SLOT), B16),
            pltpu.VMEM((3, model, 2 * SLOT), B16),
            pltpu.VMEM((2, heads // 2, 2 * SLOT, SLOT), B16),
            pltpu.VMEM((QUAD * slots, model), F32),
            pltpu.VMEM((QUAD * slots, model), F32),
            pltpu.VMEM((8, model), F32),
            pltpu.VMEM((2, 3 * model // 2, 128), F32),
            pltpu.VMEM((SLOT, SLOT), jnp.int32),
            pltpu.VMEM((table_lanes, 128), F32),
            pltpu.VMEM((heads, table_lanes), F32),
        ],
        compiler_params=pltpu.CompilerParams(
            vmem_limit_bytes=VMEM_LIMIT, collective_id=1, has_side_effects=True
        ),
    )(live, patches, out_grad, patches, labels, off, tab, weights_in, weights_in, gains, biases)


MLP_COLS = 512
MLP_CHUNKS = 4
MLP_ROWS = 480
EARLY_UP = 6


def mlp_kernel(
    sizes,
    live_ref,
    low_ref,
    high_ref,
    n2_ref,
    first_ref,
    wup_ref,
    wout_ref,
    gains_ref,
    biases_ref,
    dwup_ref,
    dwout_ref,
    gf_ref,
    own_ref,
    next_ref,
    early_ref,
    bup,
    vecs,
    sums,
    band,
    cot,
    res,
    dn2,
    act_all,
    pre_all,
):
    window, half, width, model, least, share = sizes
    pages = low_ref.shape[0]
    slots = window * window
    count = width // window
    quads = count // QUAD
    chunk = pl.program_id(0)
    tokens = n2_ref.shape[0]
    cols = wup_ref.shape[1]
    lines = model // 128

    for c in range(MLP_CHUNKS):

        @pl.when(chunk == c)
        def _():
            lay_row(bup, 0, biases_ref, 6 * lines + c * (cols // 128), cols // 128)

    @pl.when(chunk == 0)
    def _():
        early_ref[...] = jnp.zeros_like(early_ref)
        vecs[0:1, :] = gains_ref[1:2, :]
        lay_row(vecs, 1, biases_ref, 5 * lines, lines)
        for page in range(pages):
            live = live_ref[page]
            load_band(band, low_ref.at[page], high_ref.at[page], live, half, width, window, least)

            def body(j, carry):
                for w in range(QUAD):
                    alive = jnp.where(j * QUAD + w < live, 1.0, 0.0)
                    for r, part in enumerate(gather_window(band, j * QUAD * window, w, window, half)):
                        at = slots * w + window * r
                        gf_ref[at : at + window, :] = part * alive
                rows = pl.ds(pl.multiple_of((page * quads + j) * QUAD * slots, 16), QUAD * slots)
                cot[rows, :] = gf_ref[: QUAD * slots, :].astype(B16)
                return carry

            lax.fori_loop(0, quads, body, 0)

    def body(i, total):
        rows = pl.ds(pl.multiple_of(i * MLP_ROWS, 16), MLP_ROWS)
        grad = cot[rows, :]
        pre = dot(n2_ref[rows, :], wup_ref[...]) + bup[0:1, :]
        grad_act = dot(grad, wout_ref[...], "NT")
        share = 0.5 * (1.0 + lax.erf(pre * 0.5**0.5))
        act = (pre * share).astype(B16)
        slope = share + pre * (jnp.exp2((-0.5 * LOG2E) * pre * pre) * (2.0 * math.pi) ** -0.5)
        grad_pre = (grad_act * slope).astype(B16)
        act_all[rows, :] = act
        pre_all[rows, :] = grad_pre
        up = dot(act, wout_ref[...])
        down = dot(grad_pre, wup_ref[...], "NT")

        @pl.when(chunk == 0)
        def _():
            res[rows, :] = up
            dn2[rows, :] = down

        @pl.when(chunk > 0)
        def _():
            res[rows, :] += up
            dn2[rows, :] += down

        return total + fold(grad_pre.astype(F32))

    total = lax.fori_loop(0, tokens // MLP_ROWS, body, jnp.zeros((8, cols), F32))
    total = jnp.sum(total, axis=0, keepdims=True)
    for c in range(MLP_CHUNKS):

        @pl.when(chunk == c)
        def _():
            lay_lines(early_ref, EARLY_UP * lines + c * (cols // 128), total)

    grad_out = dot(act_all[...], cot[...], "TN").astype(B16)
    for s in range(dwout_ref.shape[0] // share):
        for a in range(dwout_ref.shape[1] // model):
            at = (s * (dwout_ref.shape[1] // model) + a) * share
            dwout_ref[share * s : share * s + share, model * a : model * a + model] = grad_out[at : at + share, :]
    dwup_ref[...] = dot(n2_ref[...], pre_all[...], "TN").astype(B16)

    @pl.when(chunk == pl.num_programs(0) - 1)
    def _():
        sums[...] = jnp.zeros_like(sums)
        for page in range(pages):
            live = live_ref[page]

            def body(j, carry):
                at = pl.multiple_of((page * quads + j) * QUAD * slots, 16)
                rows = pl.ds(at, QUAD * slots)
                first = first_ref[rows, :]
                res[rows, :] += first + vecs[1:2, :]
                xhat, spread = norm_stats(first)
                grad = dn2[rows, :]
                given = cot[rows, :].astype(F32)
                scaled = grad * vecs[0:1, :]
                mean_one = jnp.mean(scaled, axis=-1, keepdims=True)
                mean_two = jnp.mean(scaled * xhat, axis=-1, keepdims=True)
                whole = given + spread * (scaled - mean_one - xhat * mean_two)
                gf_ref[rows, :] = whole
                sums[0:8, :] += fold(grad * xhat)
                sums[8:16, :] += fold(whole)
                sums[16:24, :] += fold(grad)
                sums[24:32, :] += fold(given)
                for w in range(QUAD):
                    for r in range(window):
                        ref, skip = piece(band, r, j * QUAD * window, w, window, half)
                        ref[skip : skip + window, :] = res[
                            pl.ds(at + slots * w // 8 * 8, slots + 4), :
                        ][slots * w % 8 + window * r : slots * w % 8 + window * r + window, :]
                return carry

            lax.fori_loop(0, quads, body, 0)
            unwrap_band(band, live, half, width, window, least)
            own_ref[page] = band[:half, :width].astype(B16)
            next_ref[page] = band[half:, :width].astype(B16)
        for k in range(4):
            lay_lines(early_ref, (2 + k) * lines, jnp.sum(sums[8 * k : 8 * k + 8, :], axis=0, keepdims=True))


def mlp(live, out_grad, halo, n2, first, weights_in, weights_out, gains, biases, least, share, lines):
    pages, window, width, model = out_grad.shape
    half = window // 2
    tokens = n2.shape[0]
    hidden = weights_out.shape[0]
    skip = (weights_in.shape[1] - hidden) // MLP_COLS
    once = pl.Buffered(1)
    whole = lambda a: pl.BlockSpec(a.shape, lambda c: (0,) * a.ndim, pipeline_mode=once)
    band_block = (pages, half, width, model)
    return pl.pallas_call(
        functools.partial(mlp_kernel, (window, half, width, model, least, share)),
        grid=(hidden // MLP_COLS,),
        in_specs=[
            pl.BlockSpec(memory_space=pltpu.SMEM),
            pl.BlockSpec(band_block, lambda c: (0, 1, 0, 0), pipeline_mode=once),
            pl.BlockSpec(band_block, lambda c: (0, 0, 0, 0), pipeline_mode=once),
            whole(n2),
            whole(first),
            pl.BlockSpec((model, MLP_COLS), lambda c: (0, c + skip)),
            pl.BlockSpec((MLP_COLS, model), lambda c: (c, 0)),
            whole(gains),
            whole(biases),
        ],
        out_specs=[
            pl.BlockSpec((model, MLP_COLS), lambda c: (0, c)),
            pl.BlockSpec((model * MLP_COLS // hidden, hidden), lambda c: (c, 0)),
            pl.BlockSpec((tokens, model), lambda c: (0, 0), pipeline_mode=once),
            pl.BlockSpec(band_block, lambda c: (0, 1, 0, 0), pipeline_mode=once),
            pl.BlockSpec(band_block, lambda c: (0, 0, 0, 0), pipeline_mode=once),
            pl.BlockSpec((lines, 128), lambda c: (0, 0)),
        ],
        out_shape=[
            jax.ShapeDtypeStruct((model, hidden), B16),
            jax.ShapeDtypeStruct((model, hidden), B16),
            jax.ShapeDtypeStruct((tokens, model), F32),
            jax.ShapeDtypeStruct(out_grad.shape, B16),
            jax.ShapeDtypeStruct(band_block, B16),
            jax.ShapeDtypeStruct((lines, 128), F32),
        ],
        scratch_shapes=[
            pltpu.VMEM((8, MLP_COLS), F32),
            pltpu.VMEM((8, model), F32),
            pltpu.VMEM((32, model), F32),
            pltpu.VMEM((window, width + 8, model), F32),
            pltpu.VMEM((tokens, model), B16),
            pltpu.VMEM((tokens, model), F32),
            pltpu.VMEM((tokens, model), F32),
            pltpu.VMEM((tokens, MLP_COLS), B16),
            pltpu.VMEM((tokens, MLP_COLS), B16),
        ],
        compiler_params=pltpu.CompilerParams(vmem_limit_bytes=VMEM_LIMIT),
    )(live, out_grad, halo, n2, first, weights_in, weights_out, gains, biases)


def table_sum(off_ref, grad_ref, out_ref, at, heads, chunks):
    rows = 128 * chunks
    keys = grad_ref.shape[1]
    names = lax.broadcasted_iota(jnp.int32, (rows, SLOT), 0)
    total = jnp.zeros((3 * heads, rows), F32)
    grad = jnp.swapaxes(grad_ref[...], 0, 1)
    for k in range(0, keys, 8):
        hot = jnp.concatenate(
            [jnp.where(names == off_ref[i : i + 1, :], 1.0, 0.0).astype(B16) for i in range(k, k + 8)], axis=1
        )
        value = jnp.concatenate([grad[i] for i in range(k, k + 8)], axis=1)
        high = value.astype(B16)
        rest = value - high.astype(F32)
        middle = rest.astype(B16)
        low = (rest - middle.astype(F32)).astype(B16)
        total += dot(jnp.concatenate([high, middle, low], axis=0), hot, "NT")
    total = total[:heads] + total[heads : 2 * heads] + total[2 * heads :]
    for c in range(chunks):
        out_ref[at + heads * c : at + heads * c + heads, :] = total[:, 128 * c : 128 * c + 128]


class Exchange:
    def __init__(self, pages, chips, share, bufs, sems):
        self.pages, self.chips, self.share = pages, chips, share
        self.rec1, self.s1, self.rec2, self.s2, self.rec3, self.s3, self.rec4 = bufs
        self.send1, self.recv1, self.send2, self.recv2, self.send3, self.recv3, self.send4, self.recv4 = sems
        self.page, row = lax.axis_index("page"), lax.axis_index("rows")
        self.chip, self.core = row // 2, row % 2
        self.other = 2 * self.chip + 1 - self.core
        self.cols = self.s3.shape[-1]

    def page_peer(self, d):
        return lax.rem(self.page + d, self.pages)

    def chip_peer(self, d):
        return lax.rem(self.chip + d, self.chips)

    def along(self, d):
        return {"rows": 2 * self.chip_peer(d) + self.core}

    def rows_of(self, ref, z, c):
        return ref.at[pl.ds(pl.multiple_of((2 * z + c) * self.share, 16), self.share), :]

    def one(self, m, grad):
        return [
            remote(
                self.rows_of(grad, z, 1 - self.core),
                self.rec1.at[m, z],
                self.send1.at[m, z],
                self.recv1.at[m, z],
                {"rows": self.other},
            )
            for z in range(self.chips)
        ]

    def two(self, m):
        return [
            remote(
                self.s1.at[m, self.page_peer(d)],
                self.rec2.at[m, self.page],
                self.send2.at[m, d],
                self.recv2.at[m, d],
                {"page": self.page_peer(d)},
            )
            for d in range(1, self.pages)
        ]

    def three(self, m):
        return [
            remote(
                self.s2.at[m, self.chip_peer(d)],
                self.rec3.at[m, self.chip],
                self.send3.at[m, d],
                self.recv3.at[m, d],
                self.along(d),
            )
            for d in range(1, self.chips)
        ]

    def four(self, m):
        return [
            remote(
                self.s3.at[m],
                self.rec4.at[m, self.page],
                self.send4.at[m, d],
                self.recv4.at[m, d],
                {"page": self.page_peer(d)},
            )
            for d in range(1, self.pages)
        ]

    def start_one(self, m, grad):
        start(self.one(m, grad))

    def start_two(self, m, grad, own):
        wait(self.one(m, grad))
        for q in range(self.pages):
            at = slice(self.cols * q, self.cols * q + self.cols)
            for z in range(self.chips):
                self.s1[m, q, z] = (own(z)[:, at].astype(F32) + self.rec1[m, z, :, at].astype(F32)).astype(B16)
        start(self.two(m))
        self.rec2[m, self.page] = self.s1[m, self.page]

    def start_three(self, m):
        wait(self.two(m))
        total = self.rec2[m, 0].astype(F32)
        for q in range(1, self.pages):
            total = total + self.rec2[m, q].astype(F32)
        self.s2[m] = total.astype(B16)
        start(self.three(m))
        self.rec3[m, self.chip] = self.s2[m, self.chip]

    def start_four(self, m):
        wait(self.three(m))
        total = self.rec3[m, 0].astype(F32)
        for z in range(1, self.chips):
            total = total + self.rec3[m, z].astype(F32)
        self.s3[m] = total.astype(B16)
        start(self.four(m))
        self.rec4[m, self.page] = self.s3[m]

    def finish(self, m, out_ref):
        wait(self.four(m))
        for q in range(self.pages):
            out_ref[:, self.cols * q : self.cols * q + self.cols] = self.rec4[m, q]


class SmallExchange:
    def __init__(self, big, bufs, sems):
        self.big = big
        self.mine, self.one_in, self.two_out, self.two_in, self.three_out, self.three_in = bufs
        self.send, self.recv = sems

    def one(self):
        return [remote(self.mine, self.one_in, self.send.at[0], self.recv.at[0], {"rows": self.big.other})]

    def two(self):
        big = self.big
        return [
            remote(
                self.two_out,
                self.two_in.at[big.page],
                self.send.at[d],
                self.recv.at[d],
                {"page": big.page_peer(d)},
            )
            for d in range(1, big.pages)
        ]

    def three(self):
        big = self.big
        return [
            remote(
                self.three_out,
                self.three_in.at[big.chip],
                self.send.at[big.pages + d],
                self.recv.at[big.pages + d],
                big.along(d),
            )
            for d in range(1, big.chips)
        ]

    def start_one(self):
        start(self.one())

    def start_two(self):
        wait(self.one())
        total = self.mine[...] + self.one_in[...]
        self.two_out[...] = total
        start(self.two())
        self.two_in[self.big.page] = total

    def start_three(self):
        wait(self.two())
        total = self.two_in[0]
        for q in range(1, self.big.pages):
            total = total + self.two_in[q]
        self.three_out[...] = total
        start(self.three())
        self.three_in[self.big.chip] = total

    def finish(self, out_ref, at):
        wait(self.three())
        total = self.three_in[0]
        for z in range(1, self.big.chips):
            total = total + self.three_in[z]
        out_ref[at : at + total.shape[0], :] = total


def start(copies):
    for copy in copies:
        copy.start()


def wait(copies):
    for copy in copies:
        copy.wait()


LATE = 8


def attn_backward_kernel(
    sizes,
    live_ref,
    up_ref,
    out_ref,
    mixed_ref,
    gf_ref,
    x_ref,
    n1_ref,
    qkv_ref,
    probs_ref,
    att_ref,
    wproj_ref,
    turned_ref,
    gains_ref,
    places_ref,
    early_ref,
    sum_ref,
    small_ref,
    own_ref,
    mixed_halo_ref,
    patch_halo_ref,
    band,
    gbp,
    datt,
    dprobs,
    bdq,
    bdk,
    bdo,
    stacked,
    beside,
    dqkv,
    dwq,
    dwp,
    compact,
    dscore,
    dscores,
    dbqkv,
    sums,
    dwa,
    edge,
    own1,
    *rest,
):
    window, half, width, model, heads, least, pages, devices, share = sizes
    slots = window * window
    size_head = model // heads
    sweep, page, quad = pl.program_id(0), pl.program_id(1), pl.program_id(2)
    quads = width // window // QUAD
    step = page * quads + quad
    live = live_ref[page]
    pairs = heads // 4
    pair = 2 * size_head
    part_rows = model // 2
    lines = model // 128
    cols = 2 * model
    big = Exchange(devices[0], devices[1] // 2, share, rest[:7], rest[7:15])
    early = SmallExchange(big, (rest[15],) + rest[16:21], rest[21:23])
    late = SmallExchange(big, (rest[23],) + rest[24:29], rest[29:31])
    local, halo_send, halo_recv = rest[31:]
    row = lax.axis_index("rows")
    behind, ahead = lax.rem(row + devices[1] - 1, devices[1]), lax.rem(row + 1, devices[1])
    matrices = [dwa.at[0], dwa.at[1]]
    for ref in (up_ref, out_ref):
        for h in range(ref.shape[1] // cols):
            matrices.append(ref.at[:, pl.ds(h * cols, cols)])
    outer = range(2, len(matrices))

    def fetch(m):
        return [
            pltpu.make_async_copy(
                big.rows_of(matrices[m], z, big.core), own1.at[m - 2, z], local.at[m - 2, z]
            )
            for z in range(big.chips)
        ]

    def mixed_copy():
        return remote(mixed_ref, mixed_halo_ref, halo_send.at[0], halo_recv.at[0], {"rows": ahead})

    def edge_at(j):
        return 0 if j == 0 else width + 8 if j == quads else (j * QUAD * window + half) // 16 * 16

    def patch_copy(p, j):
        cut = pl.ds(edge_at(j), edge_at(j + 1) - edge_at(j))
        k = 1 + p * quads + j
        return remote(
            edge.at[p, :, cut, :], patch_halo_ref.at[p, :, cut, :], halo_send.at[k], halo_recv.at[k], {"rows": ahead}
        )

    def moment(at_sweep, at_step):
        return jnp.logical_and(sweep == at_sweep, step == at_step)

    @pl.when(moment(0, 0))
    def _():
        barrier = pltpu.get_barrier_semaphore()
        peers = [{"rows": big.other}, {"rows": behind}, {"rows": ahead}]
        peers += [{"page": big.page_peer(d)} for d in range(1, big.pages)]
        peers += [big.along(d) for d in range(1, big.chips)]
        for peer in peers:
            pl.semaphore_signal(barrier, inc=1, device_id=peer, device_id_type=MESH)
        pl.semaphore_wait(barrier, len(peers))
        for m in outer:
            big.start_one(m, matrices[m])
            start(fetch(m))
        mixed_copy().start()
        early.mine[...] = early_ref[...]
        for ref in (bdq, bdk, bdo, stacked, beside, gbp, dwq, dwp, dbqkv, dscore, sums):
            ref[...] = jnp.zeros_like(ref)

    def flush(h):
        for part in range(3):
            rows = slice(part * part_rows, part * part_rows + part_rows)
            dwa[h, :, rows] = dwq[rows, :].T.astype(B16)
        dwa[h, :, 3 * part_rows :] = dwp[:, h * part_rows : (h + 1) * part_rows].astype(B16)
        big.start_one(h, matrices[h])
        for k, part in enumerate((0, 2)):
            total = jnp.sum(dbqkv[part * part_rows : (part + 1) * part_rows, :].T, axis=0, keepdims=True)
            lay_lines(early.mine, lines * k + h * (lines // 2), total)
        dscores[h * heads // 2 : (h + 1) * heads // 2] = dscore[...]
        if h == 0:
            for ref in (dwq, dbqkv, dscore):
                ref[...] = jnp.zeros_like(ref)

    def two(m):
        if m >= 2:
            wait(fetch(m))
            big.start_two(m, matrices[m], lambda z: own1.at[m - 2, z])
        else:
            big.start_two(m, matrices[m], lambda z: big.rows_of(matrices[m], z, big.core))

    def table():
        chunks = -(-((2 * window - 1) ** 2) // 128)
        table_sum(places_ref, dscores, early.mine, early.mine.shape[0] - heads * chunks, heads, chunks)
        early.start_one()

    plan = {
        (0, 2): [(two, 2), (two, 3)],
        (0, 4): [(two, 4), (two, 5)],
        (1, 0): [(flush, 0)],
        (1, 1): [(big.start_three, 2), (big.start_three, 3), (two, 0)],
        (1, 4): [(big.start_three, 4), (big.start_three, 5)],
        (2, 0): [(flush, 1), (big.start_four, 2), (big.start_four, 3), (big.start_three, 0)],
        (2, 1): [(two, 1), (big.start_four, 4), (big.start_four, 5)],
        (2, 2): [(lambda _: table(), 0)],
        (2, 3): [(big.start_four, 0)],
        (2, 4): [(lambda _: early.start_two(), 0)],
    }
    for (at_sweep, at_step), acts in plan.items():

        @pl.when(moment(at_sweep, at_step))
        def _():
            for act, m in acts:
                act(m)

    @pl.when(sweep < 2)
    def _():
        for w in range(QUAD):
            gbp[SLOT * w : SLOT * w + slots, :] = gf_ref[slots * w : slots * w + slots, :].astype(B16)
        mine = pl.ds(pl.multiple_of(jnp.minimum(sweep, 1) * part_rows, part_rows), part_rows)
        datt[...] = dot(wproj_ref[mine, :], gbp[...], "NT").astype(B16)

        @pl.when(sweep == 0)
        def _():
            dwp[...] += dot(att_ref[...], gbp[...])

        ratio = size_head**-0.5
        target = dqkv.at[step, jnp.minimum(sweep, 1)]

        def score(w, g):
            low = pair * g
            lanes = slice(SLOT * w, SLOT * w + SLOT)
            for j in range(2):
                at = slice(low + size_head * j, low + size_head * (j + 1))
                cols = slice(SLOT * j, SLOT * j + SLOT)
                bdo[w % 3, at, cols] = datt[at, lanes]
                bdq[w % 3, at, cols] = qkv_ref[0, at, lanes]
                bdk[w % 3, at, cols] = qkv_ref[1, at, lanes]
            values = qkv_ref[2, low : low + pair, SLOT * w : SLOT * w + KEYS]
            dprobs[w % 2, g] = dot(values, bdo[w % 3, low : low + pair, :], "TN")

        def soften(w, g):
            probs = probs_ref[w, g, :KEYS, :].astype(F32)
            term = probs * dprobs[w % 2, g]
            grad = term - probs * jnp.sum(term, axis=0, keepdims=True)
            low_grad = grad.astype(B16)
            beside[w % 2, g, :KEYS, :] = low_grad
            for j in range(2):
                cols = slice(SLOT * j, SLOT * j + SLOT)
                dscore[2 * g + j] += grad[:, cols]
                stacked[w % 2, g, SLOT * j : SLOT * j + KEYS, :] = low_grad[:, cols]

        def attend(w, g):
            low = pair * g
            lanes = slice(SLOT * w, SLOT * w + SLOT)
            rows = slice(low, low + pair)
            got = dot(bdk[w % 3, rows, :], stacked[w % 2, g]) * ratio
            target[low : low + pair, lanes] = got.astype(B16)
            got = dot(bdq[w % 3, rows, :], beside[w % 2, g], "NT") * (1.0 / LOG2E)
            target[part_rows + low : part_rows + low + pair, lanes] = got.astype(B16)
            got = dot(bdo[w % 3, rows, :], probs_ref[w, g], "NT")
            target[2 * part_rows + low : 2 * part_rows + low + pair, lanes] = got.astype(B16)

        for stage in range(QUAD + 2):
            for g in range(pairs):
                if stage < QUAD:
                    score(stage, g)
                if 1 <= stage <= QUAD:
                    soften(stage - 1, g)
                if stage >= 2:
                    attend(stage - 2, g)

        grad = target[...]
        dwq[...] += dot(grad, n1_ref[...])
        wide = grad.astype(F32)
        both = wide[:, :SLOT]
        for w in range(1, QUAD):
            both = both + wide[:, SLOT * w : SLOT * w + SLOT]
        dbqkv[...] += both

    @pl.when(sweep == 2)
    def _():
        dn1 = dot(dqkv[step, 0], turned_ref[0], "TN") + dot(dqkv[step, 1], turned_ref[1], "TN")
        for w in range(QUAD):
            compact[slots * w : slots * w + slots, :] = dn1[SLOT * w : SLOT * w + slots, :]
        grad = compact[...]
        xhat, spread = norm_stats(x_ref[...].astype(F32))
        scaled = grad * gains_ref[0:1, :]
        mean_one = jnp.mean(scaled, axis=-1, keepdims=True)
        mean_two = jnp.mean(scaled * xhat, axis=-1, keepdims=True)
        sums[0:8, :] += fold(grad * xhat)
        sums[8:16, :] += fold(grad)
        compact[...] = gf_ref[...] + spread * (scaled - mean_one - xhat * mean_two)
        for w in range(QUAD):
            for r in range(window):
                ref, skip = piece(band, r, quad * QUAD * window, w, window, half)
                at = slots * w + window * r
                ref[skip : skip + window, :] = compact[at : at + window, :]

    for p in range(pages):
        for j in range(quads):

            @pl.when(moment(2, p * quads + j))
            def _():
                cut = slice(edge_at(j), edge_at(j + 1))
                edge[p, :, cut, :] = band[half:, cut, :].astype(B16)
                patch_copy(p, j).start()
                if j == quads - 1:
                    unwrap_band(band, live, half, width, window, least)
                    own_ref[0] = band[:half, :width].astype(B16)

    @pl.when(moment(2, pages * quads - 1))
    def _():
        big.start_three(1)
        for k in range(2):
            lay_lines(late.mine, lines * k, jnp.sum(sums[8 * k : 8 * k + 8, :], axis=0, keepdims=True))
        late.start_one()
        early.start_three()
        for m in outer:
            big.finish(m, sum_ref.at[m])
        big.finish(0, sum_ref.at[0])
        late.start_two()
        big.start_four(1)
        late.start_three()
        early.finish(small_ref, LATE)
        mixed_copy().wait()
        late.finish(small_ref, 0)
        big.finish(1, sum_ref.at[1])
        for p in range(pages):
            for j in range(quads):
                patch_copy(p, j).wait()


def attn_backward(
    live, dwup, dwout, mixed_next, gf, x, n1, qkv, probs, att, weights_in, turned, gains, places, early, shape, heads, least, share
):
    pages, window, width, model = shape
    half = window // 2
    quads = width // window // QUAD
    slots = window * window
    pairs = heads // 4
    part_rows = model // 2
    devices = (lax.axis_size("page"), lax.axis_size("rows"))
    chips = devices[1] // 2
    hidden = dwup.shape[1]
    wide = 2 * model
    cols = wide // devices[0]
    once = pl.Buffered(1)
    whole = lambda a: pl.BlockSpec(a.shape, lambda s, p, j: (0,) * a.ndim, pipeline_mode=once)
    held = lambda dims: pl.BlockSpec(dims, lambda s, p, j: (0,) * len(dims), pipeline_mode=once)
    anywhere = pl.BlockSpec(memory_space=pl.ANY)
    at = lambda p, j: p * quads + j
    last = pages * quads - 1
    both = lambda s, p, j: jnp.where(s < 2, at(p, j), last)
    first = lambda s, p, j: jnp.where(s == 0, at(p, j), last)
    third = lambda s, p, j: jnp.where(s == 2, at(p, j), 0)
    side = lambda s: jnp.minimum(s, 1)
    own_at = lambda s, p, j: (jnp.where(s == 2, p, 0), 0, 0, 0)
    dma = pltpu.SemaphoreType.DMA
    vmem = pltpu.VMEM
    n = 2 + 2 * hidden // wide
    lines = early.shape[0]

    def small_scratch(rows):
        return [
            vmem((rows, 128), F32),
            vmem((rows, 128), F32),
            vmem((rows, 128), F32),
            vmem((devices[0], rows, 128), F32),
            vmem((rows, 128), F32),
            vmem((chips, rows, 128), F32),
            dma((devices[0] + chips,)),
            dma((devices[0] + chips,)),
        ]

    return pl.pallas_call(
        functools.partial(
            attn_backward_kernel, (window, half, width, model, heads, least, pages, devices, share)
        ),
        grid=(3, pages, quads),
        in_specs=[
            pl.BlockSpec(memory_space=pltpu.SMEM),
            anywhere,
            anywhere,
            anywhere,
            pl.BlockSpec((QUAD * slots, model), lambda s, p, j: (at(p, j), 0)),
            pl.BlockSpec((QUAD * slots, model), lambda s, p, j: (third(s, p, j), 0)),
            pl.BlockSpec((QUAD * SLOT, model), lambda s, p, j: (both(s, p, j), 0)),
            pl.BlockSpec((3, part_rows, QUAD * SLOT), lambda s, p, j: (0, side(s), both(s, p, j))),
            pl.BlockSpec((QUAD, pairs, SLOT, 2 * SLOT), lambda s, p, j: (both(s, p, j), side(s), 0, 0)),
            pl.BlockSpec((model, QUAD * SLOT), lambda s, p, j: (0, first(s, p, j))),
            pl.BlockSpec((model, model), lambda s, p, j: (0, 3), pipeline_mode=once),
            whole(turned),
            whole(gains),
            whole(places),
            whole(early),
        ],
        out_specs=[
            held((n, share, wide)),
            held((LATE + lines, 128)),
            pl.BlockSpec((1, half, width, model), own_at),
            anywhere,
            anywhere,
        ],
        out_shape=[
            jax.ShapeDtypeStruct((n, share, wide), B16),
            jax.ShapeDtypeStruct((LATE + lines, 128), F32),
            jax.ShapeDtypeStruct((pages, half, width, model), B16),
            jax.ShapeDtypeStruct((pages, half, width, model), B16),
            jax.ShapeDtypeStruct((pages, half, width + 8, model), B16),
        ],
        scratch_shapes=[
            vmem((window, width + 8, model), F32),
            vmem((QUAD * SLOT, model), B16),
            vmem((part_rows, QUAD * SLOT), B16),
            vmem((2, pairs, KEYS, 2 * SLOT), F32),
            vmem((3, part_rows, 2 * SLOT), B16),
            vmem((3, part_rows, 2 * SLOT), B16),
            vmem((3, part_rows, 2 * SLOT), B16),
            vmem((2, pairs, 2 * SLOT, SLOT), B16),
            vmem((2, pairs, SLOT, 2 * SLOT), B16),
            vmem((pages * quads, 2, 3 * part_rows, QUAD * SLOT), B16),
            vmem((3 * part_rows, model), F32),
            vmem((model, model), F32),
            vmem((QUAD * slots, model), F32),
            vmem((heads // 2, KEYS, SLOT), F32),
            vmem((heads, KEYS, SLOT), F32),
            vmem((3 * part_rows, SLOT), F32),
            vmem((16, model), F32),
            vmem((2, model, wide), B16),
            vmem((pages, half, width + 8, model), B16),
            vmem((n - 2, chips, share, wide), B16),
            vmem((n, chips, share, wide), B16),
            vmem((n, devices[0], chips, share, cols), B16),
            vmem((n, devices[0], chips, share, cols), B16),
            vmem((n, chips, share, cols), B16),
            vmem((n, chips, share, cols), B16),
            vmem((n, share, cols), B16),
            vmem((n, devices[0], share, cols), B16),
            dma((n, chips)),
            dma((n, chips)),
            dma((n, devices[0])),
            dma((n, devices[0])),
            dma((n, chips)),
            dma((n, chips)),
            dma((n, devices[0])),
            dma((n, devices[0])),
        ]
        + small_scratch(lines)
        + small_scratch(LATE)
        + [dma((n - 2, chips)), dma((1 + pages * quads,)), dma((1 + pages * quads,))],
        compiler_params=pltpu.CompilerParams(
            vmem_limit_bytes=62 * 2**20, collective_id=0, has_side_effects=True
        ),
    )(live, dwup, dwout, mixed_next, gf, x, n1, qkv, probs, att, weights_in, turned, gains, places, early)


def finish_kernel(
    sizes,
    live_ref,
    sum_ref,
    min_ref,
    fin_ref,
    sin_ref,
    mout_ref,
    fout_ref,
    sout_ref,
    above_ref,
    own_ref,
    edge_ref,
    _,
    mixed_ref,
    patch_ref,
    new_in_ref,
    moment_in_ref,
    square_in_ref,
    new_out_ref,
    moment_out_ref,
    square_out_ref,
    band,
    grad_in,
):
    window, half, width, least = sizes
    step = pl.program_id(0)
    model = band.shape[2]
    part_rows = model // 2
    for s in range(FINISH_STEPS):

        @pl.when(step == s)
        def _():
            if s < 2:
                for h in range(2):
                    for part in range(2):
                        at = part * model + h * part_rows
                        from_at = (2 * s + part) * part_rows
                        grad_in[:, at : at + part_rows] = sum_ref[h, :, from_at : from_at + part_rows].astype(F32)
            else:
                grad_in[...] = sum_ref[s].astype(F32)
            cols = slice(model * (s % 2), model * (s % 2 + 1))
            grad = sum_ref[4 + s // 2, :, cols].astype(F32)
            new, moment, square = adam_update(mout_ref[...], fout_ref[...], sout_ref[...], grad)
            new_out_ref[...], moment_out_ref[...], square_out_ref[...] = new, moment, square
            if s % 2 == 0:
                mixed_ref[...] = above_ref[...]
                band[...] = edge_ref[0].astype(F32)
                unwrap_band(band, live_ref[s // 2], half, width, window, least)
                patch_ref[0] = band[:, :width].astype(B16)
            else:
                patch_ref[0] = own_ref[0]

    new, moment, square = adam_update(min_ref[...], fin_ref[...], sin_ref[...], grad_in[...])
    new_in_ref[...], moment_in_ref[...], square_in_ref[...] = new, moment, square


FINISH_STEPS = 4


def finish(live, sums, master_in, first_in, second_in, master_out, first_out, second_out, above, own, edge, mixed, least):
    pages, window, width, model = mixed.shape
    half = window // 2
    share, wide = master_in.shape
    tall = master_out.shape[0]
    cols = pl.BlockSpec((share, wide // FINISH_STEPS), lambda s: (0, s))
    rows = pl.BlockSpec((tall // FINISH_STEPS, model), lambda s: (s, 0))
    page = lambda s: (s // 2, 0, 0, 0)
    band = (1, half, width, model)
    like = lambda a: jax.ShapeDtypeStruct(a.shape, a.dtype)
    return pl.pallas_call(
        functools.partial(finish_kernel, (window, half, width, least)),
        grid=(FINISH_STEPS,),
        in_specs=[
            pl.BlockSpec(memory_space=pltpu.SMEM),
            pl.BlockSpec(sums.shape, lambda s: (0, 0, 0), pipeline_mode=pl.Buffered(1)),
            cols,
            cols,
            cols,
            rows,
            rows,
            rows,
            pl.BlockSpec(band, page),
            pl.BlockSpec(band, page),
            pl.BlockSpec((1, half, width + 8, model), page),
            pl.BlockSpec(memory_space=pl.ANY),
        ],
        out_specs=[
            pl.BlockSpec(band, page),
            pl.BlockSpec(band, lambda s: (s // 2, s % 2, 0, 0)),
        ]
        + [cols] * 3
        + [rows] * 3,
        out_shape=[like(mixed), like(mixed)] + [like(master_in)] * 3 + [like(master_out)] * 3,
        scratch_shapes=[
            pltpu.VMEM((half, width + 8, model), F32),
            pltpu.VMEM((share, wide // FINISH_STEPS), F32),
        ],
        input_output_aliases={11: 0},
        compiler_params=pltpu.CompilerParams(vmem_limit_bytes=VMEM_LIMIT),
    )(live, sums, master_in, first_in, second_in, master_out, first_out, second_out, above, own, edge, mixed)


def adam_update(master, first, second, grad):
    moment = BETA_ONE * first + (1.0 - BETA_ONE) * grad
    square = BETA_TWO * second + (1.0 - BETA_TWO) * grad * grad
    fix_one = 1.0 - BETA_ONE**STEP
    fix_two = 1.0 - BETA_TWO**STEP
    fresh = master - LEARN_RATE * (
        moment / fix_one / (jnp.sqrt(square / fix_two) + ADAM_EPS) + WEIGHT_DECAY * master
    )
    return (fresh, moment, square)


def shards(
    patches,
    out_grad,
    page_windows,
    region_ids,
    offset_index,
    weights_in,
    weights_out,
    norm_gains,
    biases,
    bias_table,
    master_in,
    master_out,
    first_in,
    second_in,
    first_out,
    second_out,
    first_small,
    second_small,
):
    pages, window, width, model = patches.shape
    half = window // 2
    count = width // window
    least = (count + 1) // 2
    slots = window * window
    table_rows, heads = bias_table.shape
    hidden = weights_out.shape[0]

    labels = region_ids.reshape(pages, window, count, window).transpose(0, 2, 1, 3)
    labels = labels.reshape(pages * count // QUAD, QUAD, slots).astype(F32)
    labels = jnp.pad(labels, ((0, 0), (0, 8 - QUAD), (0, SLOT - slots)), constant_values=-1.0)
    bias_lines = biases.reshape(-1, 128)
    lines = model // 128
    table_lanes = -(-table_rows // 128) * 128
    early_lines = EARLY_UP * lines + hidden // 128 + table_lanes * heads // 128

    x, n1, qkv, probs, att, first, n2, below_grad, turned, places = attn_forward(
        page_windows, patches, out_grad, labels, offset_index, bias_table, weights_in, norm_gains, bias_lines, least
    )
    dwup, dwout, gf, mixed_own, mixed_next, early = mlp(
        page_windows, out_grad, below_grad, n2, first, weights_in, weights_out, norm_gains, bias_lines,
        least, master_in.shape[0], early_lines,
    )
    sums, small, patch_own, above, edge = attn_backward(
        page_windows, dwup, dwout, mixed_next, gf, x, n1, qkv, probs, att, weights_in, turned, norm_gains,
        places, early, patches.shape, heads, least, master_in.shape[0],
    )
    mixed, patch_grad, new_in, moment_in, square_in, new_out, moment_out, square_out = finish(
        page_windows, sums, master_in, first_in, second_in, master_out, first_out, second_out, above, patch_own,
        edge, mixed_own, least,
    )
    small_at = [0, 4, 1, 2, 3, 5, 6, 7]
    table_at = small.shape[0] - table_lanes * heads // 128
    total_table = small[table_at:].reshape(table_lanes // 128, heads, 128).transpose(0, 2, 1)
    total_table = total_table.reshape(table_lanes, heads)[:table_rows]
    head = [small[lines * k : lines * k + lines] for k in small_at] + [small[8 * lines : table_at]]
    total_small = jnp.concatenate([jnp.concatenate(head).reshape(-1), total_table.reshape(-1)])
    small_master = jnp.concatenate([norm_gains.reshape(-1), biases, bias_table.reshape(-1)])
    new_small, moment_small, square_small = adam_update(
        small_master, first_small, second_small, total_small
    )
    return (
        mixed,
        patch_grad,
        new_in,
        moment_in,
        square_in,
        new_out,
        moment_out,
        square_out,
        new_small,
        moment_small,
        square_small,
    )


def solution(mesh):
    return jax.shard_map(
        shards,
        mesh=mesh,
        in_specs=(
            P("page", "rows", None, None),
            P("page", "rows", None, None),
            P("page"),
            P("page", "rows", None),
            P(),
            P(),
            P(),
            P(),
            P(),
            P(),
            P("rows", None),
            P("rows", None),
            P("rows", None),
            P("rows", None),
            P("rows", None),
            P("rows", None),
            P(),
            P(),
        ),
        out_specs=(
            P("page", "rows", None, None),
            P("page", "rows", None, None),
            P("rows", None),
            P("rows", None),
            P("rows", None),
            P("rows", None),
            P("rows", None),
            P("rows", None),
            P(),
            P(),
            P(),
        ),
        check_vma=False,
    )
```

```python
import functools
import math

import jax
import jax.numpy as jnp
from jax import lax
from jax.experimental import pallas as pl
from jax.experimental.pallas import tpu as pltpu
from jax.sharding import PartitionSpec as P

STEP = 10
NORM_EPS = 1e-05
BETA_ONE = 0.9
BETA_TWO = 0.999
LEARN_RATE = 0.04
WEIGHT_DECAY = 0.05
ADAM_EPS = 1e-08
MASK_VALUE = -1000000000.0

F32 = jnp.float32
B16 = jnp.bfloat16
LOG2E = math.log2(math.e)
VMEM_LIMIT = 60 * 2**20

QUAD = 4
SLOT = 128
KEYS = 104


def dot(left, right, form="NN"):
    sides = {
        "NN": ((1,), (0,)),
        "NT": ((1,), (1,)),
        "TN": ((0,), (0,)),
    }[form]
    return lax.dot_general(left, right, (sides, ((), ())), preferred_element_type=F32)


def load_band(band, low_ref, high_ref, live, half, width, window, least, start=0, end=None):
    end = width if end is None else end
    band[:half, start:end] = low_ref[:, start:end].astype(F32)
    band[half:, start:end] = high_ref[:, start:end].astype(F32)
    if end == width:
        band[:, width:] = jnp.zeros((window, band.shape[1] - width, band.shape[2]), F32)
        for count in range(least, width // window + 1):
            at = slice(count * window, count * window + half)
            band[:, at] = jnp.where(live == count, band[:, :half], band[:, at])


def unwrap_band(band, live, half, width, window, least):
    front = band[:, :half]
    for count in range(least, width // window + 1):
        at = slice(count * window, count * window + half)
        front = jnp.where(live == count, band[:, at], front)
    band[:, :half] = front
    edge = least * window // 8 * 8
    shape = (band.shape[0], width - edge, band.shape[2])
    columns = lax.broadcasted_iota(jnp.int32, shape, 1) + edge
    band[:, edge:width] = jnp.where(columns < live * window, band[:, edge:width], 0.0)


def piece(band, row, base, place, window, half):
    start = window * place + half
    aligned = start // 8 * 8
    skip = start - aligned
    size = -(-(skip + window) // 8) * 8
    ref = band.at[row, pl.ds(pl.multiple_of(base, 8) + aligned, size), :]
    return ref, skip


def gather_window(band, base, place, window, half):
    parts = []
    for row in range(window):
        ref, skip = piece(band, row, base, place, window, half)
        parts.append(ref[skip : skip + window, :])
    return parts


def norm_stats(value):
    centre = jnp.mean(value, axis=-1, keepdims=True)
    centered = value - centre
    spread = lax.rsqrt(jnp.mean(centered * centered, axis=-1, keepdims=True) + NORM_EPS)
    return centered * spread, spread


def fold(value):
    rows, cols = value.shape
    return jnp.sum(value.reshape(rows // 8, 8, cols), axis=0)


MESH = pl.DeviceIdType.MESH


def remote(src, dst, send, recv, device):
    return pltpu.make_async_remote_copy(
        src_ref=src, dst_ref=dst, send_sem=send, recv_sem=recv, device_id=device, device_id_type=MESH
    )


def lay_lines(lines_ref, at, row):
    for i in range(row.shape[1] // 128):
        lines_ref[at + i : at + i + 1, :] = row[:, 128 * i : 128 * i + 128]


def lay_row(ref, row, lines_ref, at, count):
    for i in range(count):
        ref[row : row + 1, 128 * i : 128 * i + 128] = lines_ref[at + i : at + i + 1, :]


def attn_forward_kernel(
    sizes,
    live_ref,
    patches_ref,
    grads_ref,
    low_ref,
    label_ref,
    off_ref,
    tab_ref,
    wqkv_ref,
    wproj_ref,
    gains_ref,
    biases_ref,
    x_ref,
    n1_ref,
    qkv_ref,
    probs_ref,
    att_ref,
    first_ref,
    n2_ref,
    grad_halo_ref,
    turned_ref,
    places_ref,
    halo,
    send,
    recv,
    band,
    bias,
    scores,
    bdq,
    bdv,
    stacked,
    xs,
    ns,
    vecs,
    column,
    square,
    tall,
    flat,
):
    window, half, width, model, heads, least, pages, rows_count = sizes
    slots = window * window
    size_head = model // heads
    page, quad = pl.program_id(0), pl.program_id(1)
    live = live_ref[page]
    pairs = heads // 2
    part_rows = model // 2
    lines = model // 128
    row = lax.axis_index("rows")
    behind, ahead = lax.rem(row + rows_count - 1, rows_count), lax.rem(row + 1, rows_count)

    cut = -(-(QUAD * window + half) // 16) * 16

    def halo_copy(p, k):
        at = (pl.ds(0, cut), pl.ds(cut, width - cut))[k]
        return remote(
            patches_ref.at[p, pl.ds(0, half), at],
            halo.at[p, :, at],
            send.at[pages * (1 + k) + p],
            recv.at[pages * (1 + k) + p],
            {"rows": behind},
        )

    def grad_copy(p):
        return remote(
            grads_ref.at[p, pl.ds(0, half)],
            grad_halo_ref.at[p],
            send.at[p],
            recv.at[p],
            {"rows": behind},
        )

    @pl.when(jnp.logical_and(page == 0, quad == 0))
    def _():
        barrier = pltpu.get_barrier_semaphore()
        for neighbour in (behind, ahead):
            pl.semaphore_signal(barrier, inc=1, device_id={"rows": neighbour}, device_id_type=MESH)
        pl.semaphore_wait(barrier, 2)
        halo_copy(0, 0).start()
        vecs[...] = jnp.zeros_like(vecs)
        vecs[0:1, :] = gains_ref[0:1, :]
        lay_row(vecs, 1, biases_ref, 0, lines)
        lay_row(vecs, 2, biases_ref, 3 * lines, lines)
        vecs[3:4, :] = gains_ref[1:2, :]
        lay_row(vecs, 4, biases_ref, 4 * lines, lines)
        column[...] = jnp.zeros_like(column)
        for h in range(2):
            for part in range(3):
                rows = slice(part * part_rows, part * part_rows + part_rows)
                cols = slice(part * model + h * part_rows, part * model + (h + 1) * part_rows)
                turned_ref[h, rows, :] = wqkv_ref[:, cols].T
                if part != 1:
                    for i in range(part_rows // 128):
                        line = lines * (1 + part // 2) + h * (part_rows // 128) + i
                        spread = jnp.broadcast_to(biases_ref[line : line + 1, :], (128, 128))
                        at = part * part_rows + 128 * i
                        column[h, at : at + 128, :] = spread.T
        halo_copy(0, 1).start()
        square[...] = jnp.full_like(square, -1)
        square[:slots, :slots] = off_ref[...]
        places = square[...].T[:KEYS]
        places_ref[...] = places
        off = jnp.maximum(places, 0)
        tall[...] = jnp.zeros_like(tall)
        tall[: tab_ref.shape[0], :heads] = tab_ref[...] * LOG2E
        for c in range(tall.shape[0] // 128):
            flat[:, 128 * c : 128 * c + 128] = tall[128 * c : 128 * c + 128, :].T[:heads]
        low, high = jnp.bitwise_and(off, 127), jnp.right_shift(off, 7)
        for h in range(heads):
            got = jnp.zeros((KEYS, SLOT), F32)
            for c in range(tall.shape[0] // 128):
                source = jnp.broadcast_to(flat[h : h + 1, 128 * c : 128 * c + 128], (KEYS, SLOT))
                picked = jnp.take_along_axis(source, low, axis=1, mode="promise_in_bounds")
                got = jnp.where(high == c, picked, got)
            bias[h] = got
        bdq[...] = jnp.zeros_like(bdq)
        bdv[...] = jnp.zeros_like(bdv)
        stacked[...] = jnp.zeros_like(stacked)

    for p in range(pages):

        @pl.when(jnp.logical_and(page == p, quad == 0))
        def _():
            halo_copy(p, 0).wait()
            load_band(band, low_ref.at[0], halo.at[p], live, half, width, window, least, 0, cut)

        @pl.when(jnp.logical_and(page == p, quad == 1))
        def _():
            halo_copy(p, 1).wait()
            if p + 1 < pages:
                for k in range(2):
                    halo_copy(p + 1, k).start()
            load_band(band, low_ref.at[0], halo.at[p], live, half, width, window, least, cut)

    @pl.when(jnp.logical_and(page == (pages - 1) // 2, quad == 2))
    def _():
        for p in range(pages):
            grad_copy(p).start()

    @pl.when(jnp.logical_and(page == pages - 1, quad == pl.num_programs(1) - 1))
    def _():
        for p in range(pages):
            grad_copy(p).wait()

    base = quad * (QUAD * window)
    for w in range(QUAD):
        for r, part in enumerate(gather_window(band, base, w, window, half)):
            at = slots * w + window * r
            xs[at : at + window, :] = part
    x = xs[...]
    x_ref[...] = x.astype(B16)
    xhat, _ = norm_stats(x)
    ns[...] = xhat * vecs[0:1, :] + vecs[1:2, :]
    for w in range(QUAD):
        n1_ref[SLOT * w : SLOT * w + slots, :] = ns[slots * w : slots * w + slots, :].astype(B16)
        n1_ref[SLOT * w + slots : SLOT * w + SLOT, :] = jnp.zeros((SLOT - slots, model), B16)
    scale = size_head**-0.5 * LOG2E
    n1 = n1_ref[...]
    for h in range(2):
        got = dot(turned_ref[h], n1, "NT") + column[h, :, 0:1]
        at = slice(h * part_rows, h * part_rows + part_rows)
        qkv_ref[0, at, :] = (got[:part_rows] * scale).astype(B16)
        qkv_ref[1, at, :] = got[part_rows : 2 * part_rows].astype(B16)
        qkv_ref[2, at, :] = got[2 * part_rows :].astype(B16)

    sames = []
    for w in range(QUAD):
        spread = jnp.broadcast_to(label_ref[0, w : w + 1, :], (SLOT, SLOT))
        sames.append((spread == spread.T)[:KEYS])
    pair = 2 * size_head

    def score(w, g):
        low = pair * g
        lanes = slice(SLOT * w, SLOT * w + SLOT)
        for j in range(2):
            at = slice(low + size_head * j, low + size_head * (j + 1))
            cols = slice(SLOT * j, SLOT * j + SLOT)
            bdq[w % 2, at, cols] = qkv_ref[0, at, lanes]
            bdv[w % 3, at, cols] = qkv_ref[2, at, lanes]
        keys = qkv_ref[1, low : low + pair, SLOT * w : SLOT * w + KEYS]
        scores[w % 2, g] = dot(keys, bdq[w % 2, low : low + pair, :], "TN")

    def soften(w, g):
        for j in range(2):
            cols = slice(SLOT * j, SLOT * j + SLOT)
            s = jnp.where(sames[w], scores[w % 2, g, :, cols] + bias[2 * g + j], MASK_VALUE)
            s = jnp.exp2(s - jnp.max(s, axis=0, keepdims=True))
            low_probs = (s * (1.0 / jnp.sum(s, axis=0, keepdims=True))).astype(B16)
            probs_ref[w, g, :KEYS, cols] = low_probs
            probs_ref[w, g, KEYS:, cols] = jnp.zeros((SLOT - KEYS, SLOT), B16)
            stacked[w % 2, g, SLOT * j : SLOT * j + KEYS, :] = low_probs

    def attend(w, g):
        low = pair * g
        got = dot(bdv[w % 3, low : low + pair, :], stacked[w % 2, g])
        att_ref[low : low + pair, SLOT * w : SLOT * w + SLOT] = got.astype(B16)

    for step in range(QUAD + 2):
        for g in range(pairs):
            if step < QUAD:
                score(step, g)
            if 1 <= step <= QUAD:
                soften(step - 1, g)
            if step >= 2:
                attend(step - 2, g)

    branch = dot(att_ref[...], wproj_ref[...], "TN")
    for w in range(QUAD):
        rows = slice(slots * w, slots * w + slots)
        first_ref[rows, :] = xs[rows, :] + branch[SLOT * w : SLOT * w + slots, :] + vecs[2:3, :]
    xhat, _ = norm_stats(first_ref[...])
    n2_ref[...] = (xhat * vecs[3:4, :] + vecs[4:5, :]).astype(B16)


def attn_forward(live, patches, out_grad, labels, off, tab, weights_in, gains, biases, least):
    pages, window, width, model = patches.shape
    half = window // 2
    table_rows, heads = tab.shape
    table_lanes = -(-table_rows // 128) * 128
    quads = width // window // QUAD
    tokens = pages * window * width
    slots = window * window
    padded = pages * quads * QUAD * SLOT
    steps = (pages, quads)
    whole = lambda a: pl.BlockSpec(a.shape, lambda p, j: (0,) * a.ndim, pipeline_mode=pl.Buffered(1))
    at = lambda p, j: p * quads + j
    return pl.pallas_call(
        functools.partial(
            attn_forward_kernel,
            (window, half, width, model, heads, least, pages, lax.axis_size("rows")),
        ),
        grid=steps,
        in_specs=[
            pl.BlockSpec(memory_space=pltpu.SMEM),
            pl.BlockSpec(memory_space=pl.ANY),
            pl.BlockSpec(memory_space=pl.ANY),
            pl.BlockSpec((1, half, width, model), lambda p, j: (p, 1, 0, 0)),
            pl.BlockSpec((1, 8, SLOT), lambda p, j: (at(p, j), 0, 0)),
            whole(off),
            whole(tab),
            pl.BlockSpec((model, 3 * model), lambda p, j: (0, 0), pipeline_mode=pl.Buffered(1)),
            pl.BlockSpec((model, model), lambda p, j: (0, 3), pipeline_mode=pl.Buffered(1)),
            whole(gains),
            whole(biases),
        ],
        out_specs=[
            pl.BlockSpec((QUAD * slots, model), lambda p, j: (at(p, j), 0)),
            pl.BlockSpec((QUAD * SLOT, model), lambda p, j: (at(p, j), 0)),
            pl.BlockSpec((3, model, QUAD * SLOT), lambda p, j: (0, 0, at(p, j))),
            pl.BlockSpec((QUAD, heads // 2, SLOT, 2 * SLOT), lambda p, j: (at(p, j), 0, 0, 0)),
            pl.BlockSpec((model, QUAD * SLOT), lambda p, j: (0, at(p, j))),
            pl.BlockSpec((QUAD * slots, model), lambda p, j: (at(p, j), 0)),
            pl.BlockSpec((QUAD * slots, model), lambda p, j: (at(p, j), 0)),
            pl.BlockSpec(memory_space=pl.ANY),
            pl.BlockSpec((2, 3 * model // 2, model), lambda p, j: (0, 0, 0), pipeline_mode=pl.Buffered(1)),
            pl.BlockSpec((KEYS, SLOT), lambda p, j: (0, 0)),
        ],
        out_shape=[
            jax.ShapeDtypeStruct((tokens, model), B16),
            jax.ShapeDtypeStruct((padded, model), B16),
            jax.ShapeDtypeStruct((3, model, padded), B16),
            jax.ShapeDtypeStruct((pages * quads * QUAD, heads // 2, SLOT, 2 * SLOT), B16),
            jax.ShapeDtypeStruct((model, padded), B16),
            jax.ShapeDtypeStruct((tokens, model), F32),
            jax.ShapeDtypeStruct((tokens, model), B16),
            jax.ShapeDtypeStruct((pages, half, width, model), B16),
            jax.ShapeDtypeStruct((2, 3 * model // 2, model), B16),
            jax.ShapeDtypeStruct((KEYS, SLOT), jnp.int32),
        ],
        scratch_shapes=[
            pltpu.VMEM((pages, half, width, model), B16),
            pltpu.SemaphoreType.DMA((3 * pages,)),
            pltpu.SemaphoreType.DMA((3 * pages,)),
            pltpu.VMEM((window, width + 8, model), F32),
            pltpu.VMEM((heads, KEYS, SLOT), F32),
            pltpu.VMEM((2, heads // 2, KEYS, 2 * SLOT), F32),
            pltpu.VMEM((2, model, 2 * SLOT), B16),
            pltpu.VMEM((3, model, 2 * SLOT), B16),
            pltpu.VMEM((2, heads // 2, 2 * SLOT, SLOT), B16),
            pltpu.VMEM((QUAD * slots, model), F32),
            pltpu.VMEM((QUAD * slots, model), F32),
            pltpu.VMEM((8, model), F32),
            pltpu.VMEM((2, 3 * model // 2, 128), F32),
            pltpu.VMEM((SLOT, SLOT), jnp.int32),
            pltpu.VMEM((table_lanes, 128), F32),
            pltpu.VMEM((heads, table_lanes), F32),
        ],
        compiler_params=pltpu.CompilerParams(
            vmem_limit_bytes=VMEM_LIMIT, collective_id=1, has_side_effects=True
        ),
    )(live, patches, out_grad, patches, labels, off, tab, weights_in, weights_in, gains, biases)


MLP_COLS = 1024
MLP_CHUNKS = 2
MLP_ROWS = 480
EARLY_UP = 8


def mlp_kernel(
    sizes,
    live_ref,
    low_ref,
    high_ref,
    n2_ref,
    first_ref,
    wup_ref,
    wout_ref,
    gains_ref,
    biases_ref,
    dwup_ref,
    dwout_ref,
    gf_ref,
    own_ref,
    next_ref,
    early_ref,
    bup,
    vecs,
    sums,
    band,
    cot,
    res,
    dn2,
    act_all,
    pre_all,
):
    window, half, width, model, least, share = sizes
    pages = low_ref.shape[0]
    slots = window * window
    count = width // window
    quads = count // QUAD
    chunk = pl.program_id(0)
    tokens = n2_ref.shape[0]
    cols = wup_ref.shape[1]
    lines = model // 128

    for c in range(MLP_CHUNKS):

        @pl.when(chunk == c)
        def _():
            lay_row(bup, 0, biases_ref, 6 * lines + c * (cols // 128), cols // 128)

    @pl.when(chunk == 0)
    def _():
        early_ref[...] = jnp.zeros_like(early_ref)
        vecs[0:1, :] = gains_ref[1:2, :]
        lay_row(vecs, 1, biases_ref, 5 * lines, lines)
        for page in range(pages):
            live = live_ref[page]
            load_band(band, low_ref.at[page], high_ref.at[page], live, half, width, window, least)

            def body(j, carry):
                for w in range(QUAD):
                    alive = jnp.where(j * QUAD + w < live, 1.0, 0.0)
                    for r, part in enumerate(gather_window(band, j * QUAD * window, w, window, half)):
                        at = slots * w + window * r
                        gf_ref[at : at + window, :] = part * alive
                rows = pl.ds(pl.multiple_of((page * quads + j) * QUAD * slots, 16), QUAD * slots)
                cot[rows, :] = gf_ref[: QUAD * slots, :].astype(B16)
                return carry

            lax.fori_loop(0, quads, body, 0)

    def body(i, total):
        rows = pl.ds(pl.multiple_of(i * MLP_ROWS, 16), MLP_ROWS)
        grad = cot[rows, :]
        pre = dot(n2_ref[rows, :], wup_ref[...]) + bup[0:1, :]
        grad_act = dot(grad, wout_ref[...], "NT")
        share = 0.5 * (1.0 + lax.erf(pre * 0.5**0.5))
        act = (pre * share).astype(B16)
        slope = share + pre * (jnp.exp2((-0.5 * LOG2E) * pre * pre) * (2.0 * math.pi) ** -0.5)
        grad_pre = (grad_act * slope).astype(B16)
        act_all[rows, :] = act
        pre_all[rows, :] = grad_pre
        up = dot(act, wout_ref[...])
        down = dot(grad_pre, wup_ref[...], "NT")

        res[rows, :] = jnp.where(chunk == 0, 0.0, res[rows, :]) + up
        dn2[rows, :] = jnp.where(chunk == 0, 0.0, dn2[rows, :]) + down
        return total + fold(grad_pre.astype(F32))

    total = lax.fori_loop(0, tokens // MLP_ROWS, body, jnp.zeros((8, cols), F32))
    total = jnp.sum(total, axis=0, keepdims=True)
    for c in range(MLP_CHUNKS):

        @pl.when(chunk == c)
        def _():
            lay_lines(early_ref, EARLY_UP * lines + c * (cols // 128), total)

    grad_out = dot(act_all[...], cot[...], "TN").astype(B16)
    for s in range(dwout_ref.shape[0] // share):
        for a in range(dwout_ref.shape[1] // model):
            at = (s * (dwout_ref.shape[1] // model) + a) * share
            dwout_ref[share * s : share * s + share, model * a : model * a + model] = grad_out[at : at + share, :]
    dwup_ref[...] = dot(n2_ref[...], pre_all[...], "TN").astype(B16)

    @pl.when(chunk == pl.num_programs(0) - 1)
    def _():
        sums[...] = jnp.zeros_like(sums)
        for page in range(pages):
            live = live_ref[page]

            def body(j, carry):
                at = pl.multiple_of((page * quads + j) * QUAD * slots, 16)
                rows = pl.ds(at, QUAD * slots)
                first = first_ref[rows, :]
                res[rows, :] += first + vecs[1:2, :]
                xhat, spread = norm_stats(first)
                grad = dn2[rows, :]
                given = cot[rows, :].astype(F32)
                scaled = grad * vecs[0:1, :]
                mean_one = jnp.mean(scaled, axis=-1, keepdims=True)
                mean_two = jnp.mean(scaled * xhat, axis=-1, keepdims=True)
                whole = given + spread * (scaled - mean_one - xhat * mean_two)
                gf_ref[rows, :] = whole
                sums[0:8, :] += fold(grad * xhat)
                sums[8:16, :] += fold(whole)
                sums[16:24, :] += fold(grad)
                sums[24:32, :] += fold(given)
                for w in range(QUAD):
                    for r in range(window):
                        ref, skip = piece(band, r, j * QUAD * window, w, window, half)
                        ref[skip : skip + window, :] = res[
                            pl.ds(at + slots * w // 8 * 8, slots + 4), :
                        ][slots * w % 8 + window * r : slots * w % 8 + window * r + window, :]
                return carry

            lax.fori_loop(0, quads, body, 0)
            unwrap_band(band, live, half, width, window, least)
            own_ref[page] = band[:half, :width].astype(B16)
            next_ref[page] = band[half:, :width].astype(B16)
        for k in range(4):
            lay_lines(early_ref, (4 + k) * lines, jnp.sum(sums[8 * k : 8 * k + 8, :], axis=0, keepdims=True))


def mlp(live, out_grad, halo, n2, first, weights_in, weights_out, gains, biases, least, share, lines):
    pages, window, width, model = out_grad.shape
    half = window // 2
    tokens = n2.shape[0]
    hidden = weights_out.shape[0]
    skip = (weights_in.shape[1] - hidden) // MLP_COLS
    once = pl.Buffered(1)
    whole = lambda a: pl.BlockSpec(a.shape, lambda c: (0,) * a.ndim, pipeline_mode=once)
    band_block = (pages, half, width, model)
    return pl.pallas_call(
        functools.partial(mlp_kernel, (window, half, width, model, least, share)),
        grid=(hidden // MLP_COLS,),
        in_specs=[
            pl.BlockSpec(memory_space=pltpu.SMEM),
            pl.BlockSpec(band_block, lambda c: (0, 1, 0, 0), pipeline_mode=once),
            pl.BlockSpec(band_block, lambda c: (0, 0, 0, 0), pipeline_mode=once),
            whole(n2),
            whole(first),
            pl.BlockSpec((model, MLP_COLS), lambda c: (0, c + skip)),
            pl.BlockSpec((MLP_COLS, model), lambda c: (c, 0)),
            whole(gains),
            whole(biases),
        ],
        out_specs=[
            pl.BlockSpec((model, MLP_COLS), lambda c: (0, c)),
            pl.BlockSpec((model * MLP_COLS // hidden, hidden), lambda c: (c, 0)),
            pl.BlockSpec((tokens, model), lambda c: (0, 0), pipeline_mode=once),
            pl.BlockSpec(band_block, lambda c: (0, 1, 0, 0), pipeline_mode=once),
            pl.BlockSpec(band_block, lambda c: (0, 0, 0, 0), pipeline_mode=once),
            pl.BlockSpec((lines, 128), lambda c: (0, 0)),
        ],
        out_shape=[
            jax.ShapeDtypeStruct((model, hidden), B16),
            jax.ShapeDtypeStruct((model, hidden), B16),
            jax.ShapeDtypeStruct((tokens, model), F32),
            jax.ShapeDtypeStruct(out_grad.shape, B16),
            jax.ShapeDtypeStruct(band_block, B16),
            jax.ShapeDtypeStruct((lines, 128), F32),
        ],
        scratch_shapes=[
            pltpu.VMEM((8, MLP_COLS), F32),
            pltpu.VMEM((8, model), F32),
            pltpu.VMEM((32, model), F32),
            pltpu.VMEM((window, width + 8, model), F32),
            pltpu.VMEM((tokens, model), B16),
            pltpu.VMEM((tokens, model), F32),
            pltpu.VMEM((tokens, model), F32),
            pltpu.VMEM((tokens, MLP_COLS), B16),
            pltpu.VMEM((tokens, MLP_COLS), B16),
        ],
        compiler_params=pltpu.CompilerParams(vmem_limit_bytes=VMEM_LIMIT),
    )(live, out_grad, halo, n2, first, weights_in, weights_out, gains, biases)


def table_sum(off_ref, grad_ref, out_ref, at, heads, chunks):
    rows = 128 * chunks
    keys = grad_ref.shape[1]
    names = lax.broadcasted_iota(jnp.int32, (rows, SLOT), 0)
    total = jnp.zeros((3 * heads, rows), F32)
    grad = jnp.swapaxes(grad_ref[...], 0, 1)
    for k in range(0, keys, 8):
        hot = jnp.concatenate(
            [jnp.where(names == off_ref[i : i + 1, :], 1.0, 0.0).astype(B16) for i in range(k, k + 8)], axis=1
        )
        value = jnp.concatenate([grad[i] for i in range(k, k + 8)], axis=1)
        high = value.astype(B16)
        rest = value - high.astype(F32)
        middle = rest.astype(B16)
        low = (rest - middle.astype(F32)).astype(B16)
        total += dot(jnp.concatenate([high, middle, low], axis=0), hot, "NT")
    total = total[:heads] + total[heads : 2 * heads] + total[2 * heads :]
    for c in range(chunks):
        out_ref[at + heads * c : at + heads * c + heads, :] = total[:, 128 * c : 128 * c + 128]


class Exchange:
    def __init__(self, pages, chips, share, bufs, sems):
        self.pages, self.chips, self.share = pages, chips, share
        self.rec1, self.s1, self.rec2, self.s2, self.rec3, self.s3, self.rec4 = bufs
        self.send1, self.recv1, self.send2, self.recv2, self.send3, self.recv3, self.send4, self.recv4 = sems
        self.page, row = lax.axis_index("page"), lax.axis_index("rows")
        self.chip, self.core = row // 2, row % 2
        self.other = 2 * self.chip + 1 - self.core
        self.cols = self.s3.shape[-1]

    def page_peer(self, d):
        return lax.rem(self.page + d, self.pages)

    def chip_peer(self, d):
        return lax.rem(self.chip + d, self.chips)

    def along(self, d):
        return {"rows": 2 * self.chip_peer(d) + self.core}

    def rows_of(self, ref, z, c):
        return ref.at[pl.ds(pl.multiple_of((2 * z + c) * self.share, 16), self.share), :]

    def one(self, m, grad):
        return [
            remote(
                self.rows_of(grad, z, 1 - self.core),
                self.rec1.at[m, z],
                self.send1.at[m, z],
                self.recv1.at[m, z],
                {"rows": self.other},
            )
            for z in range(self.chips)
        ]

    def two(self, m):
        return [
            remote(
                self.s1.at[m, self.page_peer(d)],
                self.rec2.at[m, self.page],
                self.send2.at[m, d],
                self.recv2.at[m, d],
                {"page": self.page_peer(d)},
            )
            for d in range(1, self.pages)
        ]

    def three(self, m):
        return [
            remote(
                self.s2.at[m, self.chip_peer(d)],
                self.rec3.at[m, self.chip],
                self.send3.at[m, d],
                self.recv3.at[m, d],
                self.along(d),
            )
            for d in range(1, self.chips)
        ]

    def four(self, m):
        return [
            remote(
                self.s3.at[m],
                self.rec4.at[m, self.page],
                self.send4.at[m, d],
                self.recv4.at[m, d],
                {"page": self.page_peer(d)},
            )
            for d in range(1, self.pages)
        ]

    def start_one(self, m, grad):
        start(self.one(m, grad))

    def start_two(self, m, grad, own):
        wait(self.one(m, grad))
        for q in range(self.pages):
            at = slice(self.cols * q, self.cols * q + self.cols)
            for z in range(self.chips):
                self.s1[m, q, z] = (own(z)[:, at].astype(F32) + self.rec1[m, z, :, at].astype(F32)).astype(B16)
        start(self.two(m))
        self.rec2[m, self.page] = self.s1[m, self.page]

    def start_three(self, m):
        wait(self.two(m))
        total = self.rec2[m, 0].astype(F32)
        for q in range(1, self.pages):
            total = total + self.rec2[m, q].astype(F32)
        self.s2[m] = total.astype(B16)
        start(self.three(m))
        self.rec3[m, self.chip] = self.s2[m, self.chip]

    def start_four(self, m):
        wait(self.three(m))
        total = self.rec3[m, 0].astype(F32)
        for z in range(1, self.chips):
            total = total + self.rec3[m, z].astype(F32)
        self.s3[m] = total.astype(B16)
        start(self.four(m))
        self.rec4[m, self.page] = self.s3[m]

    def finish(self, m, out_ref):
        wait(self.four(m))
        for q in range(self.pages):
            out_ref[:, self.cols * q : self.cols * q + self.cols] = self.rec4[m, q]


class SmallExchange:
    def __init__(self, big, bufs, sems):
        self.big = big
        self.mine, self.one_in, self.two_out, self.two_in, self.three_out, self.three_in = bufs
        self.send, self.recv = sems

    def one(self):
        return [remote(self.mine, self.one_in, self.send.at[0], self.recv.at[0], {"rows": self.big.other})]

    def two(self):
        big = self.big
        return [
            remote(
                self.two_out,
                self.two_in.at[big.page],
                self.send.at[d],
                self.recv.at[d],
                {"page": big.page_peer(d)},
            )
            for d in range(1, big.pages)
        ]

    def three(self):
        big = self.big
        return [
            remote(
                self.three_out,
                self.three_in.at[big.chip],
                self.send.at[big.pages + d],
                self.recv.at[big.pages + d],
                big.along(d),
            )
            for d in range(1, big.chips)
        ]

    def start_one(self):
        start(self.one())

    def start_two(self):
        wait(self.one())
        total = self.mine[...] + self.one_in[...]
        self.two_out[...] = total
        start(self.two())
        self.two_in[self.big.page] = total

    def start_three(self):
        wait(self.two())
        total = self.two_in[0]
        for q in range(1, self.big.pages):
            total = total + self.two_in[q]
        self.three_out[...] = total
        start(self.three())
        self.three_in[self.big.chip] = total

    def finish(self, out_ref, at):
        wait(self.three())
        total = self.three_in[0]
        for z in range(1, self.big.chips):
            total = total + self.three_in[z]
        out_ref[at : at + total.shape[0], :] = total


def start(copies):
    for copy in copies:
        copy.start()


def wait(copies):
    for copy in copies:
        copy.wait()


def attn_backward_kernel(
    sizes,
    live_ref,
    up_ref,
    out_ref,
    mixed_ref,
    gf_ref,
    x_ref,
    n1_ref,
    qkv_ref,
    probs_ref,
    att_ref,
    wproj_ref,
    turned_ref,
    gains_ref,
    biases_ref,
    places_ref,
    early_ref,
    sum_ref,
    small_ref,
    own_ref,
    mixed_halo_ref,
    patch_halo_ref,
    band,
    gbp,
    datt,
    dprobs,
    bdq,
    bdk,
    bdo,
    stacked,
    beside,
    dqkv,
    dwq,
    dwp,
    compact,
    dscore,
    dscores,
    dbqkv,
    vecs,
    dwa,
    edge,
    own1,
    *rest,
):
    window, half, width, model, heads, least, pages, devices, share = sizes
    slots = window * window
    size_head = model // heads
    sweep, page, quad = pl.program_id(0), pl.program_id(1), pl.program_id(2)
    quads = width // window // QUAD
    step = page * quads + quad
    live = live_ref[page]
    pairs = heads // 4
    pair = 2 * size_head
    part_rows = model // 2
    lines = model // 128
    cols = 2 * model
    big = Exchange(devices[0], devices[1] // 2, share, rest[:7], rest[7:15])
    early = SmallExchange(big, (rest[15],) + rest[16:21], rest[21:23])
    local, halo_send, halo_recv = rest[23:]
    row = lax.axis_index("rows")
    behind, ahead = lax.rem(row + devices[1] - 1, devices[1]), lax.rem(row + 1, devices[1])
    matrices = [dwa.at[0], dwa.at[1]]
    for ref in (up_ref, out_ref):
        for h in range(ref.shape[1] // cols):
            matrices.append(ref.at[:, pl.ds(h * cols, cols)])
    outer = range(2, len(matrices))

    def fetch(m):
        return [
            pltpu.make_async_copy(
                big.rows_of(matrices[m], z, big.core), own1.at[m - 2, z], local.at[m - 2, z]
            )
            for z in range(big.chips)
        ]

    def mixed_copy():
        return remote(mixed_ref, mixed_halo_ref, halo_send.at[0], halo_recv.at[0], {"rows": ahead})

    def edge_at(j):
        return 0 if j == 0 else width + 8 if j == quads else (j * QUAD * window + half) // 16 * 16

    def patch_copy(p, j):
        cut = pl.ds(edge_at(j), edge_at(j + 1) - edge_at(j))
        k = 1 + p * quads + j
        return remote(
            edge.at[p, :, cut, :], patch_halo_ref.at[p, :, cut, :], halo_send.at[k], halo_recv.at[k], {"rows": ahead}
        )

    def moment(at_sweep, at_step):
        return jnp.logical_and(sweep == at_sweep, step == at_step)

    @pl.when(moment(0, 0))
    def _():
        barrier = pltpu.get_barrier_semaphore()
        peers = [{"rows": big.other}, {"rows": behind}, {"rows": ahead}]
        peers += [{"page": big.page_peer(d)} for d in range(1, big.pages)]
        peers += [big.along(d) for d in range(1, big.chips)]
        for peer in peers:
            pl.semaphore_signal(barrier, inc=1, device_id=peer, device_id_type=MESH)
        pl.semaphore_wait(barrier, len(peers))
        for m in outer:
            big.start_one(m, matrices[m])
            start(fetch(m))
        mixed_copy().start()
        early.mine[...] = early_ref[...]
        for ref in (bdq, bdk, bdo, stacked, beside, gbp, dwq, dwp, dbqkv, dscore, vecs):
            ref[...] = jnp.zeros_like(ref)

    def flush(h):
        for part in range(3):
            rows = slice(part * part_rows, part * part_rows + part_rows)
            dwa[h, :, rows] = dwq[rows, :].T.astype(B16)
        dwa[h, :, 3 * part_rows :] = dwp[:, h * part_rows : (h + 1) * part_rows].astype(B16)
        big.start_one(h, matrices[h])
        for k, part in enumerate((0, 2)):
            total = jnp.sum(dbqkv[part * part_rows : (part + 1) * part_rows, :].T, axis=0, keepdims=True)
            lay_lines(early.mine, lines * (2 + k) + h * (lines // 2), total)
        column = jnp.sum(dbqkv[...], axis=1, keepdims=True)
        weights = turned_ref[h].astype(F32)
        shifts = jnp.sum(weights * column, axis=0, keepdims=True)
        gains = jnp.sum(weights * dwq[...], axis=0, keepdims=True)
        vecs[0:1, :] += gains
        vecs[1:2, :] += shifts
        if h == 1:
            lay_row(vecs, 2, biases_ref, 0, lines)
            total = (vecs[0:1, :] - vecs[2:3, :] * vecs[1:2, :]) / gains_ref[0:1, :]
            lay_lines(early.mine, 0, total)
            lay_lines(early.mine, lines, vecs[1:2, :])
        dscores[h * heads // 2 : (h + 1) * heads // 2] = dscore[...]
        if h == 0:
            for ref in (dwq, dbqkv, dscore):
                ref[...] = jnp.zeros_like(ref)

    def two(m):
        if m >= 2:
            wait(fetch(m))
            big.start_two(m, matrices[m], lambda z: own1.at[m - 2, z])
        else:
            big.start_two(m, matrices[m], lambda z: big.rows_of(matrices[m], z, big.core))

    def table():
        chunks = -(-((2 * window - 1) ** 2) // 128)
        table_sum(places_ref, dscores, early.mine, early.mine.shape[0] - heads * chunks, heads, chunks)
        early.start_one()

    plan = {
        (0, 2): [(two, 2), (two, 3)],
        (0, 4): [(two, 4), (two, 5)],
        (1, 0): [(flush, 0), (big.start_three, 2), (big.start_three, 3)],
        (1, 1): [(two, 0)],
        (1, 4): [(big.start_three, 4), (big.start_three, 5), (big.start_four, 2), (big.start_four, 3)],
        (2, 0): [(flush, 1), (big.start_three, 0)],
        (2, 1): [(two, 1)],
        (2, 5): [(big.start_four, 4), (big.start_four, 5), (big.start_four, 0)],
    }
    for (at_sweep, at_step), acts in plan.items():

        @pl.when(moment(at_sweep, at_step))
        def _():
            for act, m in acts:
                act(m)

    @pl.when(sweep < 2)
    def _():
        for w in range(QUAD):
            gbp[SLOT * w : SLOT * w + slots, :] = gf_ref[slots * w : slots * w + slots, :].astype(B16)
        mine = pl.ds(pl.multiple_of(jnp.minimum(sweep, 1) * part_rows, part_rows), part_rows)
        datt[...] = dot(wproj_ref[mine, :], gbp[...], "NT").astype(B16)

        @pl.when(sweep == 0)
        def _():
            dwp[...] += dot(att_ref[...], gbp[...])

        ratio = size_head**-0.5
        target = dqkv.at[step, jnp.minimum(sweep, 1)]

        def score(w, g):
            low = pair * g
            lanes = slice(SLOT * w, SLOT * w + SLOT)
            for j in range(2):
                at = slice(low + size_head * j, low + size_head * (j + 1))
                cols = slice(SLOT * j, SLOT * j + SLOT)
                bdo[w % 3, at, cols] = datt[at, lanes]
                bdq[w % 3, at, cols] = qkv_ref[0, at, lanes]
                bdk[w % 3, at, cols] = qkv_ref[1, at, lanes]
            values = qkv_ref[2, low : low + pair, SLOT * w : SLOT * w + KEYS]
            dprobs[w % 2, g] = dot(values, bdo[w % 3, low : low + pair, :], "TN")

        def soften(w, g):
            probs = probs_ref[w, g, :KEYS, :].astype(F32)
            term = probs * dprobs[w % 2, g]
            grad = term - probs * jnp.sum(term, axis=0, keepdims=True)
            low_grad = grad.astype(B16)
            beside[w % 2, g, :KEYS, :] = low_grad
            for j in range(2):
                cols = slice(SLOT * j, SLOT * j + SLOT)
                dscore[2 * g + j] += grad[:, cols]
                stacked[w % 2, g, SLOT * j : SLOT * j + KEYS, :] = low_grad[:, cols]

        def attend(w, g):
            low = pair * g
            lanes = slice(SLOT * w, SLOT * w + SLOT)
            rows = slice(low, low + pair)
            got = dot(bdk[w % 3, rows, :], stacked[w % 2, g]) * ratio
            target[low : low + pair, lanes] = got.astype(B16)
            got = dot(bdq[w % 3, rows, :], beside[w % 2, g], "NT") * (1.0 / LOG2E)
            target[part_rows + low : part_rows + low + pair, lanes] = got.astype(B16)
            got = dot(bdo[w % 3, rows, :], probs_ref[w, g], "NT")
            target[2 * part_rows + low : 2 * part_rows + low + pair, lanes] = got.astype(B16)

        for stage in range(QUAD + 2):
            for g in range(pairs):
                if stage < QUAD:
                    score(stage, g)
                if 1 <= stage <= QUAD:
                    soften(stage - 1, g)
                if stage >= 2:
                    attend(stage - 2, g)

        grad = target[...]
        dwq[...] += dot(grad, n1_ref[...])
        wide = grad.astype(F32)
        both = wide[:, :SLOT]
        for w in range(1, QUAD):
            both = both + wide[:, SLOT * w : SLOT * w + SLOT]
        dbqkv[...] += both

    @pl.when(sweep == 2)
    def _():
        dn1 = dot(dqkv[step, 0], turned_ref[0], "TN") + dot(dqkv[step, 1], turned_ref[1], "TN")
        for w in range(QUAD):
            compact[slots * w : slots * w + slots, :] = dn1[SLOT * w : SLOT * w + slots, :]
        grad = compact[...]
        xhat, spread = norm_stats(x_ref[...].astype(F32))
        scaled = grad * gains_ref[0:1, :]
        mean_one = jnp.mean(scaled, axis=-1, keepdims=True)
        mean_two = jnp.mean(scaled * xhat, axis=-1, keepdims=True)
        compact[...] = gf_ref[...] + spread * (scaled - mean_one - xhat * mean_two)
        for w in range(QUAD):
            for r in range(window):
                ref, skip = piece(band, r, quad * QUAD * window, w, window, half)
                at = slots * w + window * r
                ref[skip : skip + window, :] = compact[at : at + window, :]

    for p in range(pages):
        for j in range(quads):

            @pl.when(moment(2, p * quads + j))
            def _():
                cut = slice(edge_at(j), edge_at(j + 1))
                edge[p, :, cut, :] = band[half:, cut, :].astype(B16)
                patch_copy(p, j).start()
                if j == quads - 1:
                    unwrap_band(band, live, half, width, window, least)
                    own_ref[0] = band[:half, :width].astype(B16)

    @pl.when(moment(2, pages * quads - 1))
    def _():
        table()
        big.start_three(1)
        early.start_two()
        for m in outer:
            big.finish(m, sum_ref.at[m])
        big.finish(0, sum_ref.at[0])
        early.start_three()
        big.start_four(1)
        mixed_copy().wait()
        early.finish(small_ref, 0)
        big.finish(1, sum_ref.at[1])
        for p in range(pages):
            for j in range(quads):
                patch_copy(p, j).wait()


def attn_backward(
    live, dwup, dwout, mixed_next, gf, x, n1, qkv, probs, att, weights_in, turned, gains, biases, places, early, shape, heads, least, share
):
    pages, window, width, model = shape
    half = window // 2
    quads = width // window // QUAD
    slots = window * window
    pairs = heads // 4
    part_rows = model // 2
    devices = (lax.axis_size("page"), lax.axis_size("rows"))
    chips = devices[1] // 2
    hidden = dwup.shape[1]
    wide = 2 * model
    cols = wide // devices[0]
    once = pl.Buffered(1)
    whole = lambda a: pl.BlockSpec(a.shape, lambda s, p, j: (0,) * a.ndim, pipeline_mode=once)
    held = lambda dims: pl.BlockSpec(dims, lambda s, p, j: (0,) * len(dims), pipeline_mode=once)
    anywhere = pl.BlockSpec(memory_space=pl.ANY)
    at = lambda p, j: p * quads + j
    last = pages * quads - 1
    both = lambda s, p, j: jnp.where(s < 2, at(p, j), last)
    first = lambda s, p, j: jnp.where(s == 0, at(p, j), last)
    third = lambda s, p, j: jnp.where(s == 2, at(p, j), 0)
    side = lambda s: jnp.minimum(s, 1)
    own_at = lambda s, p, j: (jnp.where(s == 2, p, 0), 0, 0, 0)
    dma = pltpu.SemaphoreType.DMA
    vmem = pltpu.VMEM
    n = 2 + 2 * hidden // wide
    lines = early.shape[0]

    def small_scratch(rows):
        return [
            vmem((rows, 128), F32),
            vmem((rows, 128), F32),
            vmem((rows, 128), F32),
            vmem((devices[0], rows, 128), F32),
            vmem((rows, 128), F32),
            vmem((chips, rows, 128), F32),
            dma((devices[0] + chips,)),
            dma((devices[0] + chips,)),
        ]

    return pl.pallas_call(
        functools.partial(
            attn_backward_kernel, (window, half, width, model, heads, least, pages, devices, share)
        ),
        grid=(3, pages, quads),
        in_specs=[
            pl.BlockSpec(memory_space=pltpu.SMEM),
            anywhere,
            anywhere,
            anywhere,
            pl.BlockSpec((QUAD * slots, model), lambda s, p, j: (at(p, j), 0)),
            pl.BlockSpec((QUAD * slots, model), lambda s, p, j: (third(s, p, j), 0)),
            pl.BlockSpec((QUAD * SLOT, model), lambda s, p, j: (both(s, p, j), 0)),
            pl.BlockSpec((3, part_rows, QUAD * SLOT), lambda s, p, j: (0, side(s), both(s, p, j))),
            pl.BlockSpec((QUAD, pairs, SLOT, 2 * SLOT), lambda s, p, j: (both(s, p, j), side(s), 0, 0)),
            pl.BlockSpec((model, QUAD * SLOT), lambda s, p, j: (0, first(s, p, j))),
            pl.BlockSpec((model, model), lambda s, p, j: (0, 3), pipeline_mode=once),
            whole(turned),
            whole(gains),
            whole(biases),
            whole(places),
            whole(early),
        ],
        out_specs=[
            held((n, share, wide)),
            held((lines, 128)),
            pl.BlockSpec((1, half, width, model), own_at),
            anywhere,
            anywhere,
        ],
        out_shape=[
            jax.ShapeDtypeStruct((n, share, wide), B16),
            jax.ShapeDtypeStruct((lines, 128), F32),
            jax.ShapeDtypeStruct((pages, half, width, model), B16),
            jax.ShapeDtypeStruct((pages, half, width, model), B16),
            jax.ShapeDtypeStruct((pages, half, width + 8, model), B16),
        ],
        scratch_shapes=[
            vmem((window, width + 8, model), F32),
            vmem((QUAD * SLOT, model), B16),
            vmem((part_rows, QUAD * SLOT), B16),
            vmem((2, pairs, KEYS, 2 * SLOT), F32),
            vmem((3, part_rows, 2 * SLOT), B16),
            vmem((3, part_rows, 2 * SLOT), B16),
            vmem((3, part_rows, 2 * SLOT), B16),
            vmem((2, pairs, 2 * SLOT, SLOT), B16),
            vmem((2, pairs, SLOT, 2 * SLOT), B16),
            vmem((pages * quads, 2, 3 * part_rows, QUAD * SLOT), B16),
            vmem((3 * part_rows, model), F32),
            vmem((model, model), F32),
            vmem((QUAD * slots, model), F32),
            vmem((heads // 2, KEYS, SLOT), F32),
            vmem((heads, KEYS, SLOT), F32),
            vmem((3 * part_rows, SLOT), F32),
            vmem((8, model), F32),
            vmem((2, model, wide), B16),
            vmem((pages, half, width + 8, model), B16),
            vmem((n - 2, chips, share, wide), B16),
            vmem((n, chips, share, wide), B16),
            vmem((n, devices[0], chips, share, cols), B16),
            vmem((n, devices[0], chips, share, cols), B16),
            vmem((n, chips, share, cols), B16),
            vmem((n, chips, share, cols), B16),
            vmem((n, share, cols), B16),
            vmem((n, devices[0], share, cols), B16),
            dma((n, chips)),
            dma((n, chips)),
            dma((n, devices[0])),
            dma((n, devices[0])),
            dma((n, chips)),
            dma((n, chips)),
            dma((n, devices[0])),
            dma((n, devices[0])),
        ]
        + small_scratch(lines)
        + [dma((n - 2, chips)), dma((1 + pages * quads,)), dma((1 + pages * quads,))],
        compiler_params=pltpu.CompilerParams(
            vmem_limit_bytes=62 * 2**20, collective_id=0, has_side_effects=True
        ),
    )(live, dwup, dwout, mixed_next, gf, x, n1, qkv, probs, att, weights_in, turned, gains, biases, places, early)


def finish_kernel(
    sizes,
    live_ref,
    sum_ref,
    min_ref,
    fin_ref,
    sin_ref,
    mout_ref,
    fout_ref,
    sout_ref,
    above_ref,
    own_ref,
    edge_ref,
    _,
    mixed_ref,
    patch_ref,
    new_in_ref,
    moment_in_ref,
    square_in_ref,
    new_out_ref,
    moment_out_ref,
    square_out_ref,
    band,
    grad_in,
):
    window, half, width, least = sizes
    step = pl.program_id(0)
    model = band.shape[2]
    part_rows = model // 2
    for s in range(FINISH_STEPS):

        @pl.when(step == s)
        def _():
            if s < 2:
                for h in range(2):
                    for part in range(2):
                        at = part * model + h * part_rows
                        from_at = (2 * s + part) * part_rows
                        grad_in[:, at : at + part_rows] = sum_ref[h, :, from_at : from_at + part_rows].astype(F32)
            else:
                grad_in[...] = sum_ref[s].astype(F32)
            cols = slice(model * (s % 2), model * (s % 2 + 1))
            grad = sum_ref[4 + s // 2, :, cols].astype(F32)
            new, moment, square = adam_update(mout_ref[...], fout_ref[...], sout_ref[...], grad)
            new_out_ref[...], moment_out_ref[...], square_out_ref[...] = new, moment, square
            if s % 2 == 0:
                mixed_ref[...] = above_ref[...]
                band[...] = edge_ref[0].astype(F32)
                unwrap_band(band, live_ref[s // 2], half, width, window, least)
                patch_ref[0] = band[:, :width].astype(B16)
            else:
                patch_ref[0] = own_ref[0]

    new, moment, square = adam_update(min_ref[...], fin_ref[...], sin_ref[...], grad_in[...])
    new_in_ref[...], moment_in_ref[...], square_in_ref[...] = new, moment, square


FINISH_STEPS = 4


def finish(live, sums, master_in, first_in, second_in, master_out, first_out, second_out, above, own, edge, mixed, least):
    pages, window, width, model = mixed.shape
    half = window // 2
    share, wide = master_in.shape
    tall = master_out.shape[0]
    cols = pl.BlockSpec((share, wide // FINISH_STEPS), lambda s: (0, s))
    rows = pl.BlockSpec((tall // FINISH_STEPS, model), lambda s: (s, 0))
    page = lambda s: (s // 2, 0, 0, 0)
    band = (1, half, width, model)
    like = lambda a: jax.ShapeDtypeStruct(a.shape, a.dtype)
    return pl.pallas_call(
        functools.partial(finish_kernel, (window, half, width, least)),
        grid=(FINISH_STEPS,),
        in_specs=[
            pl.BlockSpec(memory_space=pltpu.SMEM),
            pl.BlockSpec(sums.shape, lambda s: (0, 0, 0), pipeline_mode=pl.Buffered(1)),
            cols,
            cols,
            cols,
            rows,
            rows,
            rows,
            pl.BlockSpec(band, page),
            pl.BlockSpec(band, page),
            pl.BlockSpec((1, half, width + 8, model), page),
            pl.BlockSpec(memory_space=pl.ANY),
        ],
        out_specs=[
            pl.BlockSpec(band, page),
            pl.BlockSpec(band, lambda s: (s // 2, s % 2, 0, 0)),
        ]
        + [cols] * 3
        + [rows] * 3,
        out_shape=[like(mixed), like(mixed)] + [like(master_in)] * 3 + [like(master_out)] * 3,
        scratch_shapes=[
            pltpu.VMEM((half, width + 8, model), F32),
            pltpu.VMEM((share, wide // FINISH_STEPS), F32),
        ],
        input_output_aliases={11: 0},
        compiler_params=pltpu.CompilerParams(vmem_limit_bytes=VMEM_LIMIT),
    )(live, sums, master_in, first_in, second_in, master_out, first_out, second_out, above, own, edge, mixed)


def adam_update(master, first, second, grad):
    moment = BETA_ONE * first + (1.0 - BETA_ONE) * grad
    square = BETA_TWO * second + (1.0 - BETA_TWO) * grad * grad
    fix_one = 1.0 - BETA_ONE**STEP
    fix_two = 1.0 - BETA_TWO**STEP
    fresh = master - LEARN_RATE * (
        moment / fix_one / (jnp.sqrt(square / fix_two) + ADAM_EPS) + WEIGHT_DECAY * master
    )
    return (fresh, moment, square)


def shards(
    patches,
    out_grad,
    page_windows,
    region_ids,
    offset_index,
    weights_in,
    weights_out,
    norm_gains,
    biases,
    bias_table,
    master_in,
    master_out,
    first_in,
    second_in,
    first_out,
    second_out,
    first_small,
    second_small,
):
    pages, window, width, model = patches.shape
    half = window // 2
    count = width // window
    least = (count + 1) // 2
    slots = window * window
    table_rows, heads = bias_table.shape
    hidden = weights_out.shape[0]

    labels = region_ids.reshape(pages, window, count, window).transpose(0, 2, 1, 3)
    labels = labels.reshape(pages * count // QUAD, QUAD, slots).astype(F32)
    labels = jnp.pad(labels, ((0, 0), (0, 8 - QUAD), (0, SLOT - slots)), constant_values=-1.0)
    bias_lines = biases.reshape(-1, 128)
    lines = model // 128
    table_lanes = -(-table_rows // 128) * 128
    early_lines = EARLY_UP * lines + hidden // 128 + table_lanes * heads // 128

    x, n1, qkv, probs, att, first, n2, below_grad, turned, places = attn_forward(
        page_windows, patches, out_grad, labels, offset_index, bias_table, weights_in, norm_gains, bias_lines, least
    )
    dwup, dwout, gf, mixed_own, mixed_next, early = mlp(
        page_windows, out_grad, below_grad, n2, first, weights_in, weights_out, norm_gains, bias_lines,
        least, master_in.shape[0], early_lines,
    )
    sums, small, patch_own, above, edge = attn_backward(
        page_windows, dwup, dwout, mixed_next, gf, x, n1, qkv, probs, att, weights_in, turned, norm_gains,
        bias_lines, places, early, patches.shape, heads, least, master_in.shape[0],
    )
    mixed, patch_grad, new_in, moment_in, square_in, new_out, moment_out, square_out = finish(
        page_windows, sums, master_in, first_in, second_in, master_out, first_out, second_out, above, patch_own,
        edge, mixed_own, least,
    )
    small_at = [0, 4, 1, 2, 3, 5, 6, 7]
    table_at = small.shape[0] - table_lanes * heads // 128
    total_table = small[table_at:].reshape(table_lanes // 128, heads, 128).transpose(0, 2, 1)
    total_table = total_table.reshape(table_lanes, heads)[:table_rows]
    head = [small[lines * k : lines * k + lines] for k in small_at] + [small[8 * lines : table_at]]
    total_small = jnp.concatenate([jnp.concatenate(head).reshape(-1), total_table.reshape(-1)])
    small_master = jnp.concatenate([norm_gains.reshape(-1), biases, bias_table.reshape(-1)])
    new_small, moment_small, square_small = adam_update(
        small_master, first_small, second_small, total_small
    )
    return (
        mixed,
        patch_grad,
        new_in,
        moment_in,
        square_in,
        new_out,
        moment_out,
        square_out,
        new_small,
        moment_small,
        square_small,
    )


def solution(mesh):
    return jax.shard_map(
        shards,
        mesh=mesh,
        in_specs=(
            P("page", "rows", None, None),
            P("page", "rows", None, None),
            P("page"),
            P("page", "rows", None),
            P(),
            P(),
            P(),
            P(),
            P(),
            P(),
            P("rows", None),
            P("rows", None),
            P("rows", None),
            P("rows", None),
            P("rows", None),
            P("rows", None),
            P(),
            P(),
        ),
        out_specs=(
            P("page", "rows", None, None),
            P("page", "rows", None, None),
            P("rows", None),
            P("rows", None),
            P("rows", None),
            P("rows", None),
            P("rows", None),
            P("rows", None),
            P(),
            P(),
            P(),
        ),
        check_vma=False,
    )
```

```python
import functools
import math

import jax
import jax.numpy as jnp
from jax import lax
from jax.experimental import pallas as pl
from jax.experimental.pallas import tpu as pltpu
from jax.sharding import PartitionSpec as P

STEP = 10
NORM_EPS = 1e-05
BETA_ONE = 0.9
BETA_TWO = 0.999
LEARN_RATE = 0.04
WEIGHT_DECAY = 0.05
ADAM_EPS = 1e-08
MASK_VALUE = -1000000000.0

F32 = jnp.float32
B16 = jnp.bfloat16
LOG2E = math.log2(math.e)
VMEM_LIMIT = 60 * 2**20

QUAD = 4
SLOT = 128
KEYS = 104


def dot(left, right, form="NN"):
    sides = {
        "NN": ((1,), (0,)),
        "NT": ((1,), (1,)),
        "TN": ((0,), (0,)),
    }[form]
    return lax.dot_general(left, right, (sides, ((), ())), preferred_element_type=F32)


def load_band(band, low_ref, high_ref, live, half, width, window, least, start=0, end=None):
    end = width if end is None else end
    band[:half, start:end] = low_ref[:, start:end].astype(F32)
    band[half:, start:end] = high_ref[:, start:end].astype(F32)
    if end == width:
        band[:, width:] = jnp.zeros((window, band.shape[1] - width, band.shape[2]), F32)
        for count in range(least, width // window + 1):
            at = slice(count * window, count * window + half)
            band[:, at] = jnp.where(live == count, band[:, :half], band[:, at])


def unwrap_band(band, live, half, width, window, least):
    front = band[:, :half]
    for count in range(least, width // window + 1):
        at = slice(count * window, count * window + half)
        front = jnp.where(live == count, band[:, at], front)
    band[:, :half] = front
    edge = least * window // 8 * 8
    shape = (band.shape[0], width - edge, band.shape[2])
    columns = lax.broadcasted_iota(jnp.int32, shape, 1) + edge
    band[:, edge:width] = jnp.where(columns < live * window, band[:, edge:width], 0.0)


def piece(band, row, base, place, window, half):
    start = window * place + half
    aligned = start // 8 * 8
    skip = start - aligned
    size = -(-(skip + window) // 8) * 8
    ref = band.at[row, pl.ds(pl.multiple_of(base, 8) + aligned, size), :]
    return ref, skip


def gather_window(band, base, place, window, half):
    parts = []
    for row in range(window):
        ref, skip = piece(band, row, base, place, window, half)
        parts.append(ref[skip : skip + window, :])
    return parts


def norm_stats(value):
    centre = jnp.mean(value, axis=-1, keepdims=True)
    centered = value - centre
    spread = lax.rsqrt(jnp.mean(centered * centered, axis=-1, keepdims=True) + NORM_EPS)
    return centered * spread, spread


def fold(value):
    rows, cols = value.shape
    return jnp.sum(value.reshape(rows // 8, 8, cols), axis=0)


MESH = pl.DeviceIdType.MESH


def remote(src, dst, send, recv, device):
    return pltpu.make_async_remote_copy(
        src_ref=src, dst_ref=dst, send_sem=send, recv_sem=recv, device_id=device, device_id_type=MESH
    )


def lay_lines(lines_ref, at, row):
    for i in range(row.shape[1] // 128):
        lines_ref[at + i : at + i + 1, :] = row[:, 128 * i : 128 * i + 128]


def lay_row(ref, row, lines_ref, at, count):
    for i in range(count):
        ref[row : row + 1, 128 * i : 128 * i + 128] = lines_ref[at + i : at + i + 1, :]


def attn_forward_kernel(
    sizes,
    live_ref,
    patches_ref,
    grads_ref,
    low_ref,
    label_ref,
    off_ref,
    tab_ref,
    wqkv_ref,
    wproj_ref,
    gains_ref,
    biases_ref,
    x_ref,
    n1_ref,
    qkv_ref,
    probs_ref,
    att_ref,
    first_ref,
    n2_ref,
    grad_halo_ref,
    turned_ref,
    places_ref,
    halo,
    send,
    recv,
    band,
    bias,
    scores,
    bdq,
    bdv,
    stacked,
    xs,
    ns,
    vecs,
    column,
    square,
    flat,
    marks,
):
    window, half, width, model, heads, least, pages, rows_count = sizes
    slots = window * window
    size_head = model // heads
    page, quad = pl.program_id(0), pl.program_id(1)
    live = live_ref[page]
    pairs = heads // 2
    part_rows = model // 2
    lines = model // 128
    row = lax.axis_index("rows")
    behind, ahead = lax.rem(row + rows_count - 1, rows_count), lax.rem(row + 1, rows_count)

    cut = -(-(QUAD * window + half) // 16) * 16

    def halo_copy(p, k):
        at = (pl.ds(0, cut), pl.ds(cut, width - cut))[k]
        return remote(
            patches_ref.at[p, pl.ds(0, half), at],
            halo.at[p, :, at],
            send.at[pages * (1 + k) + p],
            recv.at[pages * (1 + k) + p],
            {"rows": behind},
        )

    def grad_copy(p):
        return remote(
            grads_ref.at[p, pl.ds(0, half)],
            grad_halo_ref.at[p],
            send.at[p],
            recv.at[p],
            {"rows": behind},
        )

    @pl.when(jnp.logical_and(page == 0, quad == 0))
    def _():
        barrier = pltpu.get_barrier_semaphore()
        for neighbour in (behind, ahead):
            pl.semaphore_signal(barrier, inc=1, device_id={"rows": neighbour}, device_id_type=MESH)
        pl.semaphore_wait(barrier, 2)
        halo_copy(0, 0).start()
        vecs[...] = jnp.zeros_like(vecs)
        vecs[0:1, :] = gains_ref[0:1, :]
        lay_row(vecs, 1, biases_ref, 0, lines)
        lay_row(vecs, 2, biases_ref, 3 * lines, lines)
        vecs[3:4, :] = gains_ref[1:2, :]
        lay_row(vecs, 4, biases_ref, 4 * lines, lines)
        column[...] = jnp.zeros_like(column)
        for h in range(2):
            for part in range(3):
                rows = slice(part * part_rows, part * part_rows + part_rows)
                cols = slice(part * model + h * part_rows, part * model + (h + 1) * part_rows)
                turned_ref[h, rows, :] = wqkv_ref[:, cols].T
                if part != 1:
                    for i in range(part_rows // 128):
                        line = lines * (1 + part // 2) + h * (part_rows // 128) + i
                        spread = jnp.broadcast_to(biases_ref[line : line + 1, :], (128, 128))
                        at = part * part_rows + 128 * i
                        column[h, at : at + 128, :] = spread.T
        halo_copy(0, 1).start()
        square[...] = jnp.full_like(square, -1)
        square[:slots, :slots] = off_ref[...]
        places = square[...].T[:KEYS]
        places_ref[...] = places
        off = jnp.maximum(places, 0)
        flat[...] = jnp.zeros_like(flat)
        flat[:, : tab_ref.shape[1]] = tab_ref[...] * LOG2E
        low, high = jnp.bitwise_and(off, 127), jnp.right_shift(off, 7)
        for h in range(heads):
            got = jnp.zeros((KEYS, SLOT), F32)
            for c in range(flat.shape[1] // 128):
                source = jnp.broadcast_to(flat[h : h + 1, 128 * c : 128 * c + 128], (KEYS, SLOT))
                picked = jnp.take_along_axis(source, low, axis=1, mode="promise_in_bounds")
                got = jnp.where(high == c, picked, got)
            bias[h] = got
        bdq[...] = jnp.zeros_like(bdq)
        bdv[...] = jnp.zeros_like(bdv)
        stacked[...] = jnp.zeros_like(stacked)

    for p in range(pages):

        @pl.when(jnp.logical_and(page == p, quad == 0))
        def _():
            halo_copy(p, 0).wait()
            load_band(band, low_ref.at[0], halo.at[p], live, half, width, window, least, 0, cut)

        @pl.when(jnp.logical_and(page == p, quad == 1))
        def _():
            halo_copy(p, 1).wait()
            if p + 1 < pages:
                for k in range(2):
                    halo_copy(p + 1, k).start()
            load_band(band, low_ref.at[0], halo.at[p], live, half, width, window, least, cut)

    @pl.when(jnp.logical_and(page == (pages - 1) // 2, quad == 2))
    def _():
        for p in range(pages):
            grad_copy(p).start()

    @pl.when(jnp.logical_and(page == pages - 1, quad == pl.num_programs(1) - 1))
    def _():
        for p in range(pages):
            grad_copy(p).wait()

    base = quad * (QUAD * window)
    for w in range(QUAD):
        for r, part in enumerate(gather_window(band, base, w, window, half)):
            at = slots * w + window * r
            xs[at : at + window, :] = part
    x = xs[...]
    x_ref[...] = x.astype(B16)
    xhat, _ = norm_stats(x)
    ns[...] = xhat * vecs[0:1, :] + vecs[1:2, :]
    for w in range(QUAD):
        n1_ref[SLOT * w : SLOT * w + slots, :] = ns[slots * w : slots * w + slots, :].astype(B16)
        n1_ref[SLOT * w + slots : SLOT * w + SLOT, :] = jnp.zeros((SLOT - slots, model), B16)
    scale = size_head**-0.5 * LOG2E
    n1 = n1_ref[...]
    for h in range(2):
        got = dot(turned_ref[h], n1, "NT") + column[h, :, 0:1]
        at = slice(h * part_rows, h * part_rows + part_rows)
        qkv_ref[0, at, :] = (got[:part_rows] * scale).astype(B16)
        qkv_ref[1, at, :] = got[part_rows : 2 * part_rows].astype(B16)
        qkv_ref[2, at, :] = got[2 * part_rows :].astype(B16)

    sames = []
    lane = lax.broadcasted_iota(jnp.int32, (1, SLOT), 1)
    for j in range(width // window // QUAD):

        @pl.when(quad == j)
        def _():
            at = QUAD * window * j
            marks[:, : QUAD * window] = label_ref[0, :, at : at + QUAD * window].astype(F32)

    for w in range(QUAD):
        label = jnp.full((1, SLOT), -1.0, F32)
        for r in range(window):
            turned = pltpu.roll(marks[r : r + 1, :], (window * (r - w)) % SLOT, 1)
            here = jnp.logical_and(lane >= window * r, lane < window * (r + 1))
            label = jnp.where(here, turned, label)
        spread = jnp.broadcast_to(label, (SLOT, SLOT))
        sames.append((spread == spread.T)[:KEYS])
    pair = 2 * size_head

    def score(w, g):
        low = pair * g
        lanes = slice(SLOT * w, SLOT * w + SLOT)
        for j in range(2):
            at = slice(low + size_head * j, low + size_head * (j + 1))
            cols = slice(SLOT * j, SLOT * j + SLOT)
            bdq[w % 2, at, cols] = qkv_ref[0, at, lanes]
            bdv[w % 3, at, cols] = qkv_ref[2, at, lanes]
        keys = qkv_ref[1, low : low + pair, SLOT * w : SLOT * w + KEYS]
        scores[w % 2, g] = dot(keys, bdq[w % 2, low : low + pair, :], "TN")

    def soften(w, g):
        for j in range(2):
            cols = slice(SLOT * j, SLOT * j + SLOT)
            s = jnp.where(sames[w], scores[w % 2, g, :, cols] + bias[2 * g + j], MASK_VALUE)
            s = jnp.exp2(s - jnp.max(s, axis=0, keepdims=True))
            low_probs = (s * (1.0 / jnp.sum(s, axis=0, keepdims=True))).astype(B16)
            probs_ref[w, g, :KEYS, cols] = low_probs
            probs_ref[w, g, KEYS:, cols] = jnp.zeros((SLOT - KEYS, SLOT), B16)
            stacked[w % 2, g, SLOT * j : SLOT * j + KEYS, :] = low_probs

    def attend(w, g):
        low = pair * g
        got = dot(bdv[w % 3, low : low + pair, :], stacked[w % 2, g])
        att_ref[low : low + pair, SLOT * w : SLOT * w + SLOT] = got.astype(B16)

    for step in range(QUAD + 2):
        for g in range(pairs):
            if step < QUAD:
                score(step, g)
            if 1 <= step <= QUAD:
                soften(step - 1, g)
            if step >= 2:
                attend(step - 2, g)

    branch = dot(att_ref[...], wproj_ref[...], "TN")
    for w in range(QUAD):
        rows = slice(slots * w, slots * w + slots)
        first_ref[rows, :] = xs[rows, :] + branch[SLOT * w : SLOT * w + slots, :] + vecs[2:3, :]
    xhat, _ = norm_stats(first_ref[...])
    n2_ref[...] = (xhat * vecs[3:4, :] + vecs[4:5, :]).astype(B16)


def attn_forward(live, patches, out_grad, labels, off, tab, weights_in, gains, biases, least):
    pages, window, width, model = patches.shape
    half = window // 2
    heads, table_rows = tab.shape
    table_lanes = -(-table_rows // 128) * 128
    quads = width // window // QUAD
    tokens = pages * window * width
    slots = window * window
    padded = pages * quads * QUAD * SLOT
    steps = (pages, quads)
    whole = lambda a: pl.BlockSpec(a.shape, lambda p, j: (0,) * a.ndim, pipeline_mode=pl.Buffered(1))
    at = lambda p, j: p * quads + j
    return pl.pallas_call(
        functools.partial(
            attn_forward_kernel,
            (window, half, width, model, heads, least, pages, lax.axis_size("rows")),
        ),
        grid=steps,
        in_specs=[
            pl.BlockSpec(memory_space=pltpu.SMEM),
            pl.BlockSpec(memory_space=pl.ANY),
            pl.BlockSpec(memory_space=pl.ANY),
            pl.BlockSpec((1, half, width, model), lambda p, j: (p, 1, 0, 0)),
            pl.BlockSpec((1, window, width), lambda p, j: (p, 0, 0)),
            whole(off),
            whole(tab),
            pl.BlockSpec((model, 3 * model), lambda p, j: (0, 0), pipeline_mode=pl.Buffered(1)),
            pl.BlockSpec((model, model), lambda p, j: (0, 3), pipeline_mode=pl.Buffered(1)),
            whole(gains),
            whole(biases),
        ],
        out_specs=[
            pl.BlockSpec((QUAD * slots, model), lambda p, j: (at(p, j), 0)),
            pl.BlockSpec((QUAD * SLOT, model), lambda p, j: (at(p, j), 0)),
            pl.BlockSpec((3, model, QUAD * SLOT), lambda p, j: (0, 0, at(p, j))),
            pl.BlockSpec((QUAD, heads // 2, SLOT, 2 * SLOT), lambda p, j: (at(p, j), 0, 0, 0)),
            pl.BlockSpec((model, QUAD * SLOT), lambda p, j: (0, at(p, j))),
            pl.BlockSpec((QUAD * slots, model), lambda p, j: (at(p, j), 0)),
            pl.BlockSpec((QUAD * slots, model), lambda p, j: (at(p, j), 0)),
            pl.BlockSpec(memory_space=pl.ANY),
            pl.BlockSpec((2, 3 * model // 2, model), lambda p, j: (0, 0, 0), pipeline_mode=pl.Buffered(1)),
            pl.BlockSpec((KEYS, SLOT), lambda p, j: (0, 0)),
        ],
        out_shape=[
            jax.ShapeDtypeStruct((tokens, model), B16),
            jax.ShapeDtypeStruct((padded, model), B16),
            jax.ShapeDtypeStruct((3, model, padded), B16),
            jax.ShapeDtypeStruct((pages * quads * QUAD, heads // 2, SLOT, 2 * SLOT), B16),
            jax.ShapeDtypeStruct((model, padded), B16),
            jax.ShapeDtypeStruct((tokens, model), F32),
            jax.ShapeDtypeStruct((tokens, model), B16),
            jax.ShapeDtypeStruct((pages, half, width, model), B16),
            jax.ShapeDtypeStruct((2, 3 * model // 2, model), B16),
            jax.ShapeDtypeStruct((KEYS, SLOT), jnp.int32),
        ],
        scratch_shapes=[
            pltpu.VMEM((pages, half, width, model), B16),
            pltpu.SemaphoreType.DMA((3 * pages,)),
            pltpu.SemaphoreType.DMA((3 * pages,)),
            pltpu.VMEM((window, width + 8, model), F32),
            pltpu.VMEM((heads, KEYS, SLOT), F32),
            pltpu.VMEM((2, heads // 2, KEYS, 2 * SLOT), F32),
            pltpu.VMEM((2, model, 2 * SLOT), B16),
            pltpu.VMEM((3, model, 2 * SLOT), B16),
            pltpu.VMEM((2, heads // 2, 2 * SLOT, SLOT), B16),
            pltpu.VMEM((QUAD * slots, model), F32),
            pltpu.VMEM((QUAD * slots, model), F32),
            pltpu.VMEM((8, model), F32),
            pltpu.VMEM((2, 3 * model // 2, 128), F32),
            pltpu.VMEM((SLOT, SLOT), jnp.int32),
            pltpu.VMEM((heads, table_lanes), F32),
            pltpu.VMEM((window, SLOT), F32),
        ],
        compiler_params=pltpu.CompilerParams(
            vmem_limit_bytes=VMEM_LIMIT, collective_id=1, has_side_effects=True
        ),
    )(live, patches, out_grad, patches, labels, off, tab, weights_in, weights_in, gains, biases)


MLP_COLS = 1024
MLP_CHUNKS = 2
MLP_ROWS = 480
EARLY_UP = 8


def mlp_kernel(
    sizes,
    live_ref,
    low_ref,
    high_ref,
    n2_ref,
    first_ref,
    wup_ref,
    wout_ref,
    gains_ref,
    biases_ref,
    dwup_ref,
    dwout_ref,
    gf_ref,
    own_ref,
    next_ref,
    early_ref,
    bup,
    vecs,
    sums,
    band,
    cot,
    res,
    dn2,
    act_all,
    pre_all,
):
    window, half, width, model, least, share = sizes
    pages = low_ref.shape[0]
    slots = window * window
    count = width // window
    quads = count // QUAD
    chunk = pl.program_id(0)
    tokens = n2_ref.shape[0]
    cols = wup_ref.shape[1]
    lines = model // 128

    for c in range(MLP_CHUNKS):

        @pl.when(chunk == c)
        def _():
            lay_row(bup, 0, biases_ref, 6 * lines + c * (cols // 128), cols // 128)

    @pl.when(chunk == 0)
    def _():
        early_ref[...] = jnp.zeros_like(early_ref)
        vecs[0:1, :] = gains_ref[1:2, :]
        lay_row(vecs, 1, biases_ref, 5 * lines, lines)
        for page in range(pages):
            live = live_ref[page]
            load_band(band, low_ref.at[page], high_ref.at[page], live, half, width, window, least)

            def body(j, carry):
                for w in range(QUAD):
                    alive = jnp.where(j * QUAD + w < live, 1.0, 0.0)
                    for r, part in enumerate(gather_window(band, j * QUAD * window, w, window, half)):
                        at = slots * w + window * r
                        gf_ref[at : at + window, :] = part * alive
                rows = pl.ds(pl.multiple_of((page * quads + j) * QUAD * slots, 16), QUAD * slots)
                cot[rows, :] = gf_ref[: QUAD * slots, :].astype(B16)
                return carry

            lax.fori_loop(0, quads, body, 0)

    def body(i, total):
        rows = pl.ds(pl.multiple_of(i * MLP_ROWS, 16), MLP_ROWS)
        grad = cot[rows, :]
        pre = dot(n2_ref[rows, :], wup_ref[...]) + bup[0:1, :]
        grad_act = dot(grad, wout_ref[...], "NT")
        share = 0.5 * (1.0 + lax.erf(pre * 0.5**0.5))
        act = (pre * share).astype(B16)
        slope = share + pre * (jnp.exp2((-0.5 * LOG2E) * pre * pre) * (2.0 * math.pi) ** -0.5)
        grad_pre = (grad_act * slope).astype(B16)
        act_all[rows, :] = act
        pre_all[rows, :] = grad_pre
        up = dot(act, wout_ref[...])
        down = dot(grad_pre, wup_ref[...], "NT")

        res[rows, :] = jnp.where(chunk == 0, 0.0, res[rows, :]) + up
        dn2[rows, :] = jnp.where(chunk == 0, 0.0, dn2[rows, :]) + down
        return total + fold(grad_pre.astype(F32))

    total = lax.fori_loop(0, tokens // MLP_ROWS, body, jnp.zeros((8, cols), F32))
    total = jnp.sum(total, axis=0, keepdims=True)
    for c in range(MLP_CHUNKS):

        @pl.when(chunk == c)
        def _():
            lay_lines(early_ref, EARLY_UP * lines + c * (cols // 128), total)

    grad_out = dot(act_all[...], cot[...], "TN").astype(B16)
    for s in range(dwout_ref.shape[0] // share):
        for a in range(dwout_ref.shape[1] // model):
            at = (s * (dwout_ref.shape[1] // model) + a) * share
            dwout_ref[share * s : share * s + share, model * a : model * a + model] = grad_out[at : at + share, :]
    dwup_ref[...] = dot(n2_ref[...], pre_all[...], "TN").astype(B16)

    @pl.when(chunk == pl.num_programs(0) - 1)
    def _():
        sums[...] = jnp.zeros_like(sums)
        for page in range(pages):
            live = live_ref[page]

            def body(j, carry):
                at = pl.multiple_of((page * quads + j) * QUAD * slots, 16)
                rows = pl.ds(at, QUAD * slots)
                first = first_ref[rows, :]
                res[rows, :] += first + vecs[1:2, :]
                xhat, spread = norm_stats(first)
                grad = dn2[rows, :]
                given = cot[rows, :].astype(F32)
                scaled = grad * vecs[0:1, :]
                mean_one = jnp.mean(scaled, axis=-1, keepdims=True)
                mean_two = jnp.mean(scaled * xhat, axis=-1, keepdims=True)
                whole = given + spread * (scaled - mean_one - xhat * mean_two)
                gf_ref[rows, :] = whole
                sums[0:8, :] += fold(grad * xhat)
                sums[8:16, :] += fold(whole)
                sums[16:24, :] += fold(grad)
                sums[24:32, :] += fold(given)
                for w in range(QUAD):
                    for r in range(window):
                        ref, skip = piece(band, r, j * QUAD * window, w, window, half)
                        ref[skip : skip + window, :] = res[
                            pl.ds(at + slots * w // 8 * 8, slots + 4), :
                        ][slots * w % 8 + window * r : slots * w % 8 + window * r + window, :]
                return carry

            lax.fori_loop(0, quads, body, 0)
            unwrap_band(band, live, half, width, window, least)
            own_ref[page] = band[:half, :width].astype(B16)
            next_ref[page] = band[half:, :width].astype(B16)
        for k, place in enumerate((1, 5, 6, 7)):
            lay_lines(early_ref, place * lines, jnp.sum(sums[8 * k : 8 * k + 8, :], axis=0, keepdims=True))


def mlp(live, out_grad, halo, n2, first, weights_in, weights_out, gains, biases, least, share, lines):
    pages, window, width, model = out_grad.shape
    half = window // 2
    tokens = n2.shape[0]
    hidden = weights_out.shape[0]
    skip = (weights_in.shape[1] - hidden) // MLP_COLS
    once = pl.Buffered(1)
    whole = lambda a: pl.BlockSpec(a.shape, lambda c: (0,) * a.ndim, pipeline_mode=once)
    band_block = (pages, half, width, model)
    return pl.pallas_call(
        functools.partial(mlp_kernel, (window, half, width, model, least, share)),
        grid=(hidden // MLP_COLS,),
        in_specs=[
            pl.BlockSpec(memory_space=pltpu.SMEM),
            pl.BlockSpec(band_block, lambda c: (0, 1, 0, 0), pipeline_mode=once),
            pl.BlockSpec(band_block, lambda c: (0, 0, 0, 0), pipeline_mode=once),
            whole(n2),
            whole(first),
            pl.BlockSpec((model, MLP_COLS), lambda c: (0, c + skip)),
            pl.BlockSpec((MLP_COLS, model), lambda c: (c, 0)),
            whole(gains),
            whole(biases),
        ],
        out_specs=[
            pl.BlockSpec((model, MLP_COLS), lambda c: (0, c)),
            pl.BlockSpec((model * MLP_COLS // hidden, hidden), lambda c: (c, 0)),
            pl.BlockSpec((tokens, model), lambda c: (0, 0), pipeline_mode=once),
            pl.BlockSpec(band_block, lambda c: (0, 1, 0, 0), pipeline_mode=once),
            pl.BlockSpec(band_block, lambda c: (0, 0, 0, 0), pipeline_mode=once),
            pl.BlockSpec((lines, 128), lambda c: (0, 0)),
        ],
        out_shape=[
            jax.ShapeDtypeStruct((model, hidden), B16),
            jax.ShapeDtypeStruct((model, hidden), B16),
            jax.ShapeDtypeStruct((tokens, model), F32),
            jax.ShapeDtypeStruct(out_grad.shape, B16),
            jax.ShapeDtypeStruct(band_block, B16),
            jax.ShapeDtypeStruct((lines, 128), F32),
        ],
        scratch_shapes=[
            pltpu.VMEM((8, MLP_COLS), F32),
            pltpu.VMEM((8, model), F32),
            pltpu.VMEM((32, model), F32),
            pltpu.VMEM((window, width + 8, model), F32),
            pltpu.VMEM((tokens, model), B16),
            pltpu.VMEM((tokens, model), F32),
            pltpu.VMEM((tokens, model), F32),
            pltpu.VMEM((tokens, MLP_COLS), B16),
            pltpu.VMEM((tokens, MLP_COLS), B16),
        ],
        compiler_params=pltpu.CompilerParams(vmem_limit_bytes=VMEM_LIMIT),
    )(live, out_grad, halo, n2, first, weights_in, weights_out, gains, biases)


def table_sum(off_ref, grad_ref, out_ref, at, heads, chunks):
    rows = 128 * chunks
    keys = grad_ref.shape[1]
    names = lax.broadcasted_iota(jnp.int32, (rows, SLOT), 0)
    total = jnp.zeros((3 * heads, rows), F32)
    grad = jnp.swapaxes(grad_ref[...], 0, 1)
    for k in range(0, keys, 8):
        hot = jnp.concatenate(
            [jnp.where(names == off_ref[i : i + 1, :], 1.0, 0.0).astype(B16) for i in range(k, k + 8)], axis=1
        )
        value = jnp.concatenate([grad[i] for i in range(k, k + 8)], axis=1)
        high = value.astype(B16)
        rest = value - high.astype(F32)
        middle = rest.astype(B16)
        low = (rest - middle.astype(F32)).astype(B16)
        total += dot(jnp.concatenate([high, middle, low], axis=0), hot, "NT")
    total = total[:heads] + total[heads : 2 * heads] + total[2 * heads :]
    for c in range(chunks):
        out_ref[at + heads * c : at + heads * c + heads, :] = total[:, 128 * c : 128 * c + 128]


class Exchange:
    def __init__(self, pages, chips, share, bufs, sems):
        self.pages, self.chips, self.share = pages, chips, share
        self.rec1, self.s1, self.rec2, self.s2, self.rec3, self.s3, self.rec4 = bufs
        self.send1, self.recv1, self.send2, self.recv2, self.send3, self.recv3, self.send4, self.recv4 = sems
        self.page, row = lax.axis_index("page"), lax.axis_index("rows")
        self.chip, self.core = row // 2, row % 2
        self.other = 2 * self.chip + 1 - self.core
        self.cols = self.s3.shape[-1]

    def page_peer(self, d):
        return lax.rem(self.page + d, self.pages)

    def chip_peer(self, d):
        return lax.rem(self.chip + d, self.chips)

    def along(self, d):
        return {"rows": 2 * self.chip_peer(d) + self.core}

    def rows_of(self, ref, z, c):
        return ref.at[pl.ds(pl.multiple_of((2 * z + c) * self.share, 16), self.share), :]

    def one(self, m, grad):
        return [
            remote(
                self.rows_of(grad, z, 1 - self.core),
                self.rec1.at[m, z],
                self.send1.at[m, z],
                self.recv1.at[m, z],
                {"rows": self.other},
            )
            for z in range(self.chips)
        ]

    def two(self, m):
        return [
            remote(
                self.s1.at[m, self.page_peer(d)],
                self.rec2.at[m, self.page],
                self.send2.at[m, d],
                self.recv2.at[m, d],
                {"page": self.page_peer(d)},
            )
            for d in range(1, self.pages)
        ]

    def three(self, m):
        return [
            remote(
                self.s2.at[m, self.chip_peer(d)],
                self.rec3.at[m, self.chip],
                self.send3.at[m, d],
                self.recv3.at[m, d],
                self.along(d),
            )
            for d in range(1, self.chips)
        ]

    def four(self, m):
        return [
            remote(
                self.s3.at[m],
                self.rec4.at[m, self.page],
                self.send4.at[m, d],
                self.recv4.at[m, d],
                {"page": self.page_peer(d)},
            )
            for d in range(1, self.pages)
        ]

    def start_one(self, m, grad):
        start(self.one(m, grad))

    def start_two(self, m, grad, own):
        wait(self.one(m, grad))
        for q in range(self.pages):
            at = slice(self.cols * q, self.cols * q + self.cols)
            for z in range(self.chips):
                self.s1[m, q, z] = (own(z)[:, at].astype(F32) + self.rec1[m, z, :, at].astype(F32)).astype(B16)
        start(self.two(m))
        self.rec2[m, self.page] = self.s1[m, self.page]

    def start_three(self, m):
        wait(self.two(m))
        total = self.rec2[m, 0].astype(F32)
        for q in range(1, self.pages):
            total = total + self.rec2[m, q].astype(F32)
        self.s2[m] = total.astype(B16)
        start(self.three(m))
        self.rec3[m, self.chip] = self.s2[m, self.chip]

    def start_four(self, m):
        wait(self.three(m))
        total = self.rec3[m, 0].astype(F32)
        for z in range(1, self.chips):
            total = total + self.rec3[m, z].astype(F32)
        self.s3[m] = total.astype(B16)
        start(self.four(m))
        self.rec4[m, self.page] = self.s3[m]

    def finish(self, m, out_ref):
        wait(self.four(m))
        for q in range(self.pages):
            out_ref[:, self.cols * q : self.cols * q + self.cols] = self.rec4[m, q]


class SmallExchange:
    def __init__(self, big, bufs, sems):
        self.big = big
        self.mine, self.one_in, self.two_out, self.two_in, self.three_out, self.three_in = bufs
        self.send, self.recv = sems

    def one(self):
        return [remote(self.mine, self.one_in, self.send.at[0], self.recv.at[0], {"rows": self.big.other})]

    def two(self):
        big = self.big
        return [
            remote(
                self.two_out,
                self.two_in.at[big.page],
                self.send.at[d],
                self.recv.at[d],
                {"page": big.page_peer(d)},
            )
            for d in range(1, big.pages)
        ]

    def three(self):
        big = self.big
        return [
            remote(
                self.three_out,
                self.three_in.at[big.chip],
                self.send.at[big.pages + d],
                self.recv.at[big.pages + d],
                big.along(d),
            )
            for d in range(1, big.chips)
        ]

    def start_one(self):
        start(self.one())

    def start_two(self):
        wait(self.one())
        total = self.mine[...] + self.one_in[...]
        self.two_out[...] = total
        start(self.two())
        self.two_in[self.big.page] = total

    def start_three(self):
        wait(self.two())
        total = self.two_in[0]
        for q in range(1, self.big.pages):
            total = total + self.two_in[q]
        self.three_out[...] = total
        start(self.three())
        self.three_in[self.big.chip] = total

    def finish(self, out_ref, at):
        wait(self.three())
        total = self.three_in[0]
        for z in range(1, self.big.chips):
            total = total + self.three_in[z]
        out_ref[at : at + total.shape[0], :] = total


def start(copies):
    for copy in copies:
        copy.start()


def wait(copies):
    for copy in copies:
        copy.wait()


def attn_backward_kernel(
    sizes,
    live_ref,
    up_ref,
    out_ref,
    mixed_ref,
    gf_ref,
    x_ref,
    n1_ref,
    qkv_ref,
    probs_ref,
    att_ref,
    wproj_ref,
    turned_ref,
    gains_ref,
    biases_ref,
    places_ref,
    early_ref,
    sum_ref,
    small_ref,
    table_ref,
    own_ref,
    mixed_halo_ref,
    patch_halo_ref,
    band,
    gbp,
    datt,
    dprobs,
    bdq,
    bdk,
    bdo,
    stacked,
    beside,
    dqkv,
    dwq,
    dwp,
    compact,
    dscore,
    dscores,
    dbqkv,
    vecs,
    dwa,
    edge,
    own1,
    *rest,
):
    window, half, width, model, heads, least, pages, devices, share = sizes
    slots = window * window
    size_head = model // heads
    sweep, page, quad = pl.program_id(0), pl.program_id(1), pl.program_id(2)
    quads = width // window // QUAD
    step = page * quads + quad
    live = live_ref[page]
    pairs = heads // 4
    pair = 2 * size_head
    part_rows = model // 2
    lines = model // 128
    cols = 2 * model
    big = Exchange(devices[0], devices[1] // 2, share, rest[:7], rest[7:15])
    early = SmallExchange(big, (rest[15],) + rest[16:21], rest[21:23])
    local, halo_send, halo_recv = rest[23:]
    row = lax.axis_index("rows")
    behind, ahead = lax.rem(row + devices[1] - 1, devices[1]), lax.rem(row + 1, devices[1])
    matrices = [dwa.at[0], dwa.at[1]]
    for ref in (up_ref, out_ref):
        for h in range(ref.shape[1] // cols):
            matrices.append(ref.at[:, pl.ds(h * cols, cols)])
    outer = range(2, len(matrices))

    def fetch(m):
        return [
            pltpu.make_async_copy(
                big.rows_of(matrices[m], z, big.core), own1.at[m - 2, z], local.at[m - 2, z]
            )
            for z in range(big.chips)
        ]

    def mixed_copy():
        return remote(mixed_ref, mixed_halo_ref, halo_send.at[0], halo_recv.at[0], {"rows": ahead})

    def edge_at(j):
        return 0 if j == 0 else width + 8 if j == quads else (j * QUAD * window + half) // 16 * 16

    def patch_copy(p, j):
        cut = pl.ds(edge_at(j), edge_at(j + 1) - edge_at(j))
        k = 1 + p * quads + j
        return remote(
            edge.at[p, :, cut, :], patch_halo_ref.at[p, :, cut, :], halo_send.at[k], halo_recv.at[k], {"rows": ahead}
        )

    def moment(at_sweep, at_step):
        return jnp.logical_and(sweep == at_sweep, step == at_step)

    @pl.when(moment(0, 0))
    def _():
        barrier = pltpu.get_barrier_semaphore()
        peers = [{"rows": big.other}, {"rows": behind}, {"rows": ahead}]
        peers += [{"page": big.page_peer(d)} for d in range(1, big.pages)]
        peers += [big.along(d) for d in range(1, big.chips)]
        for peer in peers:
            pl.semaphore_signal(barrier, inc=1, device_id=peer, device_id_type=MESH)
        pl.semaphore_wait(barrier, len(peers))
        for m in outer:
            big.start_one(m, matrices[m])
            start(fetch(m))
        mixed_copy().start()
        early.mine[...] = early_ref[...]
        for ref in (bdq, bdk, bdo, stacked, beside, gbp, dwq, dwp, dbqkv, dscore, vecs):
            ref[...] = jnp.zeros_like(ref)

    def flush(h):
        for part in range(3):
            rows = slice(part * part_rows, part * part_rows + part_rows)
            dwa[h, :, rows] = dwq[rows, :].T.astype(B16)
        dwa[h, :, 3 * part_rows :] = dwp[:, h * part_rows : (h + 1) * part_rows].astype(B16)
        big.start_one(h, matrices[h])
        for k, part in enumerate((0, 2)):
            total = jnp.sum(dbqkv[part * part_rows : (part + 1) * part_rows, :].T, axis=0, keepdims=True)
            lay_lines(early.mine, lines * (3 + k) + h * (lines // 2), total)
        column = jnp.sum(dbqkv[...], axis=1, keepdims=True)
        weights = turned_ref[h].astype(F32)
        shifts = jnp.sum(weights * column, axis=0, keepdims=True)
        gains = jnp.sum(weights * dwq[...], axis=0, keepdims=True)
        vecs[0:1, :] += gains
        vecs[1:2, :] += shifts
        if h == 1:
            lay_row(vecs, 2, biases_ref, 0, lines)
            total = (vecs[0:1, :] - vecs[2:3, :] * vecs[1:2, :]) / gains_ref[0:1, :]
            lay_lines(early.mine, 0, total)
            lay_lines(early.mine, 2 * lines, vecs[1:2, :])
        dscores[h * heads // 2 : (h + 1) * heads // 2] = dscore[...]
        if h == 0:
            for ref in (dwq, dbqkv, dscore):
                ref[...] = jnp.zeros_like(ref)

    def two(m):
        if m >= 2:
            wait(fetch(m))
            big.start_two(m, matrices[m], lambda z: own1.at[m - 2, z])
        else:
            big.start_two(m, matrices[m], lambda z: big.rows_of(matrices[m], z, big.core))

    def table():
        chunks = -(-((2 * window - 1) ** 2) // 128)
        table_sum(places_ref, dscores, early.mine, early.mine.shape[0] - heads * chunks, heads, chunks)
        early.start_one()

    plan = {
        (0, 2): [(two, 2), (two, 3)],
        (0, 4): [(two, 4), (two, 5)],
        (1, 0): [(flush, 0), (big.start_three, 2), (big.start_three, 3)],
        (1, 1): [(two, 0)],
        (1, 4): [(big.start_three, 4), (big.start_three, 5), (big.start_four, 2), (big.start_four, 3)],
        (2, 0): [(flush, 1), (big.start_three, 0)],
        (2, 1): [(two, 1)],
        (2, 5): [(big.start_four, 4), (big.start_four, 5), (big.start_four, 0)],
    }
    for (at_sweep, at_step), acts in plan.items():

        @pl.when(moment(at_sweep, at_step))
        def _():
            for act, m in acts:
                act(m)

    @pl.when(sweep < 2)
    def _():
        for w in range(QUAD):
            gbp[SLOT * w : SLOT * w + slots, :] = gf_ref[slots * w : slots * w + slots, :].astype(B16)
        mine = pl.ds(pl.multiple_of(jnp.minimum(sweep, 1) * part_rows, part_rows), part_rows)
        datt[...] = dot(wproj_ref[mine, :], gbp[...], "NT").astype(B16)

        @pl.when(sweep == 0)
        def _():
            dwp[...] += dot(att_ref[...], gbp[...])

        ratio = size_head**-0.5
        target = dqkv.at[step, jnp.minimum(sweep, 1)]

        def score(w, g):
            low = pair * g
            lanes = slice(SLOT * w, SLOT * w + SLOT)
            for j in range(2):
                at = slice(low + size_head * j, low + size_head * (j + 1))
                cols = slice(SLOT * j, SLOT * j + SLOT)
                bdo[w % 3, at, cols] = datt[at, lanes]
                bdq[w % 3, at, cols] = qkv_ref[0, at, lanes]
                bdk[w % 3, at, cols] = qkv_ref[1, at, lanes]
            values = qkv_ref[2, low : low + pair, SLOT * w : SLOT * w + KEYS]
            dprobs[w % 2, g] = dot(values, bdo[w % 3, low : low + pair, :], "TN")

        def soften(w, g):
            probs = probs_ref[w, g, :KEYS, :].astype(F32)
            term = probs * dprobs[w % 2, g]
            grad = term - probs * jnp.sum(term, axis=0, keepdims=True)
            low_grad = grad.astype(B16)
            beside[w % 2, g, :KEYS, :] = low_grad
            for j in range(2):
                cols = slice(SLOT * j, SLOT * j + SLOT)
                dscore[2 * g + j] += grad[:, cols]
                stacked[w % 2, g, SLOT * j : SLOT * j + KEYS, :] = low_grad[:, cols]

        def attend(w, g):
            low = pair * g
            lanes = slice(SLOT * w, SLOT * w + SLOT)
            rows = slice(low, low + pair)
            got = dot(bdk[w % 3, rows, :], stacked[w % 2, g]) * ratio
            target[low : low + pair, lanes] = got.astype(B16)
            got = dot(bdq[w % 3, rows, :], beside[w % 2, g], "NT") * (1.0 / LOG2E)
            target[part_rows + low : part_rows + low + pair, lanes] = got.astype(B16)
            got = dot(bdo[w % 3, rows, :], probs_ref[w, g], "NT")
            target[2 * part_rows + low : 2 * part_rows + low + pair, lanes] = got.astype(B16)

        for stage in range(QUAD + 2):
            for g in range(pairs):
                if stage < QUAD:
                    score(stage, g)
                if 1 <= stage <= QUAD:
                    soften(stage - 1, g)
                if stage >= 2:
                    attend(stage - 2, g)

        grad = target[...]
        dwq[...] += dot(grad, n1_ref[...])
        wide = grad.astype(F32)
        both = wide[:, :SLOT]
        for w in range(1, QUAD):
            both = both + wide[:, SLOT * w : SLOT * w + SLOT]
        dbqkv[...] += both

    @pl.when(sweep == 2)
    def _():
        dn1 = dot(dqkv[step, 0], turned_ref[0], "TN") + dot(dqkv[step, 1], turned_ref[1], "TN")
        for w in range(QUAD):
            compact[slots * w : slots * w + slots, :] = dn1[SLOT * w : SLOT * w + slots, :]
        grad = compact[...]
        xhat, spread = norm_stats(x_ref[...].astype(F32))
        scaled = grad * gains_ref[0:1, :]
        mean_one = jnp.mean(scaled, axis=-1, keepdims=True)
        mean_two = jnp.mean(scaled * xhat, axis=-1, keepdims=True)
        compact[...] = gf_ref[...] + spread * (scaled - mean_one - xhat * mean_two)
        for w in range(QUAD):
            for r in range(window):
                ref, skip = piece(band, r, quad * QUAD * window, w, window, half)
                at = slots * w + window * r
                ref[skip : skip + window, :] = compact[at : at + window, :]

    for p in range(pages):
        for j in range(quads):

            @pl.when(moment(2, p * quads + j))
            def _():
                cut = slice(edge_at(j), edge_at(j + 1))
                edge[p, :, cut, :] = band[half:, cut, :].astype(B16)
                patch_copy(p, j).start()
                if j == quads - 1:
                    unwrap_band(band, live, half, width, window, least)
                    own_ref[0] = band[:half, :width].astype(B16)

    @pl.when(moment(2, pages * quads - 1))
    def _():
        table()
        big.start_three(1)
        early.start_two()
        for m in outer:
            big.finish(m, sum_ref.at[m])
        big.finish(0, sum_ref.at[0])
        early.start_three()
        big.start_four(1)
        mixed_copy().wait()
        early.finish(early.mine, 0)
        top = small_ref.shape[0]
        small_ref[...] = early.mine[:top]
        for c in range(table_ref.shape[0] // 128):
            table_ref[128 * c : 128 * c + 128, :] = early.mine[top + heads * c : top + heads * (c + 1), :].T
        big.finish(1, sum_ref.at[1])
        for p in range(pages):
            for j in range(quads):
                patch_copy(p, j).wait()


def attn_backward(
    live, dwup, dwout, mixed_next, gf, x, n1, qkv, probs, att, weights_in, turned, gains, biases, places, early, shape, heads, least, share
):
    pages, window, width, model = shape
    half = window // 2
    quads = width // window // QUAD
    slots = window * window
    pairs = heads // 4
    part_rows = model // 2
    devices = (lax.axis_size("page"), lax.axis_size("rows"))
    chips = devices[1] // 2
    hidden = dwup.shape[1]
    wide = 2 * model
    cols = wide // devices[0]
    once = pl.Buffered(1)
    whole = lambda a: pl.BlockSpec(a.shape, lambda s, p, j: (0,) * a.ndim, pipeline_mode=once)
    held = lambda dims: pl.BlockSpec(dims, lambda s, p, j: (0,) * len(dims), pipeline_mode=once)
    anywhere = pl.BlockSpec(memory_space=pl.ANY)
    at = lambda p, j: p * quads + j
    last = pages * quads - 1
    both = lambda s, p, j: jnp.where(s < 2, at(p, j), last)
    first = lambda s, p, j: jnp.where(s == 0, at(p, j), last)
    third = lambda s, p, j: jnp.where(s == 2, at(p, j), 0)
    side = lambda s: jnp.minimum(s, 1)
    own_at = lambda s, p, j: (jnp.where(s == 2, p, 0), 0, 0, 0)
    dma = pltpu.SemaphoreType.DMA
    vmem = pltpu.VMEM
    n = 2 + 2 * hidden // wide
    lines = early.shape[0]
    chunks = -(-((2 * window - 1) ** 2) // 128)

    def small_scratch(rows):
        return [
            vmem((rows, 128), F32),
            vmem((rows, 128), F32),
            vmem((rows, 128), F32),
            vmem((devices[0], rows, 128), F32),
            vmem((rows, 128), F32),
            vmem((chips, rows, 128), F32),
            dma((devices[0] + chips,)),
            dma((devices[0] + chips,)),
        ]

    return pl.pallas_call(
        functools.partial(
            attn_backward_kernel, (window, half, width, model, heads, least, pages, devices, share)
        ),
        grid=(3, pages, quads),
        in_specs=[
            pl.BlockSpec(memory_space=pltpu.SMEM),
            anywhere,
            anywhere,
            anywhere,
            pl.BlockSpec((QUAD * slots, model), lambda s, p, j: (at(p, j), 0)),
            pl.BlockSpec((QUAD * slots, model), lambda s, p, j: (third(s, p, j), 0)),
            pl.BlockSpec((QUAD * SLOT, model), lambda s, p, j: (both(s, p, j), 0)),
            pl.BlockSpec((3, part_rows, QUAD * SLOT), lambda s, p, j: (0, side(s), both(s, p, j))),
            pl.BlockSpec((QUAD, pairs, SLOT, 2 * SLOT), lambda s, p, j: (both(s, p, j), side(s), 0, 0)),
            pl.BlockSpec((model, QUAD * SLOT), lambda s, p, j: (0, first(s, p, j))),
            pl.BlockSpec((model, model), lambda s, p, j: (0, 3), pipeline_mode=once),
            whole(turned),
            whole(gains),
            whole(biases),
            whole(places),
            whole(early),
        ],
        out_specs=[
            held((n, share, wide)),
            held((lines - chunks * heads, 128)),
            held((128 * chunks, heads)),
            pl.BlockSpec((1, half, width, model), own_at),
            anywhere,
            anywhere,
        ],
        out_shape=[
            jax.ShapeDtypeStruct((n, share, wide), B16),
            jax.ShapeDtypeStruct((lines - chunks * heads, 128), F32),
            jax.ShapeDtypeStruct((128 * chunks, heads), F32),
            jax.ShapeDtypeStruct((pages, half, width, model), B16),
            jax.ShapeDtypeStruct((pages, half, width, model), B16),
            jax.ShapeDtypeStruct((pages, half, width + 8, model), B16),
        ],
        scratch_shapes=[
            vmem((window, width + 8, model), F32),
            vmem((QUAD * SLOT, model), B16),
            vmem((part_rows, QUAD * SLOT), B16),
            vmem((2, pairs, KEYS, 2 * SLOT), F32),
            vmem((3, part_rows, 2 * SLOT), B16),
            vmem((3, part_rows, 2 * SLOT), B16),
            vmem((3, part_rows, 2 * SLOT), B16),
            vmem((2, pairs, 2 * SLOT, SLOT), B16),
            vmem((2, pairs, SLOT, 2 * SLOT), B16),
            vmem((pages * quads, 2, 3 * part_rows, QUAD * SLOT), B16),
            vmem((3 * part_rows, model), F32),
            vmem((model, model), F32),
            vmem((QUAD * slots, model), F32),
            vmem((heads // 2, KEYS, SLOT), F32),
            vmem((heads, KEYS, SLOT), F32),
            vmem((3 * part_rows, SLOT), F32),
            vmem((8, model), F32),
            vmem((2, model, wide), B16),
            vmem((pages, half, width + 8, model), B16),
            vmem((n - 2, chips, share, wide), B16),
            vmem((n, chips, share, wide), B16),
            vmem((n, devices[0], chips, share, cols), B16),
            vmem((n, devices[0], chips, share, cols), B16),
            vmem((n, chips, share, cols), B16),
            vmem((n, chips, share, cols), B16),
            vmem((n, share, cols), B16),
            vmem((n, devices[0], share, cols), B16),
            dma((n, chips)),
            dma((n, chips)),
            dma((n, devices[0])),
            dma((n, devices[0])),
            dma((n, chips)),
            dma((n, chips)),
            dma((n, devices[0])),
            dma((n, devices[0])),
        ]
        + small_scratch(lines)
        + [dma((n - 2, chips)), dma((1 + pages * quads,)), dma((1 + pages * quads,))],
        compiler_params=pltpu.CompilerParams(
            vmem_limit_bytes=62 * 2**20, collective_id=0, has_side_effects=True
        ),
    )(live, dwup, dwout, mixed_next, gf, x, n1, qkv, probs, att, weights_in, turned, gains, biases, places, early)


def finish_kernel(
    sizes,
    live_ref,
    sum_hbm,
    min_hbm,
    fin_hbm,
    sin_hbm,
    mout_hbm,
    fout_hbm,
    sout_hbm,
    above_ref,
    own_ref,
    edge_hbm,
    _,
    mixed_ref,
    patch_ref,
    new_in_ref,
    moment_in_ref,
    square_in_ref,
    new_out_ref,
    moment_out_ref,
    square_out_ref,
    sums,
    olds_in,
    news_in,
    olds_out,
    news_out,
    edges,
    tops,
    passed,
    band,
    sems,
    frame_sems,
    in_sems,
    out_sems,
):
    window, half, width, least = sizes
    model = band.shape[2]
    part_rows = model // 2
    share = sums.shape[1]
    pages = edges.shape[0]
    pieces = olds_in.shape[2] // (2 * model)
    tall = olds_out.shape[1] // pieces

    def cut(ref, k):
        return ref.at[:, pl.ds(2 * model * k, 2 * model)]

    def stripe(ref, k):
        return ref.at[pl.ds(tall * k, tall), :]

    copy = pltpu.make_async_copy
    passing = [copy(above_ref, passed.at[0], sems.at[2]), copy(own_ref, passed.at[1], sems.at[3])]
    framed = [
        copy(passed.at[0], mixed_ref.at[:, pl.ds(0, half)], frame_sems.at[0]),
        copy(passed.at[1], patch_ref.at[:, pl.ds(half, half)], frame_sems.at[1]),
    ]
    fetched = [copy(sum_hbm, sums, sems.at[0]), copy(edge_hbm, edges, sems.at[1])]
    laid = copy(tops, patch_ref.at[:, pl.ds(0, half)], frame_sems.at[2])
    ins, outs = [], []
    for k in range(pieces):
        for i, (src, dst) in enumerate(zip((min_hbm, fin_hbm, sin_hbm), (new_in_ref, moment_in_ref, square_in_ref))):
            ins.append(copy(cut(src, k), cut(olds_in.at[i], k), in_sems.at[6 * k + i]))
            outs.append(copy(cut(news_in.at[i], k), cut(dst, k), out_sems.at[6 * k + i]))
        for i, (src, dst) in enumerate(zip((mout_hbm, fout_hbm, sout_hbm), (new_out_ref, moment_out_ref, square_out_ref))):
            ins.append(copy(stripe(src, k), stripe(olds_out.at[i], k), in_sems.at[6 * k + 3 + i]))
            outs.append(copy(stripe(news_out.at[i], k), stripe(dst, k), out_sems.at[6 * k + 3 + i]))
    start(fetched)
    start(ins[:6])
    start(passing)
    start(ins[6:])
    wait(fetched)
    for p in range(pages):
        band[...] = edges[p].astype(F32)
        unwrap_band(band, live_ref[p], half, width, window, least)
        tops[p] = band[:, :width].astype(B16)
    laid.start()
    wait(passing)
    start(framed)
    for k in range(pieces):
        wait(ins[6 * k : 6 * k + 6])
        at = slice(2 * model * k, 2 * model * (k + 1))
        if k < 2:
            grad = jnp.concatenate(
                [
                    sums[h, :, (2 * k + part) * part_rows : (2 * k + part + 1) * part_rows]
                    for part in range(2)
                    for h in range(2)
                ],
                axis=1,
            )
        else:
            grad = sums[k]
        updated = adam_update(olds_in[0, :, at], olds_in[1, :, at], olds_in[2, :, at], grad.astype(F32))
        for i in range(3):
            news_in[i, :, at] = updated[i]
        start(outs[6 * k : 6 * k + 3])
        rows = slice(tall * k, tall * (k + 1))
        grad = sums[4 + k // 2, :, model * (k % 2) : model * (k % 2 + 1)]
        updated = adam_update(olds_out[0, rows], olds_out[1, rows], olds_out[2, rows], grad.astype(F32))
        for i in range(3):
            news_out[i, rows] = updated[i]
        start(outs[6 * k + 3 : 6 * k + 6])
    wait(framed)
    wait(outs)
    laid.wait()


def finish(live, sums, master_in, first_in, second_in, master_out, first_out, second_out, above, own, edge, mixed, least):
    pages, window, width, model = mixed.shape
    half = window // 2
    pieces = master_in.shape[1] // (2 * model)
    anywhere = pl.BlockSpec(memory_space=pl.ANY)
    like = lambda a: jax.ShapeDtypeStruct(a.shape, a.dtype)
    dma = pltpu.SemaphoreType.DMA
    return pl.pallas_call(
        functools.partial(finish_kernel, (window, half, width, least)),
        in_specs=[pl.BlockSpec(memory_space=pltpu.SMEM)] + [anywhere] * 11,
        out_specs=[anywhere] * 8,
        out_shape=[like(mixed), like(mixed)] + [like(master_in)] * 3 + [like(master_out)] * 3,
        scratch_shapes=[
            pltpu.VMEM(sums.shape, B16),
            pltpu.VMEM((3,) + master_in.shape, F32),
            pltpu.VMEM((3,) + master_in.shape, F32),
            pltpu.VMEM((3,) + master_out.shape, F32),
            pltpu.VMEM((3,) + master_out.shape, F32),
            pltpu.VMEM(edge.shape, B16),
            pltpu.VMEM(above.shape, B16),
            pltpu.VMEM((2,) + above.shape, B16),
            pltpu.VMEM((half, width + 8, model), F32),
            dma((4,)),
            dma((3,)),
            dma((6 * pieces,)),
            dma((6 * pieces,)),
        ],
        input_output_aliases={11: 0},
        compiler_params=pltpu.CompilerParams(vmem_limit_bytes=VMEM_LIMIT),
    )(live, sums, master_in, first_in, second_in, master_out, first_out, second_out, above, own, edge, mixed)


def adam_update(master, first, second, grad):
    moment = BETA_ONE * first + (1.0 - BETA_ONE) * grad
    square = BETA_TWO * second + (1.0 - BETA_TWO) * grad * grad
    fix_one = 1.0 - BETA_ONE**STEP
    fix_two = 1.0 - BETA_TWO**STEP
    fresh = master - LEARN_RATE * (
        moment / fix_one / (jnp.sqrt(square / fix_two) + ADAM_EPS) + WEIGHT_DECAY * master
    )
    return (fresh, moment, square)


def shards(
    patches,
    out_grad,
    page_windows,
    region_ids,
    offset_index,
    weights_in,
    weights_out,
    norm_gains,
    biases,
    bias_table,
    master_in,
    master_out,
    first_in,
    second_in,
    first_out,
    second_out,
    first_small,
    second_small,
):
    pages, window, width, model = patches.shape
    half = window // 2
    count = width // window
    least = (count + 1) // 2
    slots = window * window
    table_rows, heads = bias_table.shape
    hidden = weights_out.shape[0]

    bias_lines = biases.reshape(-1, 128)
    lines = model // 128
    table_lanes = -(-table_rows // 128) * 128
    early_lines = EARLY_UP * lines + hidden // 128 + table_lanes * heads // 128

    x, n1, qkv, probs, att, first, n2, below_grad, turned, places = attn_forward(
        page_windows, patches, out_grad, region_ids, offset_index, bias_table.T, weights_in, norm_gains, bias_lines, least
    )
    dwup, dwout, gf, mixed_own, mixed_next, early = mlp(
        page_windows, out_grad, below_grad, n2, first, weights_in, weights_out, norm_gains, bias_lines,
        least, master_in.shape[0], early_lines,
    )
    sums, small, total_table, patch_own, above, edge = attn_backward(
        page_windows, dwup, dwout, mixed_next, gf, x, n1, qkv, probs, att, weights_in, turned, norm_gains,
        bias_lines, places, early, patches.shape, heads, least, master_in.shape[0],
    )
    mixed, patch_grad, new_in, moment_in, square_in, new_out, moment_out, square_out = finish(
        page_windows, sums, master_in, first_in, second_in, master_out, first_out, second_out, above, patch_own,
        edge, mixed_own, least,
    )
    total_small = jnp.concatenate([small.reshape(-1), total_table[:table_rows].reshape(-1)])
    small_master = jnp.concatenate([norm_gains.reshape(-1), biases, bias_table.reshape(-1)])
    new_small, moment_small, square_small = adam_update(
        small_master, first_small, second_small, total_small
    )
    return (
        mixed,
        patch_grad,
        new_in,
        moment_in,
        square_in,
        new_out,
        moment_out,
        square_out,
        new_small,
        moment_small,
        square_small,
    )


def solution(mesh):
    return jax.shard_map(
        shards,
        mesh=mesh,
        in_specs=(
            P("page", "rows", None, None),
            P("page", "rows", None, None),
            P("page"),
            P("page", "rows", None),
            P(),
            P(),
            P(),
            P(),
            P(),
            P(),
            P("rows", None),
            P("rows", None),
            P("rows", None),
            P("rows", None),
            P("rows", None),
            P("rows", None),
            P(),
            P(),
        ),
        out_specs=(
            P("page", "rows", None, None),
            P("page", "rows", None, None),
            P("rows", None),
            P("rows", None),
            P("rows", None),
            P("rows", None),
            P("rows", None),
            P("rows", None),
            P(),
            P(),
            P(),
        ),
        check_vma=False,
    )
```

```python
import functools
import math

import jax
import jax.numpy as jnp
from jax import lax
from jax.experimental import pallas as pl
from jax.experimental.pallas import tpu as pltpu
from jax.sharding import PartitionSpec as P

STEP = 10
NORM_EPS = 1e-05
BETA_ONE = 0.9
BETA_TWO = 0.999
LEARN_RATE = 0.04
WEIGHT_DECAY = 0.05
ADAM_EPS = 1e-08
MASK_VALUE = -1000000000.0

F32 = jnp.float32
B16 = jnp.bfloat16
LOG2E = math.log2(math.e)
VMEM_LIMIT = 60 * 2**20

QUAD = 4
SLOT = 128
KEYS = 104


def dot(left, right, form="NN"):
    sides = {
        "NN": ((1,), (0,)),
        "NT": ((1,), (1,)),
        "TN": ((0,), (0,)),
    }[form]
    return lax.dot_general(left, right, (sides, ((), ())), preferred_element_type=F32)


def load_band(band, low_ref, high_ref, live, half, width, window, least, start=0, end=None):
    end = width if end is None else end
    band[:half, start:end] = low_ref[:, start:end].astype(F32)
    band[half:, start:end] = high_ref[:, start:end].astype(F32)
    if end == width:
        band[:, width:] = jnp.zeros((window, band.shape[1] - width, band.shape[2]), F32)
        for count in range(least, width // window + 1):
            at = slice(count * window, count * window + half)
            band[:, at] = jnp.where(live == count, band[:, :half], band[:, at])


def unwrap_band(band, live, half, width, window, least):
    front = band[:, :half]
    for count in range(least, width // window + 1):
        at = slice(count * window, count * window + half)
        front = jnp.where(live == count, band[:, at], front)
    band[:, :half] = front
    edge = least * window // 8 * 8
    shape = (band.shape[0], width - edge, band.shape[2])
    columns = lax.broadcasted_iota(jnp.int32, shape, 1) + edge
    band[:, edge:width] = jnp.where(columns < live * window, band[:, edge:width], 0.0)


def piece(band, row, base, place, window, half):
    start = window * place + half
    aligned = start // 8 * 8
    skip = start - aligned
    size = -(-(skip + window) // 8) * 8
    ref = band.at[row, pl.ds(pl.multiple_of(base, 8) + aligned, size), :]
    return ref, skip


def gather_window(band, base, place, window, half):
    parts = []
    for row in range(window):
        ref, skip = piece(band, row, base, place, window, half)
        parts.append(ref[skip : skip + window, :])
    return parts


def norm_stats(value):
    centre = jnp.mean(value, axis=-1, keepdims=True)
    centered = value - centre
    spread = lax.rsqrt(jnp.mean(centered * centered, axis=-1, keepdims=True) + NORM_EPS)
    return centered * spread, spread


def fold(value):
    rows, cols = value.shape
    return jnp.sum(value.reshape(rows // 8, 8, cols), axis=0)


MESH = pl.DeviceIdType.MESH


def remote(src, dst, send, recv, device):
    return pltpu.make_async_remote_copy(
        src_ref=src, dst_ref=dst, send_sem=send, recv_sem=recv, device_id=device, device_id_type=MESH
    )


def lay_lines(lines_ref, at, row):
    for i in range(row.shape[1] // 128):
        lines_ref[at + i : at + i + 1, :] = row[:, 128 * i : 128 * i + 128]


def lay_row(ref, row, lines_ref, at, count):
    for i in range(count):
        ref[row : row + 1, 128 * i : 128 * i + 128] = lines_ref[at + i : at + i + 1, :]


def attn_forward_kernel(
    sizes,
    live_ref,
    patches_ref,
    grads_ref,
    low_ref,
    label_ref,
    off_ref,
    tab_ref,
    wqkv_ref,
    wproj_ref,
    gains_ref,
    biases_ref,
    x_ref,
    n1_ref,
    qkv_ref,
    probs_ref,
    att_ref,
    first_ref,
    n2_ref,
    grad_halo_ref,
    turned_ref,
    places_ref,
    halo,
    send,
    recv,
    band,
    bias,
    scores,
    bdq,
    bdv,
    stacked,
    xs,
    ns,
    vecs,
    column,
    square,
    flat,
    marks,
):
    window, half, width, model, heads, least, pages, rows_count = sizes
    slots = window * window
    size_head = model // heads
    page, quad = pl.program_id(0), pl.program_id(1)
    live = live_ref[page]
    pairs = heads // 2
    part_rows = model // 2
    lines = model // 128
    row = lax.axis_index("rows")
    behind, ahead = lax.rem(row + rows_count - 1, rows_count), lax.rem(row + 1, rows_count)

    cut = -(-(QUAD * window + half) // 16) * 16

    def halo_copy(p, k):
        at = (pl.ds(0, cut), pl.ds(cut, width - cut))[k]
        return remote(
            patches_ref.at[p, pl.ds(0, half), at],
            halo.at[p, :, at],
            send.at[pages * (1 + k) + p],
            recv.at[pages * (1 + k) + p],
            {"rows": behind},
        )

    def grad_copy(p):
        return remote(
            grads_ref.at[p, pl.ds(0, half)],
            grad_halo_ref.at[p],
            send.at[p],
            recv.at[p],
            {"rows": behind},
        )

    @pl.when(jnp.logical_and(page == 0, quad == 0))
    def _():
        barrier = pltpu.get_barrier_semaphore()
        for neighbour in (behind, ahead):
            pl.semaphore_signal(barrier, inc=1, device_id={"rows": neighbour}, device_id_type=MESH)
        pl.semaphore_wait(barrier, 2)
        halo_copy(0, 0).start()
        vecs[...] = jnp.zeros_like(vecs)
        vecs[0:1, :] = gains_ref[0:1, :]
        lay_row(vecs, 1, biases_ref, 0, lines)
        lay_row(vecs, 2, biases_ref, 3 * lines, lines)
        vecs[3:4, :] = gains_ref[1:2, :]
        lay_row(vecs, 4, biases_ref, 4 * lines, lines)
        column[...] = jnp.zeros_like(column)
        for h in range(2):
            for part in range(3):
                rows = slice(part * part_rows, part * part_rows + part_rows)
                cols = slice(part * model + h * part_rows, part * model + (h + 1) * part_rows)
                turned_ref[h, rows, :] = wqkv_ref[:, cols].T
                if part != 1:
                    for i in range(part_rows // 128):
                        line = lines * (1 + part // 2) + h * (part_rows // 128) + i
                        spread = jnp.broadcast_to(biases_ref[line : line + 1, :], (128, 128))
                        at = part * part_rows + 128 * i
                        column[h, at : at + 128, :] = spread.T
        halo_copy(0, 1).start()
        square[...] = jnp.full_like(square, -1)
        square[:slots, :slots] = off_ref[...]
        places = square[...].T[:KEYS]
        places_ref[...] = places
        off = jnp.maximum(places, 0)
        flat[...] = jnp.zeros_like(flat)
        flat[:, : tab_ref.shape[1]] = tab_ref[...] * LOG2E
        low, high = jnp.bitwise_and(off, 127), jnp.right_shift(off, 7)
        for h in range(heads):
            got = jnp.zeros((KEYS, SLOT), F32)
            for c in range(flat.shape[1] // 128):
                source = jnp.broadcast_to(flat[h : h + 1, 128 * c : 128 * c + 128], (KEYS, SLOT))
                picked = jnp.take_along_axis(source, low, axis=1, mode="promise_in_bounds")
                got = jnp.where(high == c, picked, got)
            bias[h] = got
        bdq[...] = jnp.zeros_like(bdq)
        bdv[...] = jnp.zeros_like(bdv)
        stacked[...] = jnp.zeros_like(stacked)

    for p in range(pages):

        @pl.when(jnp.logical_and(page == p, quad == 0))
        def _():
            halo_copy(p, 0).wait()
            load_band(band, low_ref.at[0], halo.at[p], live, half, width, window, least, 0, cut)

        @pl.when(jnp.logical_and(page == p, quad == 1))
        def _():
            halo_copy(p, 1).wait()
            if p + 1 < pages:
                for k in range(2):
                    halo_copy(p + 1, k).start()
            load_band(band, low_ref.at[0], halo.at[p], live, half, width, window, least, cut)

    @pl.when(jnp.logical_and(page == (pages - 1) // 2, quad == 2))
    def _():
        for p in range(pages):
            grad_copy(p).start()

    @pl.when(jnp.logical_and(page == pages - 1, quad == pl.num_programs(1) - 1))
    def _():
        for p in range(pages):
            grad_copy(p).wait()

    base = quad * (QUAD * window)
    for w in range(QUAD):
        for r, part in enumerate(gather_window(band, base, w, window, half)):
            at = slots * w + window * r
            xs[at : at + window, :] = part
    x = xs[...]
    x_ref[...] = x.astype(B16)
    xhat, _ = norm_stats(x)
    ns[...] = xhat * vecs[0:1, :] + vecs[1:2, :]
    for w in range(QUAD):
        n1_ref[SLOT * w : SLOT * w + slots, :] = ns[slots * w : slots * w + slots, :].astype(B16)
        n1_ref[SLOT * w + slots : SLOT * w + SLOT, :] = jnp.zeros((SLOT - slots, model), B16)
    scale = size_head**-0.5 * LOG2E
    n1 = n1_ref[...]
    for h in range(2):
        got = dot(turned_ref[h], n1, "NT") + column[h, :, 0:1]
        at = slice(h * part_rows, h * part_rows + part_rows)
        qkv_ref[0, at, :] = (got[:part_rows] * scale).astype(B16)
        qkv_ref[1, at, :] = got[part_rows : 2 * part_rows].astype(B16)
        qkv_ref[2, at, :] = got[2 * part_rows :].astype(B16)

    sames = []
    lane = lax.broadcasted_iota(jnp.int32, (1, SLOT), 1)
    for j in range(width // window // QUAD):

        @pl.when(quad == j)
        def _():
            at = QUAD * window * j
            marks[:, : QUAD * window] = label_ref[0, :, at : at + QUAD * window].astype(F32)

    for w in range(QUAD):
        label = jnp.full((1, SLOT), -1.0, F32)
        for r in range(window):
            turned = pltpu.roll(marks[r : r + 1, :], (window * (r - w)) % SLOT, 1)
            here = jnp.logical_and(lane >= window * r, lane < window * (r + 1))
            label = jnp.where(here, turned, label)
        spread = jnp.broadcast_to(label, (SLOT, SLOT))
        sames.append((spread == spread.T)[:KEYS])
    pair = 2 * size_head

    def score(w, g):
        low = pair * g
        lanes = slice(SLOT * w, SLOT * w + SLOT)
        for j in range(2):
            at = slice(low + size_head * j, low + size_head * (j + 1))
            cols = slice(SLOT * j, SLOT * j + SLOT)
            bdq[w % 2, at, cols] = qkv_ref[0, at, lanes]
            bdv[w % 3, at, cols] = qkv_ref[2, at, lanes]
        keys = qkv_ref[1, low : low + pair, SLOT * w : SLOT * w + KEYS]
        scores[w % 2, g] = dot(keys, bdq[w % 2, low : low + pair, :], "TN")

    def soften(w, g):
        for j in range(2):
            cols = slice(SLOT * j, SLOT * j + SLOT)
            s = jnp.where(sames[w], scores[w % 2, g, :, cols] + bias[2 * g + j], MASK_VALUE)
            s = jnp.exp2(s - jnp.max(s, axis=0, keepdims=True))
            low_probs = (s * (1.0 / jnp.sum(s, axis=0, keepdims=True))).astype(B16)
            probs_ref[w, g, :KEYS, cols] = low_probs
            probs_ref[w, g, KEYS:, cols] = jnp.zeros((SLOT - KEYS, SLOT), B16)
            stacked[w % 2, g, SLOT * j : SLOT * j + KEYS, :] = low_probs

    def attend(w, g):
        low = pair * g
        got = dot(bdv[w % 3, low : low + pair, :], stacked[w % 2, g])
        att_ref[low : low + pair, SLOT * w : SLOT * w + SLOT] = got.astype(B16)

    for step in range(QUAD + 2):
        for g in range(pairs):
            if step < QUAD:
                score(step, g)
            if 1 <= step <= QUAD:
                soften(step - 1, g)
            if step >= 2:
                attend(step - 2, g)

    branch = dot(att_ref[...], wproj_ref[...], "TN")
    for w in range(QUAD):
        rows = slice(slots * w, slots * w + slots)
        first_ref[rows, :] = xs[rows, :] + branch[SLOT * w : SLOT * w + slots, :] + vecs[2:3, :]
    xhat, _ = norm_stats(first_ref[...])
    n2_ref[...] = (xhat * vecs[3:4, :] + vecs[4:5, :]).astype(B16)


def attn_forward(live, patches, out_grad, labels, off, tab, weights_in, gains, biases, least):
    pages, window, width, model = patches.shape
    half = window // 2
    heads, table_rows = tab.shape
    table_lanes = -(-table_rows // 128) * 128
    quads = width // window // QUAD
    tokens = pages * window * width
    slots = window * window
    padded = pages * quads * QUAD * SLOT
    steps = (pages, quads)
    whole = lambda a: pl.BlockSpec(a.shape, lambda p, j: (0,) * a.ndim, pipeline_mode=pl.Buffered(1))
    at = lambda p, j: p * quads + j
    return pl.pallas_call(
        functools.partial(
            attn_forward_kernel,
            (window, half, width, model, heads, least, pages, lax.axis_size("rows")),
        ),
        grid=steps,
        in_specs=[
            pl.BlockSpec(memory_space=pltpu.SMEM),
            pl.BlockSpec(memory_space=pl.ANY),
            pl.BlockSpec(memory_space=pl.ANY),
            pl.BlockSpec((1, half, width, model), lambda p, j: (p, 1, 0, 0)),
            pl.BlockSpec((1, window, width), lambda p, j: (p, 0, 0)),
            whole(off),
            whole(tab),
            pl.BlockSpec((model, 3 * model), lambda p, j: (0, 0), pipeline_mode=pl.Buffered(1)),
            pl.BlockSpec((model, model), lambda p, j: (0, 3), pipeline_mode=pl.Buffered(1)),
            whole(gains),
            whole(biases),
        ],
        out_specs=[
            pl.BlockSpec((QUAD * slots, model), lambda p, j: (at(p, j), 0)),
            pl.BlockSpec((QUAD * SLOT, model), lambda p, j: (at(p, j), 0)),
            pl.BlockSpec((3, model, QUAD * SLOT), lambda p, j: (0, 0, at(p, j))),
            pl.BlockSpec((QUAD, heads // 2, SLOT, 2 * SLOT), lambda p, j: (at(p, j), 0, 0, 0)),
            pl.BlockSpec((model, QUAD * SLOT), lambda p, j: (0, at(p, j))),
            pl.BlockSpec((QUAD * slots, model), lambda p, j: (at(p, j), 0)),
            pl.BlockSpec((QUAD * slots, model), lambda p, j: (at(p, j), 0)),
            pl.BlockSpec(memory_space=pl.ANY),
            pl.BlockSpec((2, 3 * model // 2, model), lambda p, j: (0, 0, 0), pipeline_mode=pl.Buffered(1)),
            pl.BlockSpec((KEYS, SLOT), lambda p, j: (0, 0)),
        ],
        out_shape=[
            jax.ShapeDtypeStruct((tokens, model), B16),
            jax.ShapeDtypeStruct((padded, model), B16),
            jax.ShapeDtypeStruct((3, model, padded), B16),
            jax.ShapeDtypeStruct((pages * quads * QUAD, heads // 2, SLOT, 2 * SLOT), B16),
            jax.ShapeDtypeStruct((model, padded), B16),
            jax.ShapeDtypeStruct((tokens, model), F32),
            jax.ShapeDtypeStruct((tokens, model), B16),
            jax.ShapeDtypeStruct((pages, half, width, model), B16),
            jax.ShapeDtypeStruct((2, 3 * model // 2, model), B16),
            jax.ShapeDtypeStruct((KEYS, SLOT), jnp.int32),
        ],
        scratch_shapes=[
            pltpu.VMEM((pages, half, width, model), B16),
            pltpu.SemaphoreType.DMA((3 * pages,)),
            pltpu.SemaphoreType.DMA((3 * pages,)),
            pltpu.VMEM((window, width + 8, model), F32),
            pltpu.VMEM((heads, KEYS, SLOT), F32),
            pltpu.VMEM((2, heads // 2, KEYS, 2 * SLOT), F32),
            pltpu.VMEM((2, model, 2 * SLOT), B16),
            pltpu.VMEM((3, model, 2 * SLOT), B16),
            pltpu.VMEM((2, heads // 2, 2 * SLOT, SLOT), B16),
            pltpu.VMEM((QUAD * slots, model), F32),
            pltpu.VMEM((QUAD * slots, model), F32),
            pltpu.VMEM((8, model), F32),
            pltpu.VMEM((2, 3 * model // 2, 128), F32),
            pltpu.VMEM((SLOT, SLOT), jnp.int32),
            pltpu.VMEM((heads, table_lanes), F32),
            pltpu.VMEM((window, SLOT), F32),
        ],
        compiler_params=pltpu.CompilerParams(
            vmem_limit_bytes=VMEM_LIMIT, collective_id=1, has_side_effects=True
        ),
    )(live, patches, out_grad, patches, labels, off, tab, weights_in, weights_in, gains, biases)


MLP_COLS = 1024
MLP_CHUNKS = 2
MLP_ROWS = 800
EARLY_UP = 8


def mlp_kernel(
    sizes,
    live_ref,
    low_ref,
    high_ref,
    n2_ref,
    first_hbm,
    wup_ref,
    wout_ref,
    gains_ref,
    biases_ref,
    dwup_ref,
    dwout_ref,
    gf_hbm,
    own_hbm,
    next_hbm,
    early_ref,
    bup,
    vecs,
    sums,
    band,
    cot,
    res,
    dn2,
    act_all,
    pre_all,
    first_ref,
    held,
    frames,
    first_sem,
    gf_sems,
    frame_sems,
):
    window, half, width, model, least, share = sizes
    pages = low_ref.shape[0]
    slots = window * window
    count = width // window
    quads = count // QUAD
    chunk = pl.program_id(0)
    tokens = n2_ref.shape[0]
    cols = wup_ref.shape[1]
    lines = model // 128

    for c in range(MLP_CHUNKS):

        @pl.when(chunk == c)
        def _():
            lay_row(bup, 0, biases_ref, 6 * lines + c * (cols // 128), cols // 128)

    first_copy = pltpu.make_async_copy(first_hbm, first_ref, first_sem)

    def gf_copy(k):
        rows = pl.ds(pl.multiple_of(k * QUAD * slots, 16), QUAD * slots)
        return pltpu.make_async_copy(dn2.at[rows, :], gf_hbm.at[rows, :], gf_sems.at[k])

    def frame_copies(page):
        return [
            pltpu.make_async_copy(frames.at[page, 0], own_hbm.at[page, pl.ds(half, half)], frame_sems.at[page, 0]),
            pltpu.make_async_copy(frames.at[page, 1], next_hbm.at[page], frame_sems.at[page, 1]),
        ]

    @pl.when(chunk == 0)
    def _():
        first_copy.start()
        early_ref[...] = jnp.zeros_like(early_ref)
        vecs[0:1, :] = gains_ref[1:2, :]
        lay_row(vecs, 1, biases_ref, 5 * lines, lines)
        for page in range(pages):
            live = live_ref[page]
            load_band(band, low_ref.at[page], high_ref.at[page], live, half, width, window, least)

            def body(j, carry):
                for w in range(QUAD):
                    alive = jnp.where(j * QUAD + w < live, 1.0, 0.0)
                    for r, part in enumerate(gather_window(band, j * QUAD * window, w, window, half)):
                        at = slots * w + window * r
                        held[at : at + window, :] = part * alive
                rows = pl.ds(pl.multiple_of((page * quads + j) * QUAD * slots, 16), QUAD * slots)
                cot[rows, :] = held[...].astype(B16)
                return carry

            lax.fori_loop(0, quads, body, 0)

    def body(i, total):
        rows = pl.ds(pl.multiple_of(i * MLP_ROWS, 16), MLP_ROWS)
        grad = cot[rows, :]
        pre = dot(n2_ref[rows, :], wup_ref[...]) + bup[0:1, :]
        grad_act = dot(grad, wout_ref[...], "NT")
        share = 0.5 * (1.0 + lax.erf(pre * 0.5**0.5))
        act = (pre * share).astype(B16)
        slope = share + pre * (jnp.exp2((-0.5 * LOG2E) * pre * pre) * (2.0 * math.pi) ** -0.5)
        grad_pre = (grad_act * slope).astype(B16)
        act_all[rows, :] = act
        pre_all[rows, :] = grad_pre
        up = dot(act, wout_ref[...])
        down = dot(grad_pre, wup_ref[...], "NT")

        res[rows, :] = jnp.where(chunk == 0, 0.0, res[rows, :]) + up
        dn2[rows, :] = jnp.where(chunk == 0, 0.0, dn2[rows, :]) + down
        return total + fold(grad_pre.astype(F32))

    total = lax.fori_loop(0, tokens // MLP_ROWS, body, jnp.zeros((8, cols), F32))
    total = jnp.sum(total, axis=0, keepdims=True)
    for c in range(MLP_CHUNKS):

        @pl.when(chunk == c)
        def _():
            lay_lines(early_ref, EARLY_UP * lines + c * (cols // 128), total)

    grad_out = dot(act_all[...], cot[...], "TN").astype(B16)
    for s in range(dwout_ref.shape[0] // share):
        for a in range(dwout_ref.shape[1] // model):
            at = (s * (dwout_ref.shape[1] // model) + a) * share
            dwout_ref[share * s : share * s + share, model * a : model * a + model] = grad_out[at : at + share, :]
    dwup_ref[...] = dot(n2_ref[...], pre_all[...], "TN").astype(B16)

    @pl.when(chunk == pl.num_programs(0) - 1)
    def _():
        sums[...] = jnp.zeros_like(sums)
        first_copy.wait()
        for page in range(pages):
            live = live_ref[page]

            def body(j, carry):
                at = pl.multiple_of((page * quads + j) * QUAD * slots, 16)
                rows = pl.ds(at, QUAD * slots)
                first = first_ref[rows, :]
                res[rows, :] += first + vecs[1:2, :]
                xhat, spread = norm_stats(first)
                grad = dn2[rows, :]
                given = cot[rows, :].astype(F32)
                scaled = grad * vecs[0:1, :]
                mean_one = jnp.mean(scaled, axis=-1, keepdims=True)
                mean_two = jnp.mean(scaled * xhat, axis=-1, keepdims=True)
                whole = given + spread * (scaled - mean_one - xhat * mean_two)
                dn2[rows, :] = whole
                gf_copy(page * quads + j).start()
                sums[0:8, :] += fold(grad * xhat)
                sums[8:16, :] += fold(whole)
                sums[16:24, :] += fold(grad)
                sums[24:32, :] += fold(given)
                for w in range(QUAD):
                    for r in range(window):
                        ref, skip = piece(band, r, j * QUAD * window, w, window, half)
                        ref[skip : skip + window, :] = res[
                            pl.ds(at + slots * w // 8 * 8, slots + 4), :
                        ][slots * w % 8 + window * r : slots * w % 8 + window * r + window, :]
                return carry

            lax.fori_loop(0, quads, body, 0)
            unwrap_band(band, live, half, width, window, least)
            frames[page, 0] = band[:half, :width].astype(B16)
            frames[page, 1] = band[half:, :width].astype(B16)
            start(frame_copies(page))
        for k, place in enumerate((1, 5, 6, 7)):
            lay_lines(early_ref, place * lines, jnp.sum(sums[8 * k : 8 * k + 8, :], axis=0, keepdims=True))
        for k in range(pages * quads):
            gf_copy(k).wait()
        for page in range(pages):
            wait(frame_copies(page))


def mlp(live, out_grad, halo, n2, first, weights_in, weights_out, gains, biases, least, share, lines):
    pages, window, width, model = out_grad.shape
    half = window // 2
    tokens = n2.shape[0]
    hidden = weights_out.shape[0]
    skip = (weights_in.shape[1] - hidden) // MLP_COLS
    once = pl.Buffered(1)
    whole = lambda a: pl.BlockSpec(a.shape, lambda c: (0,) * a.ndim, pipeline_mode=once)
    band_block = (pages, half, width, model)
    return pl.pallas_call(
        functools.partial(mlp_kernel, (window, half, width, model, least, share)),
        grid=(hidden // MLP_COLS,),
        in_specs=[
            pl.BlockSpec(memory_space=pltpu.SMEM),
            pl.BlockSpec(band_block, lambda c: (0, 1, 0, 0), pipeline_mode=once),
            pl.BlockSpec(band_block, lambda c: (0, 0, 0, 0), pipeline_mode=once),
            whole(n2),
            pl.BlockSpec(memory_space=pl.ANY),
            pl.BlockSpec((model, MLP_COLS), lambda c: (0, c + skip)),
            pl.BlockSpec((MLP_COLS, model), lambda c: (c, 0)),
            whole(gains),
            whole(biases),
        ],
        out_specs=[
            pl.BlockSpec((model, MLP_COLS), lambda c: (0, c)),
            pl.BlockSpec((model * MLP_COLS // hidden, hidden), lambda c: (c, 0)),
            pl.BlockSpec(memory_space=pl.ANY),
            pl.BlockSpec(memory_space=pl.ANY),
            pl.BlockSpec(memory_space=pl.ANY),
            pl.BlockSpec((lines, 128), lambda c: (0, 0)),
        ],
        out_shape=[
            jax.ShapeDtypeStruct((model, hidden), B16),
            jax.ShapeDtypeStruct((model, hidden), B16),
            jax.ShapeDtypeStruct((tokens, model), F32),
            jax.ShapeDtypeStruct(out_grad.shape, B16),
            jax.ShapeDtypeStruct(band_block, B16),
            jax.ShapeDtypeStruct((lines, 128), F32),
        ],
        scratch_shapes=[
            pltpu.VMEM((8, MLP_COLS), F32),
            pltpu.VMEM((8, model), F32),
            pltpu.VMEM((32, model), F32),
            pltpu.VMEM((window, width + 8, model), F32),
            pltpu.VMEM((tokens, model), B16),
            pltpu.VMEM((tokens, model), F32),
            pltpu.VMEM((tokens, model), F32),
            pltpu.VMEM((tokens, MLP_COLS), B16),
            pltpu.VMEM((tokens, MLP_COLS), B16),
            pltpu.VMEM((tokens, model), F32),
            pltpu.VMEM((QUAD * window * window, model), F32),
            pltpu.VMEM((pages, 2, half, width, model), B16),
            pltpu.SemaphoreType.DMA,
            pltpu.SemaphoreType.DMA((tokens // (QUAD * window * window),)),
            pltpu.SemaphoreType.DMA((pages, 2)),
        ],
        compiler_params=pltpu.CompilerParams(vmem_limit_bytes=VMEM_LIMIT),
    )(live, out_grad, halo, n2, first, weights_in, weights_out, gains, biases)


def table_sum(off_ref, grad_ref, out_ref, at, heads, chunks):
    rows = 128 * chunks
    keys = grad_ref.shape[1]
    names = lax.broadcasted_iota(jnp.int32, (rows, SLOT), 0)
    total = jnp.zeros((3 * heads, rows), F32)
    grad = jnp.swapaxes(grad_ref[...], 0, 1)
    for k in range(0, keys, 8):
        hot = jnp.concatenate(
            [jnp.where(names == off_ref[i : i + 1, :], 1.0, 0.0).astype(B16) for i in range(k, k + 8)], axis=1
        )
        value = jnp.concatenate([grad[i] for i in range(k, k + 8)], axis=1)
        high = value.astype(B16)
        rest = value - high.astype(F32)
        middle = rest.astype(B16)
        low = (rest - middle.astype(F32)).astype(B16)
        total += dot(jnp.concatenate([high, middle, low], axis=0), hot, "NT")
    total = total[:heads] + total[heads : 2 * heads] + total[2 * heads :]
    for c in range(chunks):
        out_ref[at + heads * c : at + heads * c + heads, :] = total[:, 128 * c : 128 * c + 128]


class Exchange:
    def __init__(self, pages, chips, share, bufs, sems):
        self.pages, self.chips, self.share = pages, chips, share
        self.rec1, self.s1, self.rec2, self.s2, self.rec3, self.s3, self.rec4 = bufs
        self.send1, self.recv1, self.send2, self.recv2, self.send3, self.recv3, self.send4, self.recv4 = sems
        self.page, row = lax.axis_index("page"), lax.axis_index("rows")
        self.chip, self.core = row // 2, row % 2
        self.other = 2 * self.chip + 1 - self.core
        self.cols = self.s3.shape[-1]

    def page_peer(self, d):
        return lax.rem(self.page + d, self.pages)

    def chip_peer(self, d):
        return lax.rem(self.chip + d, self.chips)

    def along(self, d):
        return {"rows": 2 * self.chip_peer(d) + self.core}

    def rows_of(self, ref, z, c):
        return ref.at[pl.ds(pl.multiple_of((2 * z + c) * self.share, 16), self.share), :]

    def one(self, m, grad):
        return [
            remote(
                self.rows_of(grad, z, 1 - self.core),
                self.rec1.at[m, z],
                self.send1.at[m, z],
                self.recv1.at[m, z],
                {"rows": self.other},
            )
            for z in range(self.chips)
        ]

    def two(self, m):
        return [
            remote(
                self.s1.at[m, self.page_peer(d)],
                self.rec2.at[m, self.page],
                self.send2.at[m, d],
                self.recv2.at[m, d],
                {"page": self.page_peer(d)},
            )
            for d in range(1, self.pages)
        ]

    def three(self, m):
        return [
            remote(
                self.s2.at[m, self.chip_peer(d)],
                self.rec3.at[m, self.chip],
                self.send3.at[m, d],
                self.recv3.at[m, d],
                self.along(d),
            )
            for d in range(1, self.chips)
        ]

    def four(self, m):
        return [
            remote(
                self.s3.at[m],
                self.rec4.at[m, self.page],
                self.send4.at[m, d],
                self.recv4.at[m, d],
                {"page": self.page_peer(d)},
            )
            for d in range(1, self.pages)
        ]

    def start_one(self, m, grad):
        start(self.one(m, grad))

    def start_two(self, m, grad, own):
        wait(self.one(m, grad))
        for q in range(self.pages):
            at = slice(self.cols * q, self.cols * q + self.cols)
            for z in range(self.chips):
                self.s1[m, q, z] = (own(z)[:, at].astype(F32) + self.rec1[m, z, :, at].astype(F32)).astype(B16)
        start(self.two(m))
        self.rec2[m, self.page] = self.s1[m, self.page]

    def start_three(self, m):
        wait(self.two(m))
        total = self.rec2[m, 0].astype(F32)
        for q in range(1, self.pages):
            total = total + self.rec2[m, q].astype(F32)
        self.s2[m] = total.astype(B16)
        start(self.three(m))
        self.rec3[m, self.chip] = self.s2[m, self.chip]

    def start_four(self, m):
        wait(self.three(m))
        total = self.rec3[m, 0].astype(F32)
        for z in range(1, self.chips):
            total = total + self.rec3[m, z].astype(F32)
        self.s3[m] = total.astype(B16)
        start(self.four(m))
        self.rec4[m, self.page] = self.s3[m]

    def finish(self, m, out_ref):
        wait(self.four(m))
        for q in range(self.pages):
            out_ref[:, self.cols * q : self.cols * q + self.cols] = self.rec4[m, q]


class SmallExchange:
    def __init__(self, big, bufs, sems):
        self.big = big
        self.mine, self.one_in, self.two_out, self.two_in, self.three_out, self.three_in = bufs
        self.send, self.recv = sems

    def one(self):
        return [remote(self.mine, self.one_in, self.send.at[0], self.recv.at[0], {"rows": self.big.other})]

    def two(self):
        big = self.big
        return [
            remote(
                self.two_out,
                self.two_in.at[big.page],
                self.send.at[d],
                self.recv.at[d],
                {"page": big.page_peer(d)},
            )
            for d in range(1, big.pages)
        ]

    def three(self):
        big = self.big
        return [
            remote(
                self.three_out,
                self.three_in.at[big.chip],
                self.send.at[big.pages + d],
                self.recv.at[big.pages + d],
                big.along(d),
            )
            for d in range(1, big.chips)
        ]

    def start_one(self):
        start(self.one())

    def start_two(self):
        wait(self.one())
        total = self.mine[...] + self.one_in[...]
        self.two_out[...] = total
        start(self.two())
        self.two_in[self.big.page] = total

    def start_three(self):
        wait(self.two())
        total = self.two_in[0]
        for q in range(1, self.big.pages):
            total = total + self.two_in[q]
        self.three_out[...] = total
        start(self.three())
        self.three_in[self.big.chip] = total

    def finish(self, out_ref, at):
        wait(self.three())
        total = self.three_in[0]
        for z in range(1, self.big.chips):
            total = total + self.three_in[z]
        out_ref[at : at + total.shape[0], :] = total


def start(copies):
    for copy in copies:
        copy.start()


def wait(copies):
    for copy in copies:
        copy.wait()


def attn_backward_kernel(
    sizes,
    live_ref,
    up_ref,
    out_ref,
    mixed_ref,
    gf_ref,
    x_ref,
    n1_ref,
    qkv_ref,
    probs_ref,
    att_ref,
    wproj_ref,
    turned_ref,
    gains_ref,
    biases_ref,
    places_ref,
    early_ref,
    sum_ref,
    small_ref,
    table_ref,
    own_ref,
    mixed_halo_ref,
    patch_halo_ref,
    band,
    gbp,
    datt,
    dprobs,
    bdq,
    bdk,
    bdo,
    stacked,
    beside,
    dqkv,
    dwq,
    dwp,
    compact,
    dscore,
    dscores,
    dbqkv,
    vecs,
    dwa,
    edge,
    own1,
    *rest,
):
    window, half, width, model, heads, least, pages, devices, share = sizes
    slots = window * window
    size_head = model // heads
    sweep, page, quad = pl.program_id(0), pl.program_id(1), pl.program_id(2)
    quads = width // window // QUAD
    step = page * quads + quad
    live = live_ref[page]
    pairs = heads // 4
    pair = 2 * size_head
    part_rows = model // 2
    lines = model // 128
    cols = 2 * model
    big = Exchange(devices[0], devices[1] // 2, share, rest[:7], rest[7:15])
    early = SmallExchange(big, (rest[15],) + rest[16:21], rest[21:23])
    local, halo_send, halo_recv = rest[23:]
    row = lax.axis_index("rows")
    behind, ahead = lax.rem(row + devices[1] - 1, devices[1]), lax.rem(row + 1, devices[1])
    matrices = [dwa.at[0], dwa.at[1]]
    for ref in (up_ref, out_ref):
        for h in range(ref.shape[1] // cols):
            matrices.append(ref.at[:, pl.ds(h * cols, cols)])
    outer = range(2, len(matrices))

    def fetch(m):
        return [
            pltpu.make_async_copy(
                big.rows_of(matrices[m], z, big.core), own1.at[m - 2, z], local.at[m - 2, z]
            )
            for z in range(big.chips)
        ]

    def mixed_copy():
        return remote(mixed_ref, mixed_halo_ref, halo_send.at[0], halo_recv.at[0], {"rows": ahead})

    def edge_at(j):
        return 0 if j == 0 else width + 8 if j == quads else (j * QUAD * window + half) // 16 * 16

    def patch_copy(p, j):
        cut = pl.ds(edge_at(j), edge_at(j + 1) - edge_at(j))
        k = 1 + p * quads + j
        return remote(
            edge.at[p, :, cut, :], patch_halo_ref.at[p, :, cut, :], halo_send.at[k], halo_recv.at[k], {"rows": ahead}
        )

    def moment(at_sweep, at_step):
        return jnp.logical_and(sweep == at_sweep, step == at_step)

    @pl.when(moment(0, 0))
    def _():
        barrier = pltpu.get_barrier_semaphore()
        peers = [{"rows": big.other}, {"rows": behind}, {"rows": ahead}]
        peers += [{"page": big.page_peer(d)} for d in range(1, big.pages)]
        peers += [big.along(d) for d in range(1, big.chips)]
        for peer in peers:
            pl.semaphore_signal(barrier, inc=1, device_id=peer, device_id_type=MESH)
        pl.semaphore_wait(barrier, len(peers))
        for m in outer:
            big.start_one(m, matrices[m])
            start(fetch(m))
        mixed_copy().start()
        early.mine[...] = early_ref[...]
        for ref in (bdq, bdk, bdo, stacked, beside, gbp, dwq, dwp, dbqkv, dscore, vecs):
            ref[...] = jnp.zeros_like(ref)

    def flush(h):
        for part in range(3):
            rows = slice(part * part_rows, part * part_rows + part_rows)
            dwa[h, :, rows] = dwq[rows, :].T.astype(B16)
        dwa[h, :, 3 * part_rows :] = dwp[:, h * part_rows : (h + 1) * part_rows].astype(B16)
        big.start_one(h, matrices[h])
        for k, part in enumerate((0, 2)):
            total = jnp.sum(dbqkv[part * part_rows : (part + 1) * part_rows, :].T, axis=0, keepdims=True)
            lay_lines(early.mine, lines * (3 + k) + h * (lines // 2), total)
        column = jnp.sum(dbqkv[...], axis=1, keepdims=True)
        weights = turned_ref[h].astype(F32)
        shifts = jnp.sum(weights * column, axis=0, keepdims=True)
        gains = jnp.sum(weights * dwq[...], axis=0, keepdims=True)
        vecs[0:1, :] += gains
        vecs[1:2, :] += shifts
        if h == 1:
            lay_row(vecs, 2, biases_ref, 0, lines)
            total = (vecs[0:1, :] - vecs[2:3, :] * vecs[1:2, :]) / gains_ref[0:1, :]
            lay_lines(early.mine, 0, total)
            lay_lines(early.mine, 2 * lines, vecs[1:2, :])
        dscores[h * heads // 2 : (h + 1) * heads // 2] = dscore[...]
        if h == 0:
            for ref in (dwq, dbqkv, dscore):
                ref[...] = jnp.zeros_like(ref)

    def two(m):
        if m >= 2:
            wait(fetch(m))
            big.start_two(m, matrices[m], lambda z: own1.at[m - 2, z])
        else:
            big.start_two(m, matrices[m], lambda z: big.rows_of(matrices[m], z, big.core))

    def table():
        chunks = -(-((2 * window - 1) ** 2) // 128)
        table_sum(places_ref, dscores, early.mine, early.mine.shape[0] - heads * chunks, heads, chunks)
        early.start_one()

    plan = {
        (0, 2): [(two, 2), (two, 3)],
        (0, 4): [(two, 4), (two, 5)],
        (1, 0): [(flush, 0), (big.start_three, 2), (big.start_three, 3)],
        (1, 1): [(two, 0)],
        (1, 4): [(big.start_three, 4), (big.start_three, 5), (big.start_four, 2), (big.start_four, 3)],
        (2, 0): [(flush, 1), (big.start_three, 0)],
        (2, 1): [(two, 1)],
        (2, 5): [(big.start_four, 4), (big.start_four, 5), (big.start_four, 0)],
    }
    for (at_sweep, at_step), acts in plan.items():

        @pl.when(moment(at_sweep, at_step))
        def _():
            for act, m in acts:
                act(m)

    @pl.when(sweep < 2)
    def _():
        for w in range(QUAD):
            gbp[SLOT * w : SLOT * w + slots, :] = gf_ref[slots * w : slots * w + slots, :].astype(B16)
        mine = pl.ds(pl.multiple_of(jnp.minimum(sweep, 1) * part_rows, part_rows), part_rows)
        datt[...] = dot(wproj_ref[mine, :], gbp[...], "NT").astype(B16)

        @pl.when(sweep == 0)
        def _():
            dwp[...] += dot(att_ref[...], gbp[...])

        ratio = size_head**-0.5
        target = dqkv.at[step, jnp.minimum(sweep, 1)]

        def score(w, g):
            low = pair * g
            lanes = slice(SLOT * w, SLOT * w + SLOT)
            for j in range(2):
                at = slice(low + size_head * j, low + size_head * (j + 1))
                cols = slice(SLOT * j, SLOT * j + SLOT)
                bdo[w % 3, at, cols] = datt[at, lanes]
                bdq[w % 3, at, cols] = qkv_ref[0, at, lanes]
                bdk[w % 3, at, cols] = qkv_ref[1, at, lanes]
            values = qkv_ref[2, low : low + pair, SLOT * w : SLOT * w + KEYS]
            dprobs[w % 2, g] = dot(values, bdo[w % 3, low : low + pair, :], "TN")

        def soften(w, g):
            probs = probs_ref[w, g, :KEYS, :].astype(F32)
            term = probs * dprobs[w % 2, g]
            grad = term - probs * jnp.sum(term, axis=0, keepdims=True)
            low_grad = grad.astype(B16)
            beside[w % 2, g, :KEYS, :] = low_grad
            for j in range(2):
                cols = slice(SLOT * j, SLOT * j + SLOT)
                dscore[2 * g + j] += grad[:, cols]
                stacked[w % 2, g, SLOT * j : SLOT * j + KEYS, :] = low_grad[:, cols]

        def attend(w, g):
            low = pair * g
            lanes = slice(SLOT * w, SLOT * w + SLOT)
            rows = slice(low, low + pair)
            got = dot(bdk[w % 3, rows, :], stacked[w % 2, g]) * ratio
            target[low : low + pair, lanes] = got.astype(B16)
            got = dot(bdq[w % 3, rows, :], beside[w % 2, g], "NT") * (1.0 / LOG2E)
            target[part_rows + low : part_rows + low + pair, lanes] = got.astype(B16)
            got = dot(bdo[w % 3, rows, :], probs_ref[w, g], "NT")
            target[2 * part_rows + low : 2 * part_rows + low + pair, lanes] = got.astype(B16)

        for stage in range(QUAD + 2):
            for g in range(pairs):
                if stage < QUAD:
                    score(stage, g)
                if 1 <= stage <= QUAD:
                    soften(stage - 1, g)
                if stage >= 2:
                    attend(stage - 2, g)

        grad = target[...]
        dwq[...] += dot(grad, n1_ref[...])
        wide = grad.astype(F32)
        both = wide[:, :SLOT]
        for w in range(1, QUAD):
            both = both + wide[:, SLOT * w : SLOT * w + SLOT]
        dbqkv[...] += both

    @pl.when(sweep == 2)
    def _():
        dn1 = dot(dqkv[step, 0], turned_ref[0], "TN") + dot(dqkv[step, 1], turned_ref[1], "TN")
        for w in range(QUAD):
            compact[slots * w : slots * w + slots, :] = dn1[SLOT * w : SLOT * w + slots, :]
        grad = compact[...]
        xhat, spread = norm_stats(x_ref[...].astype(F32))
        scaled = grad * gains_ref[0:1, :]
        mean_one = jnp.mean(scaled, axis=-1, keepdims=True)
        mean_two = jnp.mean(scaled * xhat, axis=-1, keepdims=True)
        compact[...] = gf_ref[...] + spread * (scaled - mean_one - xhat * mean_two)
        for w in range(QUAD):
            for r in range(window):
                ref, skip = piece(band, r, quad * QUAD * window, w, window, half)
                at = slots * w + window * r
                ref[skip : skip + window, :] = compact[at : at + window, :]

    for p in range(pages):
        for j in range(quads):

            @pl.when(moment(2, p * quads + j))
            def _():
                cut = slice(edge_at(j), edge_at(j + 1))
                edge[p, :, cut, :] = band[half:, cut, :].astype(B16)
                patch_copy(p, j).start()
                if j == quads - 1:
                    unwrap_band(band, live, half, width, window, least)
                    own_ref[0] = band[:half, :width].astype(B16)

    @pl.when(moment(2, pages * quads - 1))
    def _():
        table()
        big.start_three(1)
        early.start_two()
        for m in outer:
            big.finish(m, sum_ref.at[m])
        big.finish(0, sum_ref.at[0])
        early.start_three()
        big.start_four(1)
        mixed_copy().wait()
        early.finish(early.mine, 0)
        top = small_ref.shape[0]
        small_ref[...] = early.mine[:top]
        for c in range(table_ref.shape[0] // 128):
            table_ref[128 * c : 128 * c + 128, :] = early.mine[top + heads * c : top + heads * (c + 1), :].T
        big.finish(1, sum_ref.at[1])
        for p in range(pages):
            for j in range(quads):
                patch_copy(p, j).wait()


def attn_backward(
    live, dwup, dwout, mixed_next, gf, x, n1, qkv, probs, att, weights_in, turned, gains, biases, places, early, shape, heads, least, share
):
    pages, window, width, model = shape
    half = window // 2
    quads = width // window // QUAD
    slots = window * window
    pairs = heads // 4
    part_rows = model // 2
    devices = (lax.axis_size("page"), lax.axis_size("rows"))
    chips = devices[1] // 2
    hidden = dwup.shape[1]
    wide = 2 * model
    cols = wide // devices[0]
    once = pl.Buffered(1)
    whole = lambda a: pl.BlockSpec(a.shape, lambda s, p, j: (0,) * a.ndim, pipeline_mode=once)
    held = lambda dims: pl.BlockSpec(dims, lambda s, p, j: (0,) * len(dims), pipeline_mode=once)
    anywhere = pl.BlockSpec(memory_space=pl.ANY)
    at = lambda p, j: p * quads + j
    last = pages * quads - 1
    both = lambda s, p, j: jnp.where(s < 2, at(p, j), last)
    first = lambda s, p, j: jnp.where(s == 0, at(p, j), last)
    third = lambda s, p, j: jnp.where(s == 2, at(p, j), 0)
    side = lambda s: jnp.minimum(s, 1)
    own_at = lambda s, p, j: (jnp.where(s == 2, p, 0), 0, 0, 0)
    dma = pltpu.SemaphoreType.DMA
    vmem = pltpu.VMEM
    n = 2 + 2 * hidden // wide
    lines = early.shape[0]
    chunks = -(-((2 * window - 1) ** 2) // 128)

    def small_scratch(rows):
        return [
            vmem((rows, 128), F32),
            vmem((rows, 128), F32),
            vmem((rows, 128), F32),
            vmem((devices[0], rows, 128), F32),
            vmem((rows, 128), F32),
            vmem((chips, rows, 128), F32),
            dma((devices[0] + chips,)),
            dma((devices[0] + chips,)),
        ]

    return pl.pallas_call(
        functools.partial(
            attn_backward_kernel, (window, half, width, model, heads, least, pages, devices, share)
        ),
        grid=(3, pages, quads),
        in_specs=[
            pl.BlockSpec(memory_space=pltpu.SMEM),
            anywhere,
            anywhere,
            anywhere,
            pl.BlockSpec((QUAD * slots, model), lambda s, p, j: (at(p, j), 0)),
            pl.BlockSpec((QUAD * slots, model), lambda s, p, j: (third(s, p, j), 0)),
            pl.BlockSpec((QUAD * SLOT, model), lambda s, p, j: (both(s, p, j), 0)),
            pl.BlockSpec((3, part_rows, QUAD * SLOT), lambda s, p, j: (0, side(s), both(s, p, j))),
            pl.BlockSpec((QUAD, pairs, SLOT, 2 * SLOT), lambda s, p, j: (both(s, p, j), side(s), 0, 0)),
            pl.BlockSpec((model, QUAD * SLOT), lambda s, p, j: (0, first(s, p, j))),
            pl.BlockSpec((model, model), lambda s, p, j: (0, 3), pipeline_mode=once),
            whole(turned),
            whole(gains),
            whole(biases),
            whole(places),
            whole(early),
        ],
        out_specs=[
            held((n, share, wide)),
            held((lines - chunks * heads, 128)),
            held((128 * chunks, heads)),
            pl.BlockSpec((1, half, width, model), own_at),
            anywhere,
            anywhere,
        ],
        out_shape=[
            jax.ShapeDtypeStruct((n, share, wide), B16),
            jax.ShapeDtypeStruct((lines - chunks * heads, 128), F32),
            jax.ShapeDtypeStruct((128 * chunks, heads), F32),
            jax.ShapeDtypeStruct((pages, half, width, model), B16),
            jax.ShapeDtypeStruct((pages, half, width, model), B16),
            jax.ShapeDtypeStruct((pages, half, width + 8, model), B16),
        ],
        scratch_shapes=[
            vmem((window, width + 8, model), F32),
            vmem((QUAD * SLOT, model), B16),
            vmem((part_rows, QUAD * SLOT), B16),
            vmem((2, pairs, KEYS, 2 * SLOT), F32),
            vmem((3, part_rows, 2 * SLOT), B16),
            vmem((3, part_rows, 2 * SLOT), B16),
            vmem((3, part_rows, 2 * SLOT), B16),
            vmem((2, pairs, 2 * SLOT, SLOT), B16),
            vmem((2, pairs, SLOT, 2 * SLOT), B16),
            vmem((pages * quads, 2, 3 * part_rows, QUAD * SLOT), B16),
            vmem((3 * part_rows, model), F32),
            vmem((model, model), F32),
            vmem((QUAD * slots, model), F32),
            vmem((heads // 2, KEYS, SLOT), F32),
            vmem((heads, KEYS, SLOT), F32),
            vmem((3 * part_rows, SLOT), F32),
            vmem((8, model), F32),
            vmem((2, model, wide), B16),
            vmem((pages, half, width + 8, model), B16),
            vmem((n - 2, chips, share, wide), B16),
            vmem((n, chips, share, wide), B16),
            vmem((n, devices[0], chips, share, cols), B16),
            vmem((n, devices[0], chips, share, cols), B16),
            vmem((n, chips, share, cols), B16),
            vmem((n, chips, share, cols), B16),
            vmem((n, share, cols), B16),
            vmem((n, devices[0], share, cols), B16),
            dma((n, chips)),
            dma((n, chips)),
            dma((n, devices[0])),
            dma((n, devices[0])),
            dma((n, chips)),
            dma((n, chips)),
            dma((n, devices[0])),
            dma((n, devices[0])),
        ]
        + small_scratch(lines)
        + [dma((n - 2, chips)), dma((1 + pages * quads,)), dma((1 + pages * quads,))],
        compiler_params=pltpu.CompilerParams(
            vmem_limit_bytes=62 * 2**20, collective_id=0, has_side_effects=True
        ),
    )(live, dwup, dwout, mixed_next, gf, x, n1, qkv, probs, att, weights_in, turned, gains, biases, places, early)


def finish_kernel(
    sizes,
    live_ref,
    sum_hbm,
    min_hbm,
    fin_hbm,
    sin_hbm,
    mout_hbm,
    fout_hbm,
    sout_hbm,
    above_ref,
    own_ref,
    edge_hbm,
    _,
    mixed_ref,
    patch_ref,
    new_in_ref,
    moment_in_ref,
    square_in_ref,
    new_out_ref,
    moment_out_ref,
    square_out_ref,
    sums,
    olds_in,
    news_in,
    olds_out,
    news_out,
    edges,
    tops,
    passed,
    band,
    sems,
    frame_sems,
    in_sems,
    out_sems,
):
    window, half, width, least = sizes
    model = band.shape[2]
    part_rows = model // 2
    share = sums.shape[1]
    pages = edges.shape[0]
    pieces = olds_in.shape[2] // (2 * model)
    tall = olds_out.shape[1] // pieces

    def cut(ref, k):
        return ref.at[:, pl.ds(2 * model * k, 2 * model)]

    def stripe(ref, k):
        return ref.at[pl.ds(tall * k, tall), :]

    copy = pltpu.make_async_copy
    passing = [copy(above_ref, passed.at[0], sems.at[2]), copy(own_ref, passed.at[1], sems.at[3])]
    framed = [
        copy(passed.at[0], mixed_ref.at[:, pl.ds(0, half)], frame_sems.at[0]),
        copy(passed.at[1], patch_ref.at[:, pl.ds(half, half)], frame_sems.at[1]),
    ]
    fetched = [copy(sum_hbm, sums, sems.at[0]), copy(edge_hbm, edges, sems.at[1])]
    laid = copy(tops, patch_ref.at[:, pl.ds(0, half)], frame_sems.at[2])
    ins, outs = [], []
    for k in range(pieces):
        for i, (src, dst) in enumerate(zip((min_hbm, fin_hbm, sin_hbm), (new_in_ref, moment_in_ref, square_in_ref))):
            ins.append(copy(cut(src, k), cut(olds_in.at[i], k), in_sems.at[6 * k + i]))
            outs.append(copy(cut(news_in.at[i], k), cut(dst, k), out_sems.at[6 * k + i]))
        for i, (src, dst) in enumerate(zip((mout_hbm, fout_hbm, sout_hbm), (new_out_ref, moment_out_ref, square_out_ref))):
            ins.append(copy(stripe(src, k), stripe(olds_out.at[i], k), in_sems.at[6 * k + 3 + i]))
            outs.append(copy(stripe(news_out.at[i], k), stripe(dst, k), out_sems.at[6 * k + 3 + i]))
    start(fetched)
    start(ins[:6])
    start(passing)
    start(ins[6:])
    wait(fetched)
    for p in range(pages):
        band[...] = edges[p].astype(F32)
        unwrap_band(band, live_ref[p], half, width, window, least)
        tops[p] = band[:, :width].astype(B16)
    laid.start()
    wait(passing)
    start(framed)
    for k in range(pieces):
        wait(ins[6 * k : 6 * k + 6])
        at = slice(2 * model * k, 2 * model * (k + 1))
        if k < 2:
            grad = jnp.concatenate(
                [
                    sums[h, :, (2 * k + part) * part_rows : (2 * k + part + 1) * part_rows]
                    for part in range(2)
                    for h in range(2)
                ],
                axis=1,
            )
        else:
            grad = sums[k]
        updated = adam_update(olds_in[0, :, at], olds_in[1, :, at], olds_in[2, :, at], grad.astype(F32))
        for i in range(3):
            news_in[i, :, at] = updated[i]
        start(outs[6 * k : 6 * k + 3])
        rows = slice(tall * k, tall * (k + 1))
        grad = sums[4 + k // 2, :, model * (k % 2) : model * (k % 2 + 1)]
        updated = adam_update(olds_out[0, rows], olds_out[1, rows], olds_out[2, rows], grad.astype(F32))
        for i in range(3):
            news_out[i, rows] = updated[i]
        start(outs[6 * k + 3 : 6 * k + 6])
    wait(framed)
    wait(outs)
    laid.wait()


def finish(live, sums, master_in, first_in, second_in, master_out, first_out, second_out, above, own, edge, mixed, least):
    pages, window, width, model = mixed.shape
    half = window // 2
    pieces = master_in.shape[1] // (2 * model)
    anywhere = pl.BlockSpec(memory_space=pl.ANY)
    like = lambda a: jax.ShapeDtypeStruct(a.shape, a.dtype)
    dma = pltpu.SemaphoreType.DMA
    return pl.pallas_call(
        functools.partial(finish_kernel, (window, half, width, least)),
        in_specs=[pl.BlockSpec(memory_space=pltpu.SMEM)] + [anywhere] * 11,
        out_specs=[anywhere] * 8,
        out_shape=[like(mixed), like(mixed)] + [like(master_in)] * 3 + [like(master_out)] * 3,
        scratch_shapes=[
            pltpu.VMEM(sums.shape, B16),
            pltpu.VMEM((3,) + master_in.shape, F32),
            pltpu.VMEM((3,) + master_in.shape, F32),
            pltpu.VMEM((3,) + master_out.shape, F32),
            pltpu.VMEM((3,) + master_out.shape, F32),
            pltpu.VMEM(edge.shape, B16),
            pltpu.VMEM(above.shape, B16),
            pltpu.VMEM((2,) + above.shape, B16),
            pltpu.VMEM((half, width + 8, model), F32),
            dma((4,)),
            dma((3,)),
            dma((6 * pieces,)),
            dma((6 * pieces,)),
        ],
        input_output_aliases={11: 0},
        compiler_params=pltpu.CompilerParams(vmem_limit_bytes=VMEM_LIMIT),
    )(live, sums, master_in, first_in, second_in, master_out, first_out, second_out, above, own, edge, mixed)


def adam_update(master, first, second, grad):
    moment = BETA_ONE * first + (1.0 - BETA_ONE) * grad
    square = BETA_TWO * second + (1.0 - BETA_TWO) * grad * grad
    fix_one = 1.0 - BETA_ONE**STEP
    fix_two = 1.0 - BETA_TWO**STEP
    fresh = master - LEARN_RATE * (
        moment / fix_one / (jnp.sqrt(square / fix_two) + ADAM_EPS) + WEIGHT_DECAY * master
    )
    return (fresh, moment, square)


def shards(
    patches,
    out_grad,
    page_windows,
    region_ids,
    offset_index,
    weights_in,
    weights_out,
    norm_gains,
    biases,
    bias_table,
    master_in,
    master_out,
    first_in,
    second_in,
    first_out,
    second_out,
    first_small,
    second_small,
):
    pages, window, width, model = patches.shape
    half = window // 2
    count = width // window
    least = (count + 1) // 2
    slots = window * window
    table_rows, heads = bias_table.shape
    hidden = weights_out.shape[0]

    bias_lines = biases.reshape(-1, 128)
    lines = model // 128
    table_lanes = -(-table_rows // 128) * 128
    early_lines = EARLY_UP * lines + hidden // 128 + table_lanes * heads // 128

    x, n1, qkv, probs, att, first, n2, below_grad, turned, places = attn_forward(
        page_windows, patches, out_grad, region_ids, offset_index, bias_table.T, weights_in, norm_gains, bias_lines, least
    )
    dwup, dwout, gf, mixed_own, mixed_next, early = mlp(
        page_windows, out_grad, below_grad, n2, first, weights_in, weights_out, norm_gains, bias_lines,
        least, master_in.shape[0], early_lines,
    )
    sums, small, total_table, patch_own, above, edge = attn_backward(
        page_windows, dwup, dwout, mixed_next, gf, x, n1, qkv, probs, att, weights_in, turned, norm_gains,
        bias_lines, places, early, patches.shape, heads, least, master_in.shape[0],
    )
    mixed, patch_grad, new_in, moment_in, square_in, new_out, moment_out, square_out = finish(
        page_windows, sums, master_in, first_in, second_in, master_out, first_out, second_out, above, patch_own,
        edge, mixed_own, least,
    )
    total_small = jnp.concatenate([small.reshape(-1), total_table[:table_rows].reshape(-1)])
    small_master = jnp.concatenate([norm_gains.reshape(-1), biases, bias_table.reshape(-1)])
    new_small, moment_small, square_small = adam_update(
        small_master, first_small, second_small, total_small
    )
    return (
        mixed,
        patch_grad,
        new_in,
        moment_in,
        square_in,
        new_out,
        moment_out,
        square_out,
        new_small,
        moment_small,
        square_small,
    )


def solution(mesh):
    return jax.shard_map(
        shards,
        mesh=mesh,
        in_specs=(
            P("page", "rows", None, None),
            P("page", "rows", None, None),
            P("page"),
            P("page", "rows", None),
            P(),
            P(),
            P(),
            P(),
            P(),
            P(),
            P("rows", None),
            P("rows", None),
            P("rows", None),
            P("rows", None),
            P("rows", None),
            P("rows", None),
            P(),
            P(),
        ),
        out_specs=(
            P("page", "rows", None, None),
            P("page", "rows", None, None),
            P("rows", None),
            P("rows", None),
            P("rows", None),
            P("rows", None),
            P("rows", None),
            P("rows", None),
            P(),
            P(),
            P(),
        ),
        check_vma=False,
    )
```

```python
import functools
import math

import jax
import jax.numpy as jnp
from jax import lax
from jax.experimental import pallas as pl
from jax.experimental.pallas import tpu as pltpu
from jax.sharding import PartitionSpec as P

STEP = 10
NORM_EPS = 1e-05
BETA_ONE = 0.9
BETA_TWO = 0.999
LEARN_RATE = 0.04
WEIGHT_DECAY = 0.05
ADAM_EPS = 1e-08
MASK_VALUE = -1000000000.0

F32 = jnp.float32
B16 = jnp.bfloat16
LOG2E = math.log2(math.e)
VMEM_LIMIT = 60 * 2**20

QUAD = 4
SLOT = 128
KEYS = 104


def dot(left, right, form="NN"):
    sides = {
        "NN": ((1,), (0,)),
        "NT": ((1,), (1,)),
        "TN": ((0,), (0,)),
    }[form]
    return lax.dot_general(left, right, (sides, ((), ())), preferred_element_type=F32)


def load_band(band, low_ref, high_ref, live, half, width, window, least, start=0, end=None):
    end = width if end is None else end
    band[:half, start:end] = low_ref[:, start:end].astype(F32)
    band[half:, start:end] = high_ref[:, start:end].astype(F32)
    if end == width:
        band[:, width:] = jnp.zeros((window, band.shape[1] - width, band.shape[2]), F32)
        for count in range(least, width // window + 1):
            at = slice(count * window, count * window + half)
            band[:, at] = jnp.where(live == count, band[:, :half], band[:, at])


def unwrap_band(band, live, half, width, window, least):
    front = band[:, :half]
    for count in range(least, width // window + 1):
        at = slice(count * window, count * window + half)
        front = jnp.where(live == count, band[:, at], front)
    band[:, :half] = front
    edge = least * window // 8 * 8
    shape = (band.shape[0], width - edge, band.shape[2])
    columns = lax.broadcasted_iota(jnp.int32, shape, 1) + edge
    band[:, edge:width] = jnp.where(columns < live * window, band[:, edge:width], 0.0)


def piece(band, row, base, place, window, half):
    start = window * place + half
    aligned = start // 8 * 8
    skip = start - aligned
    size = -(-(skip + window) // 8) * 8
    ref = band.at[row, pl.ds(pl.multiple_of(base, 8) + aligned, size), :]
    return ref, skip


def gather_window(band, base, place, window, half):
    parts = []
    for row in range(window):
        ref, skip = piece(band, row, base, place, window, half)
        parts.append(ref[skip : skip + window, :])
    return parts


def norm_stats(value):
    centre = jnp.mean(value, axis=-1, keepdims=True)
    centered = value - centre
    spread = lax.rsqrt(jnp.mean(centered * centered, axis=-1, keepdims=True) + NORM_EPS)
    return centered * spread, spread


def fold(value):
    rows, cols = value.shape
    return jnp.sum(value.reshape(rows // 8, 8, cols), axis=0)


MESH = pl.DeviceIdType.MESH


def remote(src, dst, send, recv, device):
    return pltpu.make_async_remote_copy(
        src_ref=src, dst_ref=dst, send_sem=send, recv_sem=recv, device_id=device, device_id_type=MESH
    )


def lay_lines(lines_ref, at, row):
    for i in range(row.shape[1] // 128):
        lines_ref[at + i : at + i + 1, :] = row[:, 128 * i : 128 * i + 128]


def lay_row(ref, row, lines_ref, at, count):
    for i in range(count):
        ref[row : row + 1, 128 * i : 128 * i + 128] = lines_ref[at + i : at + i + 1, :]


def attn_forward_kernel(
    sizes,
    live_ref,
    patches_ref,
    grads_ref,
    low_ref,
    label_ref,
    off_ref,
    tab_ref,
    wqkv_ref,
    wproj_ref,
    gains_ref,
    biases_ref,
    x_ref,
    n1_ref,
    qkv_ref,
    probs_ref,
    att_ref,
    first_ref,
    n2_ref,
    grad_halo_ref,
    turned_ref,
    places_ref,
    halo,
    send,
    recv,
    band,
    bias,
    scores,
    bdq,
    bdv,
    stacked,
    xs,
    ns,
    vecs,
    column,
    square,
    flat,
    marks,
):
    window, half, width, model, heads, least, pages, rows_count = sizes
    slots = window * window
    size_head = model // heads
    page, quad = pl.program_id(0), pl.program_id(1)
    live = live_ref[page]
    pairs = heads // 2
    part_rows = model // 2
    lines = model // 128
    row = lax.axis_index("rows")
    behind, ahead = lax.rem(row + rows_count - 1, rows_count), lax.rem(row + 1, rows_count)

    cut = -(-(QUAD * window + half) // 16) * 16

    def halo_copy(p, k):
        at = (pl.ds(0, cut), pl.ds(cut, width - cut))[k]
        return remote(
            patches_ref.at[p, pl.ds(0, half), at],
            halo.at[p, :, at],
            send.at[pages * (1 + k) + p],
            recv.at[pages * (1 + k) + p],
            {"rows": behind},
        )

    def grad_copy(p):
        return remote(
            grads_ref.at[p, pl.ds(0, half)],
            grad_halo_ref.at[p],
            send.at[p],
            recv.at[p],
            {"rows": behind},
        )

    @pl.when(jnp.logical_and(page == 0, quad == 0))
    def _():
        barrier = pltpu.get_barrier_semaphore()
        for neighbour in (behind, ahead):
            pl.semaphore_signal(barrier, inc=1, device_id={"rows": neighbour}, device_id_type=MESH)
        pl.semaphore_wait(barrier, 2)
        halo_copy(0, 0).start()
        vecs[...] = jnp.zeros_like(vecs)
        vecs[0:1, :] = gains_ref[0:1, :]
        lay_row(vecs, 1, biases_ref, 0, lines)
        lay_row(vecs, 2, biases_ref, 3 * lines, lines)
        vecs[3:4, :] = gains_ref[1:2, :]
        lay_row(vecs, 4, biases_ref, 4 * lines, lines)
        column[...] = jnp.zeros_like(column)
        for h in range(2):
            for part in range(3):
                rows = slice(part * part_rows, part * part_rows + part_rows)
                cols = slice(part * model + h * part_rows, part * model + (h + 1) * part_rows)
                turned_ref[h, rows, :] = wqkv_ref[:, cols].T
                if part != 1:
                    for i in range(part_rows // 128):
                        line = lines * (1 + part // 2) + h * (part_rows // 128) + i
                        spread = jnp.broadcast_to(biases_ref[line : line + 1, :], (128, 128))
                        at = part * part_rows + 128 * i
                        column[h, at : at + 128, :] = spread.T
        halo_copy(0, 1).start()
        square[...] = jnp.full_like(square, -1)
        square[:slots, :slots] = off_ref[...]
        places = square[...].T[:KEYS]
        places_ref[...] = places
        off = jnp.maximum(places, 0)
        flat[...] = jnp.zeros_like(flat)
        flat[:, : tab_ref.shape[1]] = tab_ref[...] * LOG2E
        low, high = jnp.bitwise_and(off, 127), jnp.right_shift(off, 7)
        for h in range(heads):
            got = jnp.zeros((KEYS, SLOT), F32)
            for c in range(flat.shape[1] // 128):
                source = jnp.broadcast_to(flat[h : h + 1, 128 * c : 128 * c + 128], (KEYS, SLOT))
                picked = jnp.take_along_axis(source, low, axis=1, mode="promise_in_bounds")
                got = jnp.where(high == c, picked, got)
            bias[h] = got
        bdq[...] = jnp.zeros_like(bdq)
        bdv[...] = jnp.zeros_like(bdv)
        stacked[...] = jnp.zeros_like(stacked)

    for p in range(pages):

        @pl.when(jnp.logical_and(page == p, quad == 0))
        def _():
            halo_copy(p, 0).wait()
            load_band(band, low_ref.at[0], halo.at[p], live, half, width, window, least, 0, cut)

        @pl.when(jnp.logical_and(page == p, quad == 1))
        def _():
            halo_copy(p, 1).wait()
            if p + 1 < pages:
                for k in range(2):
                    halo_copy(p + 1, k).start()
            load_band(band, low_ref.at[0], halo.at[p], live, half, width, window, least, cut)

    @pl.when(jnp.logical_and(page == (pages - 1) // 2, quad == 2))
    def _():
        for p in range(pages):
            grad_copy(p).start()

    @pl.when(jnp.logical_and(page == pages - 1, quad == pl.num_programs(1) - 1))
    def _():
        for p in range(pages):
            grad_copy(p).wait()

    base = quad * (QUAD * window)
    for w in range(QUAD):
        for r, part in enumerate(gather_window(band, base, w, window, half)):
            at = slots * w + window * r
            xs[at : at + window, :] = part
    x = xs[...]
    x_ref[...] = x.astype(B16)
    xhat, _ = norm_stats(x)
    ns[...] = xhat * vecs[0:1, :] + vecs[1:2, :]
    for w in range(QUAD):
        n1_ref[SLOT * w : SLOT * w + slots, :] = ns[slots * w : slots * w + slots, :].astype(B16)
        n1_ref[SLOT * w + slots : SLOT * w + SLOT, :] = jnp.zeros((SLOT - slots, model), B16)
    scale = size_head**-0.5 * LOG2E
    n1 = n1_ref[...]
    for h in range(2):
        got = dot(turned_ref[h], n1, "NT") + column[h, :, 0:1]
        at = slice(h * part_rows, h * part_rows + part_rows)
        qkv_ref[0, at, :] = (got[:part_rows] * scale).astype(B16)
        qkv_ref[1, at, :] = got[part_rows : 2 * part_rows].astype(B16)
        qkv_ref[2, at, :] = got[2 * part_rows :].astype(B16)

    sames = []
    lane = lax.broadcasted_iota(jnp.int32, (1, SLOT), 1)
    for j in range(width // window // QUAD):

        @pl.when(quad == j)
        def _():
            at = QUAD * window * j
            marks[:, : QUAD * window] = label_ref[0, :, at : at + QUAD * window].astype(F32)

    for w in range(QUAD):
        label = jnp.full((1, SLOT), -1.0, F32)
        for r in range(window):
            turned = pltpu.roll(marks[r : r + 1, :], (window * (r - w)) % SLOT, 1)
            here = jnp.logical_and(lane >= window * r, lane < window * (r + 1))
            label = jnp.where(here, turned, label)
        spread = jnp.broadcast_to(label, (SLOT, SLOT))
        sames.append((spread == spread.T)[:KEYS])
    pair = 2 * size_head

    def score(w, g):
        low = pair * g
        lanes = slice(SLOT * w, SLOT * w + SLOT)
        for j in range(2):
            at = slice(low + size_head * j, low + size_head * (j + 1))
            cols = slice(SLOT * j, SLOT * j + SLOT)
            bdq[w % 2, at, cols] = qkv_ref[0, at, lanes]
            bdv[w % 3, at, cols] = qkv_ref[2, at, lanes]
        keys = qkv_ref[1, low : low + pair, SLOT * w : SLOT * w + KEYS]
        scores[w % 2, g] = dot(keys, bdq[w % 2, low : low + pair, :], "TN")

    def soften(w, g):
        for j in range(2):
            cols = slice(SLOT * j, SLOT * j + SLOT)
            s = jnp.where(sames[w], scores[w % 2, g, :, cols] + bias[2 * g + j], MASK_VALUE)
            s = jnp.exp2(s - jnp.max(s, axis=0, keepdims=True))
            low_probs = (s * (1.0 / jnp.sum(s, axis=0, keepdims=True))).astype(B16)
            probs_ref[w, g, :KEYS, cols] = low_probs
            probs_ref[w, g, KEYS:, cols] = jnp.zeros((SLOT - KEYS, SLOT), B16)
            stacked[w % 2, g, SLOT * j : SLOT * j + KEYS, :] = low_probs

    def attend(w, g):
        low = pair * g
        got = dot(bdv[w % 3, low : low + pair, :], stacked[w % 2, g])
        att_ref[low : low + pair, SLOT * w : SLOT * w + SLOT] = got.astype(B16)

    for step in range(QUAD + 2):
        for g in range(pairs):
            if step < QUAD:
                score(step, g)
            if 1 <= step <= QUAD:
                soften(step - 1, g)
            if step >= 2:
                attend(step - 2, g)

    branch = dot(att_ref[...], wproj_ref[...], "TN")
    for w in range(QUAD):
        rows = slice(slots * w, slots * w + slots)
        first_ref[rows, :] = xs[rows, :] + branch[SLOT * w : SLOT * w + slots, :] + vecs[2:3, :]
    xhat, _ = norm_stats(first_ref[...])
    n2_ref[...] = (xhat * vecs[3:4, :] + vecs[4:5, :]).astype(B16)


def attn_forward(live, patches, out_grad, labels, off, tab, weights_in, gains, biases, least):
    pages, window, width, model = patches.shape
    half = window // 2
    heads, table_rows = tab.shape
    table_lanes = -(-table_rows // 128) * 128
    quads = width // window // QUAD
    tokens = pages * window * width
    slots = window * window
    padded = pages * quads * QUAD * SLOT
    steps = (pages, quads)
    whole = lambda a: pl.BlockSpec(a.shape, lambda p, j: (0,) * a.ndim, pipeline_mode=pl.Buffered(1))
    at = lambda p, j: p * quads + j
    return pl.pallas_call(
        functools.partial(
            attn_forward_kernel,
            (window, half, width, model, heads, least, pages, lax.axis_size("rows")),
        ),
        grid=steps,
        in_specs=[
            pl.BlockSpec(memory_space=pltpu.SMEM),
            pl.BlockSpec(memory_space=pl.ANY),
            pl.BlockSpec(memory_space=pl.ANY),
            pl.BlockSpec((1, half, width, model), lambda p, j: (p, 1, 0, 0)),
            pl.BlockSpec((1, window, width), lambda p, j: (p, 0, 0)),
            whole(off),
            whole(tab),
            pl.BlockSpec((model, 3 * model), lambda p, j: (0, 0), pipeline_mode=pl.Buffered(1)),
            pl.BlockSpec((model, model), lambda p, j: (0, 3), pipeline_mode=pl.Buffered(1)),
            whole(gains),
            whole(biases),
        ],
        out_specs=[
            pl.BlockSpec((QUAD * slots, model), lambda p, j: (at(p, j), 0)),
            pl.BlockSpec((QUAD * SLOT, model), lambda p, j: (at(p, j), 0)),
            pl.BlockSpec((3, model, QUAD * SLOT), lambda p, j: (0, 0, at(p, j))),
            pl.BlockSpec((QUAD, heads // 2, SLOT, 2 * SLOT), lambda p, j: (at(p, j), 0, 0, 0)),
            pl.BlockSpec((model, QUAD * SLOT), lambda p, j: (0, at(p, j))),
            pl.BlockSpec((QUAD * slots, model), lambda p, j: (at(p, j), 0)),
            pl.BlockSpec((QUAD * slots, model), lambda p, j: (at(p, j), 0)),
            pl.BlockSpec(memory_space=pl.ANY),
            pl.BlockSpec((2, 3 * model // 2, model), lambda p, j: (0, 0, 0), pipeline_mode=pl.Buffered(1)),
            pl.BlockSpec((KEYS, SLOT), lambda p, j: (0, 0)),
        ],
        out_shape=[
            jax.ShapeDtypeStruct((tokens, model), B16),
            jax.ShapeDtypeStruct((padded, model), B16),
            jax.ShapeDtypeStruct((3, model, padded), B16),
            jax.ShapeDtypeStruct((pages * quads * QUAD, heads // 2, SLOT, 2 * SLOT), B16),
            jax.ShapeDtypeStruct((model, padded), B16),
            jax.ShapeDtypeStruct((tokens, model), F32),
            jax.ShapeDtypeStruct((tokens, model), B16),
            jax.ShapeDtypeStruct((pages, half, width, model), B16),
            jax.ShapeDtypeStruct((2, 3 * model // 2, model), B16),
            jax.ShapeDtypeStruct((KEYS, SLOT), jnp.int32),
        ],
        scratch_shapes=[
            pltpu.VMEM((pages, half, width, model), B16),
            pltpu.SemaphoreType.DMA((3 * pages,)),
            pltpu.SemaphoreType.DMA((3 * pages,)),
            pltpu.VMEM((window, width + 8, model), F32),
            pltpu.VMEM((heads, KEYS, SLOT), F32),
            pltpu.VMEM((2, heads // 2, KEYS, 2 * SLOT), F32),
            pltpu.VMEM((2, model, 2 * SLOT), B16),
            pltpu.VMEM((3, model, 2 * SLOT), B16),
            pltpu.VMEM((2, heads // 2, 2 * SLOT, SLOT), B16),
            pltpu.VMEM((QUAD * slots, model), F32),
            pltpu.VMEM((QUAD * slots, model), F32),
            pltpu.VMEM((8, model), F32),
            pltpu.VMEM((2, 3 * model // 2, 128), F32),
            pltpu.VMEM((SLOT, SLOT), jnp.int32),
            pltpu.VMEM((heads, table_lanes), F32),
            pltpu.VMEM((window, SLOT), F32),
        ],
        compiler_params=pltpu.CompilerParams(
            vmem_limit_bytes=VMEM_LIMIT, collective_id=1, has_side_effects=True
        ),
    )(live, patches, out_grad, patches, labels, off, tab, weights_in, weights_in, gains, biases)


MLP_COLS = 1024
MLP_CHUNKS = 2
MLP_ROWS = 800
EARLY_UP = 8


def mlp_kernel(
    sizes,
    live_ref,
    low_ref,
    high_ref,
    n2_ref,
    first_hbm,
    wup_ref,
    wout_ref,
    gains_ref,
    biases_ref,
    dwup_ref,
    dwout_ref,
    gf_hbm,
    own_hbm,
    next_hbm,
    early_ref,
    bup,
    vecs,
    sums,
    band,
    cot,
    res,
    dn2,
    act_all,
    pre_all,
    first_ref,
    held,
    frames,
    first_sem,
    gf_sems,
    frame_sems,
):
    window, half, width, model, least, share = sizes
    pages = low_ref.shape[0]
    slots = window * window
    count = width // window
    quads = count // QUAD
    chunk = pl.program_id(0)
    tokens = n2_ref.shape[0]
    cols = wup_ref.shape[1]
    lines = model // 128

    for c in range(MLP_CHUNKS):

        @pl.when(chunk == c)
        def _():
            lay_row(bup, 0, biases_ref, 6 * lines + c * (cols // 128), cols // 128)

    first_copy = pltpu.make_async_copy(first_hbm, first_ref, first_sem)

    def gf_copy(k):
        rows = pl.ds(pl.multiple_of(k * QUAD * slots, 16), QUAD * slots)
        return pltpu.make_async_copy(dn2.at[rows, :], gf_hbm.at[rows, :], gf_sems.at[k])

    def frame_copies(page):
        return [
            pltpu.make_async_copy(frames.at[page, 0], own_hbm.at[page, pl.ds(half, half)], frame_sems.at[page, 0]),
            pltpu.make_async_copy(frames.at[page, 1], next_hbm.at[page], frame_sems.at[page, 1]),
        ]

    @pl.when(chunk == 0)
    def _():
        first_copy.start()
        early_ref[...] = jnp.zeros_like(early_ref)
        vecs[0:1, :] = gains_ref[1:2, :]
        lay_row(vecs, 1, biases_ref, 5 * lines, lines)
        for page in range(pages):
            live = live_ref[page]
            load_band(band, low_ref.at[page], high_ref.at[page], live, half, width, window, least)

            def body(j, carry):
                for w in range(QUAD):
                    alive = jnp.where(j * QUAD + w < live, 1.0, 0.0)
                    for r, part in enumerate(gather_window(band, j * QUAD * window, w, window, half)):
                        at = slots * w + window * r
                        held[at : at + window, :] = part * alive
                rows = pl.ds(pl.multiple_of((page * quads + j) * QUAD * slots, 16), QUAD * slots)
                cot[rows, :] = held[...].astype(B16)
                return carry

            lax.fori_loop(0, quads, body, 0)

    def body(i, total):
        rows = pl.ds(pl.multiple_of(i * MLP_ROWS, 16), MLP_ROWS)
        grad = cot[rows, :]
        pre = dot(n2_ref[rows, :], wup_ref[...]) + bup[0:1, :]
        grad_act = dot(grad, wout_ref[...], "NT")
        share = 0.5 * (1.0 + lax.erf(pre * 0.5**0.5))
        act = (pre * share).astype(B16)
        slope = share + pre * (jnp.exp2((-0.5 * LOG2E) * pre * pre) * (2.0 * math.pi) ** -0.5)
        grad_pre = (grad_act * slope).astype(B16)
        act_all[rows, :] = act
        pre_all[rows, :] = grad_pre
        up = dot(act, wout_ref[...])
        down = dot(grad_pre, wup_ref[...], "NT")

        res[rows, :] = jnp.where(chunk == 0, 0.0, res[rows, :]) + up
        dn2[rows, :] = jnp.where(chunk == 0, 0.0, dn2[rows, :]) + down
        return total + fold(grad_pre.astype(F32))

    total = lax.fori_loop(0, tokens // MLP_ROWS, body, jnp.zeros((8, cols), F32))
    total = jnp.sum(total, axis=0, keepdims=True)
    for c in range(MLP_CHUNKS):

        @pl.when(chunk == c)
        def _():
            lay_lines(early_ref, EARLY_UP * lines + c * (cols // 128), total)

    grad_out = dot(act_all[...], cot[...], "TN").astype(B16)
    for s in range(dwout_ref.shape[0] // share):
        for a in range(dwout_ref.shape[1] // model):
            at = (s * (dwout_ref.shape[1] // model) + a) * share
            dwout_ref[share * s : share * s + share, model * a : model * a + model] = grad_out[at : at + share, :]
    dwup_ref[...] = dot(n2_ref[...], pre_all[...], "TN").astype(B16)

    @pl.when(chunk == pl.num_programs(0) - 1)
    def _():
        sums[...] = jnp.zeros_like(sums)
        first_copy.wait()
        for page in range(pages):
            live = live_ref[page]

            def body(j, carry):
                at = pl.multiple_of((page * quads + j) * QUAD * slots, 16)
                rows = pl.ds(at, QUAD * slots)
                first = first_ref[rows, :]
                res[rows, :] += first + vecs[1:2, :]
                xhat, spread = norm_stats(first)
                grad = dn2[rows, :]
                given = cot[rows, :].astype(F32)
                scaled = grad * vecs[0:1, :]
                mean_one = jnp.mean(scaled, axis=-1, keepdims=True)
                mean_two = jnp.mean(scaled * xhat, axis=-1, keepdims=True)
                whole = given + spread * (scaled - mean_one - xhat * mean_two)
                dn2[rows, :] = whole
                gf_copy(page * quads + j).start()
                sums[0:8, :] += fold(grad * xhat)
                sums[8:16, :] += fold(whole)
                sums[16:24, :] += fold(grad)
                sums[24:32, :] += fold(given)
                for w in range(QUAD):
                    for r in range(window):
                        ref, skip = piece(band, r, j * QUAD * window, w, window, half)
                        ref[skip : skip + window, :] = res[
                            pl.ds(at + slots * w // 8 * 8, slots + 4), :
                        ][slots * w % 8 + window * r : slots * w % 8 + window * r + window, :]
                return carry

            lax.fori_loop(0, quads, body, 0)
            unwrap_band(band, live, half, width, window, least)
            frames[page, 0] = band[:half, :width].astype(B16)
            frames[page, 1] = band[half:, :width].astype(B16)
            start(frame_copies(page))
        for k, place in enumerate((1, 5, 6, 7)):
            lay_lines(early_ref, place * lines, jnp.sum(sums[8 * k : 8 * k + 8, :], axis=0, keepdims=True))
        for k in range(pages * quads):
            gf_copy(k).wait()
        for page in range(pages):
            wait(frame_copies(page))


def mlp(live, out_grad, halo, n2, first, weights_in, weights_out, gains, biases, least, share, lines):
    pages, window, width, model = out_grad.shape
    half = window // 2
    tokens = n2.shape[0]
    hidden = weights_out.shape[0]
    skip = (weights_in.shape[1] - hidden) // MLP_COLS
    once = pl.Buffered(1)
    whole = lambda a: pl.BlockSpec(a.shape, lambda c: (0,) * a.ndim, pipeline_mode=once)
    band_block = (pages, half, width, model)
    return pl.pallas_call(
        functools.partial(mlp_kernel, (window, half, width, model, least, share)),
        grid=(hidden // MLP_COLS,),
        in_specs=[
            pl.BlockSpec(memory_space=pltpu.SMEM),
            pl.BlockSpec(band_block, lambda c: (0, 1, 0, 0), pipeline_mode=once),
            pl.BlockSpec(band_block, lambda c: (0, 0, 0, 0), pipeline_mode=once),
            whole(n2),
            pl.BlockSpec(memory_space=pl.ANY),
            pl.BlockSpec((model, MLP_COLS), lambda c: (0, c + skip)),
            pl.BlockSpec((MLP_COLS, model), lambda c: (c, 0)),
            whole(gains),
            whole(biases),
        ],
        out_specs=[
            pl.BlockSpec((model, MLP_COLS), lambda c: (0, c)),
            pl.BlockSpec((model * MLP_COLS // hidden, hidden), lambda c: (c, 0)),
            pl.BlockSpec(memory_space=pl.ANY),
            pl.BlockSpec(memory_space=pl.ANY),
            pl.BlockSpec(memory_space=pl.ANY),
            pl.BlockSpec((lines, 128), lambda c: (0, 0)),
        ],
        out_shape=[
            jax.ShapeDtypeStruct((model, hidden), B16),
            jax.ShapeDtypeStruct((model, hidden), B16),
            jax.ShapeDtypeStruct((tokens, model), F32),
            jax.ShapeDtypeStruct(out_grad.shape, B16),
            jax.ShapeDtypeStruct(band_block, B16),
            jax.ShapeDtypeStruct((lines, 128), F32),
        ],
        scratch_shapes=[
            pltpu.VMEM((8, MLP_COLS), F32),
            pltpu.VMEM((8, model), F32),
            pltpu.VMEM((32, model), F32),
            pltpu.VMEM((window, width + 8, model), F32),
            pltpu.VMEM((tokens, model), B16),
            pltpu.VMEM((tokens, model), F32),
            pltpu.VMEM((tokens, model), F32),
            pltpu.VMEM((tokens, MLP_COLS), B16),
            pltpu.VMEM((tokens, MLP_COLS), B16),
            pltpu.VMEM((tokens, model), F32),
            pltpu.VMEM((QUAD * window * window, model), F32),
            pltpu.VMEM((pages, 2, half, width, model), B16),
            pltpu.SemaphoreType.DMA,
            pltpu.SemaphoreType.DMA((tokens // (QUAD * window * window),)),
            pltpu.SemaphoreType.DMA((pages, 2)),
        ],
        compiler_params=pltpu.CompilerParams(vmem_limit_bytes=VMEM_LIMIT),
    )(live, out_grad, halo, n2, first, weights_in, weights_out, gains, biases)


def table_sum(off_ref, grad_ref, out_ref, at, heads, chunks):
    rows = 128 * chunks
    keys = grad_ref.shape[1]
    names = lax.broadcasted_iota(jnp.int32, (rows, SLOT), 0)
    total = jnp.zeros((3 * heads, rows), F32)
    grad = jnp.swapaxes(grad_ref[...], 0, 1)
    for k in range(0, keys, 8):
        hot = jnp.concatenate(
            [jnp.where(names == off_ref[i : i + 1, :], 1.0, 0.0).astype(B16) for i in range(k, k + 8)], axis=1
        )
        value = jnp.concatenate([grad[i] for i in range(k, k + 8)], axis=1)
        high = value.astype(B16)
        rest = value - high.astype(F32)
        middle = rest.astype(B16)
        low = (rest - middle.astype(F32)).astype(B16)
        total += dot(jnp.concatenate([high, middle, low], axis=0), hot, "NT")
    total = total[:heads] + total[heads : 2 * heads] + total[2 * heads :]
    for c in range(chunks):
        out_ref[at + heads * c : at + heads * c + heads, :] = total[:, 128 * c : 128 * c + 128]


class Exchange:
    def __init__(self, pages, chips, share, bufs, sems):
        self.pages, self.chips, self.share = pages, chips, share
        self.rec1, self.s1, self.rec2, self.s2, self.rec3, self.s3, self.rec4 = bufs
        self.send1, self.recv1, self.send2, self.recv2, self.send3, self.recv3, self.send4, self.recv4 = sems
        self.page, row = lax.axis_index("page"), lax.axis_index("rows")
        self.chip, self.core = row // 2, row % 2
        self.other = 2 * self.chip + 1 - self.core
        self.cols = self.s3.shape[-1]

    def page_peer(self, d):
        return lax.rem(self.page + d, self.pages)

    def chip_peer(self, d):
        return lax.rem(self.chip + d, self.chips)

    def along(self, d):
        return {"rows": 2 * self.chip_peer(d) + self.core}

    def rows_of(self, ref, z, c):
        return ref.at[pl.ds(pl.multiple_of((2 * z + c) * self.share, 16), self.share), :]

    def one(self, m, grad):
        return [
            remote(
                self.rows_of(grad, z, 1 - self.core),
                self.rec1.at[m, z],
                self.send1.at[m, z],
                self.recv1.at[m, z],
                {"rows": self.other},
            )
            for z in range(self.chips)
        ]

    def two(self, m):
        return [
            remote(
                self.s1.at[m, self.page_peer(d)],
                self.rec2.at[m, self.page],
                self.send2.at[m, d],
                self.recv2.at[m, d],
                {"page": self.page_peer(d)},
            )
            for d in range(1, self.pages)
        ]

    def three(self, m):
        return [
            remote(
                self.s2.at[m, self.chip_peer(d)],
                self.rec3.at[m, self.chip],
                self.send3.at[m, d],
                self.recv3.at[m, d],
                self.along(d),
            )
            for d in range(1, self.chips)
        ]

    def four(self, m):
        return [
            remote(
                self.s3.at[m],
                self.rec4.at[m, self.page],
                self.send4.at[m, d],
                self.recv4.at[m, d],
                {"page": self.page_peer(d)},
            )
            for d in range(1, self.pages)
        ]

    def start_one(self, m, grad):
        start(self.one(m, grad))

    def start_two(self, m, grad, own):
        wait(self.one(m, grad))
        for q in range(self.pages):
            at = slice(self.cols * q, self.cols * q + self.cols)
            for z in range(self.chips):
                self.s1[m, q, z] = (own(z)[:, at].astype(F32) + self.rec1[m, z, :, at].astype(F32)).astype(B16)
        start(self.two(m))
        self.rec2[m, self.page] = self.s1[m, self.page]

    def start_three(self, m):
        wait(self.two(m))
        total = self.rec2[m, 0].astype(F32)
        for q in range(1, self.pages):
            total = total + self.rec2[m, q].astype(F32)
        self.s2[m] = total.astype(B16)
        start(self.three(m))
        self.rec3[m, self.chip] = self.s2[m, self.chip]

    def start_four(self, m):
        wait(self.three(m))
        total = self.rec3[m, 0].astype(F32)
        for z in range(1, self.chips):
            total = total + self.rec3[m, z].astype(F32)
        self.s3[m] = total.astype(B16)
        start(self.four(m))
        self.rec4[m, self.page] = self.s3[m]

    def finish(self, m, out_ref):
        wait(self.four(m))
        for q in range(self.pages):
            out_ref[:, self.cols * q : self.cols * q + self.cols] = self.rec4[m, q]


class SmallExchange:
    def __init__(self, big, bufs, sems):
        self.big = big
        self.mine, self.one_in, self.two_out, self.two_in, self.three_out, self.three_in = bufs
        self.send, self.recv = sems

    def one(self):
        return [remote(self.mine, self.one_in, self.send.at[0], self.recv.at[0], {"rows": self.big.other})]

    def two(self):
        big = self.big
        return [
            remote(
                self.two_out,
                self.two_in.at[big.page],
                self.send.at[d],
                self.recv.at[d],
                {"page": big.page_peer(d)},
            )
            for d in range(1, big.pages)
        ]

    def three(self):
        big = self.big
        return [
            remote(
                self.three_out,
                self.three_in.at[big.chip],
                self.send.at[big.pages + d],
                self.recv.at[big.pages + d],
                big.along(d),
            )
            for d in range(1, big.chips)
        ]

    def start_one(self):
        start(self.one())

    def start_two(self):
        wait(self.one())
        total = self.mine[...] + self.one_in[...]
        self.two_out[...] = total
        start(self.two())
        self.two_in[self.big.page] = total

    def start_three(self):
        wait(self.two())
        total = self.two_in[0]
        for q in range(1, self.big.pages):
            total = total + self.two_in[q]
        self.three_out[...] = total
        start(self.three())
        self.three_in[self.big.chip] = total

    def finish(self, out_ref, at):
        wait(self.three())
        total = self.three_in[0]
        for z in range(1, self.big.chips):
            total = total + self.three_in[z]
        out_ref[at : at + total.shape[0], :] = total


def start(copies):
    for copy in copies:
        copy.start()


def wait(copies):
    for copy in copies:
        copy.wait()


def attn_backward_kernel(
    sizes,
    live_ref,
    up_ref,
    out_ref,
    mixed_ref,
    gf_ref,
    x_ref,
    n1_ref,
    qkv_ref,
    probs_ref,
    att_ref,
    wproj_ref,
    turned_ref,
    gains_ref,
    biases_ref,
    places_ref,
    early_ref,
    sum_ref,
    small_ref,
    table_ref,
    own_ref,
    mixed_halo_ref,
    patch_halo_ref,
    band,
    gbp,
    datt,
    dprobs,
    bdq,
    bdk,
    bdo,
    stacked,
    beside,
    dqkv,
    dwq,
    dwp,
    compact,
    dscore,
    dscores,
    dbqkv,
    vecs,
    dwa,
    edge,
    own1,
    *rest,
):
    window, half, width, model, heads, least, pages, devices, share = sizes
    slots = window * window
    size_head = model // heads
    sweep, page, quad = pl.program_id(0), pl.program_id(1), pl.program_id(2)
    quads = width // window // QUAD
    step = page * quads + quad
    live = live_ref[page]
    pairs = heads // 4
    pair = 2 * size_head
    part_rows = model // 2
    lines = model // 128
    cols = 2 * model
    big = Exchange(devices[0], devices[1] // 2, share, rest[:7], rest[7:15])
    early = SmallExchange(big, (rest[15],) + rest[16:21], rest[21:23])
    local, halo_send, halo_recv = rest[23:]
    row = lax.axis_index("rows")
    behind, ahead = lax.rem(row + devices[1] - 1, devices[1]), lax.rem(row + 1, devices[1])
    matrices = [dwa.at[0], dwa.at[1]]
    for ref in (up_ref, out_ref):
        for h in range(ref.shape[1] // cols):
            matrices.append(ref.at[:, pl.ds(h * cols, cols)])
    outer = range(2, len(matrices))

    def fetch(m):
        return [
            pltpu.make_async_copy(
                big.rows_of(matrices[m], z, big.core), own1.at[m - 2, z], local.at[m - 2, z]
            )
            for z in range(big.chips)
        ]

    def mixed_copy():
        return remote(mixed_ref, mixed_halo_ref, halo_send.at[0], halo_recv.at[0], {"rows": ahead})

    def edge_at(j):
        return 0 if j == 0 else width + 8 if j == quads else (j * QUAD * window + half) // 16 * 16

    def patch_copy(p, j):
        cut = pl.ds(edge_at(j), edge_at(j + 1) - edge_at(j))
        k = 1 + p * quads + j
        return remote(
            edge.at[p, :, cut, :], patch_halo_ref.at[p, :, cut, :], halo_send.at[k], halo_recv.at[k], {"rows": ahead}
        )

    def moment(at_sweep, at_step):
        return jnp.logical_and(sweep == at_sweep, step == at_step)

    @pl.when(moment(0, 0))
    def _():
        barrier = pltpu.get_barrier_semaphore()
        peers = [{"rows": big.other}, {"rows": behind}, {"rows": ahead}]
        peers += [{"page": big.page_peer(d)} for d in range(1, big.pages)]
        peers += [big.along(d) for d in range(1, big.chips)]
        for peer in peers:
            pl.semaphore_signal(barrier, inc=1, device_id=peer, device_id_type=MESH)
        pl.semaphore_wait(barrier, len(peers))
        for m in outer:
            big.start_one(m, matrices[m])
            start(fetch(m))
        mixed_copy().start()
        early.mine[...] = early_ref[...]
        for ref in (bdq, bdk, bdo, stacked, beside, gbp, dwq, dwp, dbqkv, dscore, vecs):
            ref[...] = jnp.zeros_like(ref)

    def flush(h):
        for part in range(3):
            rows = slice(part * part_rows, part * part_rows + part_rows)
            dwa[h, :, rows] = dwq[rows, :].T.astype(B16)
        dwa[h, :, 3 * part_rows :] = dwp[:, h * part_rows : (h + 1) * part_rows].astype(B16)
        big.start_one(h, matrices[h])
        for k, part in enumerate((0, 2)):
            total = jnp.sum(dbqkv[part * part_rows : (part + 1) * part_rows, :].T, axis=0, keepdims=True)
            lay_lines(early.mine, lines * (3 + k) + h * (lines // 2), total)
        column = jnp.sum(dbqkv[...], axis=1, keepdims=True)
        weights = turned_ref[h].astype(F32)
        shifts = jnp.sum(weights * column, axis=0, keepdims=True)
        gains = jnp.sum(weights * dwq[...], axis=0, keepdims=True)
        vecs[0:1, :] += gains
        vecs[1:2, :] += shifts
        if h == 1:
            lay_row(vecs, 2, biases_ref, 0, lines)
            total = (vecs[0:1, :] - vecs[2:3, :] * vecs[1:2, :]) / gains_ref[0:1, :]
            lay_lines(early.mine, 0, total)
            lay_lines(early.mine, 2 * lines, vecs[1:2, :])
        dscores[h * heads // 2 : (h + 1) * heads // 2] = dscore[...]
        if h == 0:
            for ref in (dwq, dbqkv, dscore):
                ref[...] = jnp.zeros_like(ref)

    def two(m):
        if m >= 2:
            wait(fetch(m))
            big.start_two(m, matrices[m], lambda z: own1.at[m - 2, z])
        else:
            big.start_two(m, matrices[m], lambda z: big.rows_of(matrices[m], z, big.core))

    def table():
        chunks = -(-((2 * window - 1) ** 2) // 128)
        table_sum(places_ref, dscores, early.mine, early.mine.shape[0] - heads * chunks, heads, chunks)
        early.start_one()

    plan = {
        (0, 1): [(two, 2), (two, 3)],
        (0, 2): [(two, 4), (two, 5)],
        (1, 0): [(flush, 0), (big.start_three, 2), (big.start_three, 3)],
        (1, 1): [(two, 0)],
        (1, 4): [(big.start_three, 4), (big.start_three, 5), (big.start_four, 2), (big.start_four, 3)],
        (2, 0): [(flush, 1), (big.start_three, 0)],
        (2, 1): [(two, 1)],
        (2, 5): [(big.start_four, 4), (big.start_four, 5), (big.start_four, 0)],
    }
    for (at_sweep, at_step), acts in plan.items():

        @pl.when(moment(at_sweep, at_step))
        def _():
            for act, m in acts:
                act(m)

    @pl.when(sweep < 2)
    def _():
        for w in range(QUAD):
            gbp[SLOT * w : SLOT * w + slots, :] = gf_ref[slots * w : slots * w + slots, :].astype(B16)
        mine = pl.ds(pl.multiple_of(jnp.minimum(sweep, 1) * part_rows, part_rows), part_rows)
        datt[...] = dot(wproj_ref[mine, :], gbp[...], "NT").astype(B16)

        @pl.when(sweep == 0)
        def _():
            dwp[...] += dot(att_ref[...], gbp[...])

        ratio = size_head**-0.5
        target = dqkv.at[step, jnp.minimum(sweep, 1)]

        def score(w, g):
            low = pair * g
            lanes = slice(SLOT * w, SLOT * w + SLOT)
            for j in range(2):
                at = slice(low + size_head * j, low + size_head * (j + 1))
                cols = slice(SLOT * j, SLOT * j + SLOT)
                bdo[w % 3, at, cols] = datt[at, lanes]
                bdq[w % 3, at, cols] = qkv_ref[0, at, lanes]
                bdk[w % 3, at, cols] = qkv_ref[1, at, lanes]
            values = qkv_ref[2, low : low + pair, SLOT * w : SLOT * w + KEYS]
            dprobs[w % 2, g] = dot(values, bdo[w % 3, low : low + pair, :], "TN")

        def soften(w, g):
            probs = probs_ref[w, g, :KEYS, :].astype(F32)
            term = probs * dprobs[w % 2, g]
            grad = term - probs * jnp.sum(term, axis=0, keepdims=True)
            low_grad = grad.astype(B16)
            beside[w % 2, g, :KEYS, :] = low_grad
            for j in range(2):
                cols = slice(SLOT * j, SLOT * j + SLOT)
                dscore[2 * g + j] += grad[:, cols]
                stacked[w % 2, g, SLOT * j : SLOT * j + KEYS, :] = low_grad[:, cols]

        def attend(w, g):
            low = pair * g
            lanes = slice(SLOT * w, SLOT * w + SLOT)
            rows = slice(low, low + pair)
            got = dot(bdk[w % 3, rows, :], stacked[w % 2, g]) * ratio
            target[low : low + pair, lanes] = got.astype(B16)
            got = dot(bdq[w % 3, rows, :], beside[w % 2, g], "NT") * (1.0 / LOG2E)
            target[part_rows + low : part_rows + low + pair, lanes] = got.astype(B16)
            got = dot(bdo[w % 3, rows, :], probs_ref[w, g], "NT")
            target[2 * part_rows + low : 2 * part_rows + low + pair, lanes] = got.astype(B16)

        for stage in range(QUAD + 2):
            for g in range(pairs):
                if stage < QUAD:
                    score(stage, g)
                if 1 <= stage <= QUAD:
                    soften(stage - 1, g)
                if stage >= 2:
                    attend(stage - 2, g)

        grad = target[...]
        dwq[...] += dot(grad, n1_ref[...])
        wide = grad.astype(F32)
        both = wide[:, :SLOT]
        for w in range(1, QUAD):
            both = both + wide[:, SLOT * w : SLOT * w + SLOT]
        dbqkv[...] += both

    @pl.when(sweep == 2)
    def _():
        dn1 = dot(dqkv[step, 0], turned_ref[0], "TN") + dot(dqkv[step, 1], turned_ref[1], "TN")
        for w in range(QUAD):
            compact[slots * w : slots * w + slots, :] = dn1[SLOT * w : SLOT * w + slots, :]
        grad = compact[...]
        xhat, spread = norm_stats(x_ref[...].astype(F32))
        scaled = grad * gains_ref[0:1, :]
        mean_one = jnp.mean(scaled, axis=-1, keepdims=True)
        mean_two = jnp.mean(scaled * xhat, axis=-1, keepdims=True)
        compact[...] = gf_ref[...] + spread * (scaled - mean_one - xhat * mean_two)
        for w in range(QUAD):
            for r in range(window):
                ref, skip = piece(band, r, quad * QUAD * window, w, window, half)
                at = slots * w + window * r
                ref[skip : skip + window, :] = compact[at : at + window, :]

    for p in range(pages):
        for j in range(quads):

            @pl.when(moment(2, p * quads + j))
            def _():
                cut = slice(edge_at(j), edge_at(j + 1))
                edge[p, :, cut, :] = band[half:, cut, :].astype(B16)
                patch_copy(p, j).start()
                if j == quads - 1:
                    unwrap_band(band, live, half, width, window, least)
                    own_ref[0] = band[:half, :width].astype(B16)

    @pl.when(moment(2, pages * quads - 1))
    def _():
        table()
        big.start_three(1)
        early.start_two()
        for m in outer:
            big.finish(m, sum_ref.at[m])
        big.finish(0, sum_ref.at[0])
        early.start_three()
        big.start_four(1)
        mixed_copy().wait()
        early.finish(early.mine, 0)
        top = small_ref.shape[0]
        small_ref[...] = early.mine[:top]
        for c in range(table_ref.shape[0] // 128):
            table_ref[128 * c : 128 * c + 128, :] = early.mine[top + heads * c : top + heads * (c + 1), :].T
        big.finish(1, sum_ref.at[1])
        for p in range(pages):
            for j in range(quads):
                patch_copy(p, j).wait()


def attn_backward(
    live, dwup, dwout, mixed_next, gf, x, n1, qkv, probs, att, weights_in, turned, gains, biases, places, early, shape, heads, least, share
):
    pages, window, width, model = shape
    half = window // 2
    quads = width // window // QUAD
    slots = window * window
    pairs = heads // 4
    part_rows = model // 2
    devices = (lax.axis_size("page"), lax.axis_size("rows"))
    chips = devices[1] // 2
    hidden = dwup.shape[1]
    wide = 2 * model
    cols = wide // devices[0]
    once = pl.Buffered(1)
    whole = lambda a: pl.BlockSpec(a.shape, lambda s, p, j: (0,) * a.ndim, pipeline_mode=once)
    held = lambda dims: pl.BlockSpec(dims, lambda s, p, j: (0,) * len(dims), pipeline_mode=once)
    anywhere = pl.BlockSpec(memory_space=pl.ANY)
    at = lambda p, j: p * quads + j
    last = pages * quads - 1
    both = lambda s, p, j: jnp.where(s < 2, at(p, j), last)
    first = lambda s, p, j: jnp.where(s == 0, at(p, j), last)
    third = lambda s, p, j: jnp.where(s == 2, at(p, j), 0)
    side = lambda s: jnp.minimum(s, 1)
    own_at = lambda s, p, j: (jnp.where(s == 2, p, 0), 0, 0, 0)
    dma = pltpu.SemaphoreType.DMA
    vmem = pltpu.VMEM
    n = 2 + 2 * hidden // wide
    lines = early.shape[0]
    chunks = -(-((2 * window - 1) ** 2) // 128)

    def small_scratch(rows):
        return [
            vmem((rows, 128), F32),
            vmem((rows, 128), F32),
            vmem((rows, 128), F32),
            vmem((devices[0], rows, 128), F32),
            vmem((rows, 128), F32),
            vmem((chips, rows, 128), F32),
            dma((devices[0] + chips,)),
            dma((devices[0] + chips,)),
        ]

    return pl.pallas_call(
        functools.partial(
            attn_backward_kernel, (window, half, width, model, heads, least, pages, devices, share)
        ),
        grid=(3, pages, quads),
        in_specs=[
            pl.BlockSpec(memory_space=pltpu.SMEM),
            anywhere,
            anywhere,
            anywhere,
            pl.BlockSpec((QUAD * slots, model), lambda s, p, j: (at(p, j), 0)),
            pl.BlockSpec((QUAD * slots, model), lambda s, p, j: (third(s, p, j), 0)),
            pl.BlockSpec((QUAD * SLOT, model), lambda s, p, j: (both(s, p, j), 0)),
            pl.BlockSpec((3, part_rows, QUAD * SLOT), lambda s, p, j: (0, side(s), both(s, p, j))),
            pl.BlockSpec((QUAD, pairs, SLOT, 2 * SLOT), lambda s, p, j: (both(s, p, j), side(s), 0, 0)),
            pl.BlockSpec((model, QUAD * SLOT), lambda s, p, j: (0, first(s, p, j))),
            pl.BlockSpec((model, model), lambda s, p, j: (0, 3), pipeline_mode=once),
            whole(turned),
            whole(gains),
            whole(biases),
            whole(places),
            whole(early),
        ],
        out_specs=[
            held((n, share, wide)),
            held((lines - chunks * heads, 128)),
            held((128 * chunks, heads)),
            pl.BlockSpec((1, half, width, model), own_at),
            anywhere,
            anywhere,
        ],
        out_shape=[
            jax.ShapeDtypeStruct((n, share, wide), B16),
            jax.ShapeDtypeStruct((lines - chunks * heads, 128), F32),
            jax.ShapeDtypeStruct((128 * chunks, heads), F32),
            jax.ShapeDtypeStruct((pages, half, width, model), B16),
            jax.ShapeDtypeStruct((pages, half, width, model), B16),
            jax.ShapeDtypeStruct((pages, half, width + 8, model), B16),
        ],
        scratch_shapes=[
            vmem((window, width + 8, model), F32),
            vmem((QUAD * SLOT, model), B16),
            vmem((part_rows, QUAD * SLOT), B16),
            vmem((2, pairs, KEYS, 2 * SLOT), F32),
            vmem((3, part_rows, 2 * SLOT), B16),
            vmem((3, part_rows, 2 * SLOT), B16),
            vmem((3, part_rows, 2 * SLOT), B16),
            vmem((2, pairs, 2 * SLOT, SLOT), B16),
            vmem((2, pairs, SLOT, 2 * SLOT), B16),
            vmem((pages * quads, 2, 3 * part_rows, QUAD * SLOT), B16),
            vmem((3 * part_rows, model), F32),
            vmem((model, model), F32),
            vmem((QUAD * slots, model), F32),
            vmem((heads // 2, KEYS, SLOT), F32),
            vmem((heads, KEYS, SLOT), F32),
            vmem((3 * part_rows, SLOT), F32),
            vmem((8, model), F32),
            vmem((2, model, wide), B16),
            vmem((pages, half, width + 8, model), B16),
            vmem((n - 2, chips, share, wide), B16),
            vmem((n, chips, share, wide), B16),
            vmem((n, devices[0], chips, share, cols), B16),
            vmem((n, devices[0], chips, share, cols), B16),
            vmem((n, chips, share, cols), B16),
            vmem((n, chips, share, cols), B16),
            vmem((n, share, cols), B16),
            vmem((n, devices[0], share, cols), B16),
            dma((n, chips)),
            dma((n, chips)),
            dma((n, devices[0])),
            dma((n, devices[0])),
            dma((n, chips)),
            dma((n, chips)),
            dma((n, devices[0])),
            dma((n, devices[0])),
        ]
        + small_scratch(lines)
        + [dma((n - 2, chips)), dma((1 + pages * quads,)), dma((1 + pages * quads,))],
        compiler_params=pltpu.CompilerParams(
            vmem_limit_bytes=62 * 2**20, collective_id=0, has_side_effects=True
        ),
    )(live, dwup, dwout, mixed_next, gf, x, n1, qkv, probs, att, weights_in, turned, gains, biases, places, early)


def finish_kernel(
    sizes,
    live_ref,
    sum_hbm,
    min_hbm,
    fin_hbm,
    sin_hbm,
    mout_hbm,
    fout_hbm,
    sout_hbm,
    above_ref,
    own_ref,
    edge_hbm,
    _,
    mixed_ref,
    patch_ref,
    new_in_ref,
    moment_in_ref,
    square_in_ref,
    new_out_ref,
    moment_out_ref,
    square_out_ref,
    sums,
    olds_in,
    news_in,
    olds_out,
    news_out,
    edges,
    tops,
    passed,
    band,
    sems,
    frame_sems,
    in_sems,
    out_sems,
):
    window, half, width, least = sizes
    model = band.shape[2]
    part_rows = model // 2
    share = sums.shape[1]
    pages = edges.shape[0]
    pieces = olds_in.shape[2] // (2 * model)
    tall = olds_out.shape[1] // pieces

    def cut(ref, k):
        return ref.at[:, pl.ds(2 * model * k, 2 * model)]

    def stripe(ref, k):
        return ref.at[pl.ds(tall * k, tall), :]

    copy = pltpu.make_async_copy
    passing = [copy(above_ref, passed.at[0], sems.at[2]), copy(own_ref, passed.at[1], sems.at[3])]
    framed = [
        copy(passed.at[0], mixed_ref.at[:, pl.ds(0, half)], frame_sems.at[0]),
        copy(passed.at[1], patch_ref.at[:, pl.ds(half, half)], frame_sems.at[1]),
    ]
    fetched = [copy(sum_hbm, sums, sems.at[0]), copy(edge_hbm, edges, sems.at[1])]
    laid = copy(tops, patch_ref.at[:, pl.ds(0, half)], frame_sems.at[2])
    ins, outs = [], []
    for k in range(pieces):
        for i, (src, dst) in enumerate(zip((min_hbm, fin_hbm, sin_hbm), (new_in_ref, moment_in_ref, square_in_ref))):
            ins.append(copy(cut(src, k), cut(olds_in.at[i], k), in_sems.at[6 * k + i]))
            outs.append(copy(cut(news_in.at[i], k), cut(dst, k), out_sems.at[6 * k + i]))
        for i, (src, dst) in enumerate(zip((mout_hbm, fout_hbm, sout_hbm), (new_out_ref, moment_out_ref, square_out_ref))):
            ins.append(copy(stripe(src, k), stripe(olds_out.at[i], k), in_sems.at[6 * k + 3 + i]))
            outs.append(copy(stripe(news_out.at[i], k), stripe(dst, k), out_sems.at[6 * k + 3 + i]))
    start(fetched)
    start(ins[:6])
    start(passing)
    start(ins[6:])
    wait(fetched)
    for p in range(pages):
        band[...] = edges[p].astype(F32)
        unwrap_band(band, live_ref[p], half, width, window, least)
        tops[p] = band[:, :width].astype(B16)
    laid.start()
    wait(passing)
    start(framed)
    for k in range(pieces):
        wait(ins[6 * k : 6 * k + 6])
        at = slice(2 * model * k, 2 * model * (k + 1))
        if k < 2:
            grad = jnp.concatenate(
                [
                    sums[h, :, (2 * k + part) * part_rows : (2 * k + part + 1) * part_rows]
                    for part in range(2)
                    for h in range(2)
                ],
                axis=1,
            )
        else:
            grad = sums[k]
        updated = adam_update(olds_in[0, :, at], olds_in[1, :, at], olds_in[2, :, at], grad.astype(F32))
        for i in range(3):
            news_in[i, :, at] = updated[i]
        start(outs[6 * k : 6 * k + 3])
        rows = slice(tall * k, tall * (k + 1))
        grad = sums[4 + k // 2, :, model * (k % 2) : model * (k % 2 + 1)]
        updated = adam_update(olds_out[0, rows], olds_out[1, rows], olds_out[2, rows], grad.astype(F32))
        for i in range(3):
            news_out[i, rows] = updated[i]
        start(outs[6 * k + 3 : 6 * k + 6])
    wait(framed)
    wait(outs)
    laid.wait()


def finish(live, sums, master_in, first_in, second_in, master_out, first_out, second_out, above, own, edge, mixed, least):
    pages, window, width, model = mixed.shape
    half = window // 2
    pieces = master_in.shape[1] // (2 * model)
    anywhere = pl.BlockSpec(memory_space=pl.ANY)
    like = lambda a: jax.ShapeDtypeStruct(a.shape, a.dtype)
    dma = pltpu.SemaphoreType.DMA
    return pl.pallas_call(
        functools.partial(finish_kernel, (window, half, width, least)),
        in_specs=[pl.BlockSpec(memory_space=pltpu.SMEM)] + [anywhere] * 11,
        out_specs=[anywhere] * 8,
        out_shape=[like(mixed), like(mixed)] + [like(master_in)] * 3 + [like(master_out)] * 3,
        scratch_shapes=[
            pltpu.VMEM(sums.shape, B16),
            pltpu.VMEM((3,) + master_in.shape, F32),
            pltpu.VMEM((3,) + master_in.shape, F32),
            pltpu.VMEM((3,) + master_out.shape, F32),
            pltpu.VMEM((3,) + master_out.shape, F32),
            pltpu.VMEM(edge.shape, B16),
            pltpu.VMEM(above.shape, B16),
            pltpu.VMEM((2,) + above.shape, B16),
            pltpu.VMEM((half, width + 8, model), F32),
            dma((4,)),
            dma((3,)),
            dma((6 * pieces,)),
            dma((6 * pieces,)),
        ],
        input_output_aliases={11: 0},
        compiler_params=pltpu.CompilerParams(vmem_limit_bytes=VMEM_LIMIT),
    )(live, sums, master_in, first_in, second_in, master_out, first_out, second_out, above, own, edge, mixed)


def adam_update(master, first, second, grad):
    moment = BETA_ONE * first + (1.0 - BETA_ONE) * grad
    square = BETA_TWO * second + (1.0 - BETA_TWO) * grad * grad
    fix_one = 1.0 - BETA_ONE**STEP
    fix_two = 1.0 - BETA_TWO**STEP
    fresh = master - LEARN_RATE * (
        moment / fix_one / (jnp.sqrt(square / fix_two) + ADAM_EPS) + WEIGHT_DECAY * master
    )
    return (fresh, moment, square)


def shards(
    patches,
    out_grad,
    page_windows,
    region_ids,
    offset_index,
    weights_in,
    weights_out,
    norm_gains,
    biases,
    bias_table,
    master_in,
    master_out,
    first_in,
    second_in,
    first_out,
    second_out,
    first_small,
    second_small,
):
    pages, window, width, model = patches.shape
    half = window // 2
    count = width // window
    least = (count + 1) // 2
    slots = window * window
    table_rows, heads = bias_table.shape
    hidden = weights_out.shape[0]

    bias_lines = biases.reshape(-1, 128)
    lines = model // 128
    table_lanes = -(-table_rows // 128) * 128
    early_lines = EARLY_UP * lines + hidden // 128 + table_lanes * heads // 128

    x, n1, qkv, probs, att, first, n2, below_grad, turned, places = attn_forward(
        page_windows, patches, out_grad, region_ids, offset_index, bias_table.T, weights_in, norm_gains, bias_lines, least
    )
    dwup, dwout, gf, mixed_own, mixed_next, early = mlp(
        page_windows, out_grad, below_grad, n2, first, weights_in, weights_out, norm_gains, bias_lines,
        least, master_in.shape[0], early_lines,
    )
    sums, small, total_table, patch_own, above, edge = attn_backward(
        page_windows, dwup, dwout, mixed_next, gf, x, n1, qkv, probs, att, weights_in, turned, norm_gains,
        bias_lines, places, early, patches.shape, heads, least, master_in.shape[0],
    )
    mixed, patch_grad, new_in, moment_in, square_in, new_out, moment_out, square_out = finish(
        page_windows, sums, master_in, first_in, second_in, master_out, first_out, second_out, above, patch_own,
        edge, mixed_own, least,
    )
    total_small = jnp.concatenate([small.reshape(-1), total_table[:table_rows].reshape(-1)])
    small_master = jnp.concatenate([norm_gains.reshape(-1), biases, bias_table.reshape(-1)])
    new_small, moment_small, square_small = adam_update(
        small_master, first_small, second_small, total_small
    )
    return (
        mixed,
        patch_grad,
        new_in,
        moment_in,
        square_in,
        new_out,
        moment_out,
        square_out,
        new_small,
        moment_small,
        square_small,
    )


def solution(mesh):
    return jax.shard_map(
        shards,
        mesh=mesh,
        in_specs=(
            P("page", "rows", None, None),
            P("page", "rows", None, None),
            P("page"),
            P("page", "rows", None),
            P(),
            P(),
            P(),
            P(),
            P(),
            P(),
            P("rows", None),
            P("rows", None),
            P("rows", None),
            P("rows", None),
            P("rows", None),
            P("rows", None),
            P(),
            P(),
        ),
        out_specs=(
            P("page", "rows", None, None),
            P("page", "rows", None, None),
            P("rows", None),
            P("rows", None),
            P("rows", None),
            P("rows", None),
            P("rows", None),
            P("rows", None),
            P(),
            P(),
            P(),
        ),
        check_vma=False,
    )
```
